32 devices in a mesh: grp: 8 (over z, y), ctx: 4 (over x, core).
Axes of the slice: x: 2, y: 2, z: 4, core: 2. Of those that a mesh axis runs over, the one named last changes fastest.
Arguments:
- latents: bfloat16 [1024, 32, 1024], P(('grp', 'ctx')), may hold values from -6 to 6
- embeds: bfloat16 [1024, 32, 1024], P(('grp', 'ctx')), may hold values from -6 to 6
- cotangent: bfloat16 [1024, 32, 1024], P(('grp', 'ctx')), may hold values from -6 to 6
- counts: int32 [32], replicated, may hold values from 1 to 2, as said below
- w_adapt: bfloat16 [2048, 1024], P(('grp', 'ctx')), may hold values from -0.125 to 0.125
- w_query: bfloat16 [1024, 1024], P(('grp', 'ctx')), may hold values from -0.1875 to 0.1875
- w_key: bfloat16 [1024, 1024], P(('grp', 'ctx')), may hold values from -0.1875 to 0.1875
- w_value: bfloat16 [1024, 1024], P(('grp', 'ctx')), may hold values from -0.1875 to 0.1875
- w_out: bfloat16 [1024, 1024], P(('grp', 'ctx')), may hold values from -0.1875 to 0.1875
- w_gate: bfloat16 [1024, 2816], P(('grp', 'ctx')), may hold values from -0.1875 to 0.1875
- w_up: bfloat16 [1024, 2816], P(('grp', 'ctx')), may hold values from -0.1875 to 0.1875
- w_down: bfloat16 [2816, 1024], P(('grp', 'ctx')), may hold values from -0.109375 to 0.109375
- gains: bfloat16 [4, 1024], P(None, ('grp', 'ctx')), may hold values from 0.099609375 to 1.8984375
Outputs:
- final_latents: bfloat16 [1024, 32, 1024], P(('grp', 'ctx'))
- latent_grad: bfloat16 [1024, 32, 1024], P(('grp', 'ctx'))
- embed_grad: bfloat16 [1024, 32, 1024], P(('grp', 'ctx'))
- adapt_grad: float32 [2048, 1024], P(('grp', 'ctx'))
- query_grad: float32 [1024, 1024], P(('grp', 'ctx'))
- key_grad: float32 [1024, 1024], P(('grp', 'ctx'))
- value_grad: float32 [1024, 1024], P(('grp', 'ctx'))
- out_grad: float32 [1024, 1024], P(('grp', 'ctx'))
- gate_grad: float32 [1024, 2816], P(('grp', 'ctx'))
- up_grad: float32 [1024, 2816], P(('grp', 'ctx'))
- down_grad: float32 [2816, 1024], P(('grp', 'ctx'))
- gain_grad: float32 [4, 1024], P(None, ('grp', 'ctx'))
The draws below stay inside these ranges and needn't reach their ends.
Inputs may be any that keep to these rules, and one draw needn't show every extreme that they name: `counts`: exactly 16 sequences have count 2, the others count 1.
All inputs are finite; a program needn't handle non-finite values.
Results may differ from the reference program's by a relative error of at most 0.024.
Values may be sent and summed in bfloat16 or wider, within the bound.
A program may use at most 320 MiB of HBM per device.

```python
import jax
import jax.numpy as jnp
from jax import lax

D = 1024
HEADS = 8
HEAD_DIM = 128
FF = 2816
LEN = 1024
SEQS = 32


def draw_counts(key, part):
    key = jax.random.fold_in(key, 7)
    shuffled = jax.random.permutation(key, SEQS)
    return jnp.where(shuffled < SEQS // 2, 2, 1).astype(jnp.int32)


def with_spikes(entries, key, source, target, blocks, factor):
    owner, partner = [(jnp.arange(entries.shape[axis_at]) // (entries.shape[axis_at] // blocks)).reshape([-1 if axis == axis_at else 1 for axis in range(entries.ndim)]) for axis_at in (source, target)]
    chosen = jax.random.permutation(key, blocks)[partner]
    strong = (owner == chosen) | (owner == (partner + blocks // 2) % blocks)
    return jnp.where(strong, factor * entries, entries)


def steps_of(own_key, extent, pieces, low, high):
    def one(axis_at, parts):
        draws = jax.random.uniform(jax.random.fold_in(jax.random.fold_in(own_key, 6), axis_at), (parts,), jnp.float32, low / len(pieces), high / len(pieces))
        return jnp.repeat(jnp.exp(draws), extent[axis_at] // parts).reshape((-1,) + (1,) * (len(extent) - axis_at - 1))

    loudness = one(*pieces[0])
    for cut in pieces[1:]:
        loudness = loudness * one(*cut)
    return loudness


def noise(stream_key, dims, deviation, reach, pieces=(), kind=jnp.bfloat16):
    values = jax.random.normal(stream_key, dims, jnp.float32) * deviation
    if len(pieces) > 0:
        values = steps_of(stream_key, dims, pieces, -0.22, 0.18) * values
    return jnp.clip(values, min=-reach, max=reach).astype(kind)


def noise_with(rng, shape, width, bound, cuts, heavy, kind=jnp.bfloat16):
    array = width * jax.random.normal(rng, shape, jnp.float32)
    if cuts:
        array = array * steps_of(rng, shape, cuts, -0.22, 0.18)
    return jnp.clip(with_spikes(array, jax.random.fold_in(rng, 3), *heavy), -bound, bound).astype(kind)


def setup_inputs(seed: int = 0) -> dict:
    streams_of = jax.random.split(jax.random.key(seed), 14)
    return {
        "latents": noise(streams_of[0], (LEN, SEQS, D), 1.0, 6.0, ((0, 32),)),
        "embeds": noise(streams_of[1], (LEN, SEQS, D), 1.0, 6.0, ((0, 32),)),
        "cotangent": noise_with(streams_of[2], (LEN, SEQS, D), 1.0, 6.0, ((0, 32),), (0, 2, 32, 2.75)),
        "counts": draw_counts(jax.random.fold_in(streams_of[13], 71), 0),
        "w_adapt": noise(streams_of[4], (2 * D, D), (2 * D) ** -0.5, 0.125, ((0, 32),)),
        "w_query": noise(streams_of[5], (D, D), D ** -0.5, 0.1875, ((0, 32),)),
        "w_key": noise(streams_of[6], (D, D), D ** -0.5, 0.1875, ((0, 32),)),
        "w_value": noise(streams_of[7], (D, D), D ** -0.5, 0.1875, ((0, 32),)),
        "w_out": noise(streams_of[8], (D, D), D ** -0.5, 0.1875, ((0, 32),)),
        "w_gate": noise(streams_of[9], (D, FF), D ** -0.5, 0.1875, ((0, 32),)),
        "w_up": noise(streams_of[10], (D, FF), D ** -0.5, 0.1875, ((0, 32),)),
        "w_down": noise(streams_of[11], (FF, D), FF ** -0.5, 0.109375, ((0, 32),)),
        "gains": jnp.clip(1.0 + 0.18 * jax.random.normal(streams_of[12], (4, D), jnp.float32), 0.099609375, 1.8984375).astype(jnp.bfloat16),
    }


@jax.custom_vjp
def low(v):
    return lax.optimization_barrier(v.astype(jnp.bfloat16)).astype(jnp.float32)

@jax.custom_vjp
def low_back(v):
    return v

def low_keep(v):
    return (low(v), None)

def low_pass(kept, grad):
    return (grad,)

def back_keep(v):
    return (v, None)

def back_low(kept, grad):
    return (low(grad),)
low.defvjp(low_keep, low_pass)
low_back.defvjp(back_keep, back_low)
highest = lax.Precision.HIGHEST

def rms_norm(values):
    return values * lax.rsqrt(lax.optimization_barrier(jnp.mean(values * values, -1, keepdims=True)) + 1e-06)

def rope_table(positions):
    freq = 10000.0 ** (-2.0 * jnp.arange(HEAD_DIM // 2, dtype=jnp.float32) / HEAD_DIM)
    angle = positions.astype(jnp.float32)[:, None] * freq
    return (jnp.cos(angle), jnp.sin(angle))

def rotate(values, cosine, sine):
    half_dim = HEAD_DIM // 2
    first_half = values[..., :half_dim]
    second_half = values[..., half_dim:]
    cos_b = cosine[:, None, None, :]
    sin_b = sine[:, None, None, :]
    return jnp.concatenate([first_half * cos_b - second_half * sin_b, second_half * cos_b + first_half * sin_b], -1)

def project(values, matrix):
    return jnp.einsum('tsk,kn->tsn', values, matrix, precision=highest)

def core_block(latent, embedding, weights, cosine, sine, causal):
    adapt_w, query_w, key_w, value_w, output_w, gate_w, up_w, down_w, gain_rows = weights
    length = latent.shape[0]
    seq_batch = latent.shape[1]
    joined = low(jnp.concatenate([latent, embedding], -1))
    resid = low_back(project(joined, adapt_w))
    normed = low(rms_norm(resid) * gain_rows[0])

    def heads_of(matrix):
        return low_back(project(normed, matrix)).reshape(length, seq_batch, HEADS, HEAD_DIM)
    queries = low(rotate(heads_of(query_w), cosine, sine))
    keys_all = low(rotate(heads_of(key_w), cosine, sine))
    values_all = low(heads_of(value_w))
    scores = low_back(jnp.einsum('qshd,kshd->qshk', queries, keys_all, precision=highest) * HEAD_DIM ** (-0.5))
    scores = jnp.where(causal[:, None, None, :], scores, -1e+30)
    probs = low(jax.nn.softmax(scores, -1))
    mixed = low(low_back(jnp.einsum('qshk,kshd->qshd', probs, values_all, precision=highest)))
    mixed = mixed.reshape(length, seq_batch, HEADS * HEAD_DIM)
    branch = low_back(project(mixed, output_w))
    middle = resid + rms_norm(branch) * gain_rows[1]
    mlp_in = low(rms_norm(middle) * gain_rows[2])
    gate_pre = low_back(project(mlp_in, gate_w))
    up_pre = low_back(project(mlp_in, up_w))
    hidden = low(jax.nn.silu(gate_pre) * up_pre)
    down_out = low_back(project(hidden, down_w))
    return middle + rms_norm(down_out) * gain_rows[3]

def reference(latents, embeds, cotangent, counts, w_adapt, w_query, w_key, w_value, w_out, w_gate, w_up, w_down, gains):
    weights = tuple((matrix.astype(jnp.float32) for matrix in (w_adapt, w_query, w_key, w_value, w_out, w_gate, w_up, w_down, gains)))
    positions = jnp.arange(LEN, dtype=jnp.int32)
    cosine, sine = rope_table(positions)
    causal = positions[None, :] <= positions[:, None]
    batches = SEQS // 4

    def to_batches(values):
        return jnp.moveaxis(values.astype(jnp.float32).reshape(LEN, batches, 4, D), 1, 0)

    def run_block(latent, embedding, params):
        return core_block(latent, embedding, params, cosine, sine, causal)

    def one_batch(totals, batch_items):
        latent, embedding, upstream, seq_counts = batch_items
        first_pass = run_block(latent, embedding, weights)
        last_in = jnp.where(seq_counts[None, :, None] == 2, first_pass, latent)
        result, pull_back = jax.vjp(run_block, last_in, embedding, weights)
        latent_grad, embed_grad, weight_grads = pull_back(upstream)
        totals = jax.tree.map(jnp.add, totals, weight_grads)
        return (totals, (result.astype(jnp.bfloat16), latent_grad.astype(jnp.bfloat16), embed_grad.astype(jnp.bfloat16)))
    start_totals = jax.tree.map(jnp.zeros_like, weights)
    totals, results = lax.scan(one_batch, start_totals, (to_batches(latents), to_batches(embeds), to_batches(cotangent), counts.reshape(batches, 4)))

    def from_batches(values):
        return jnp.moveaxis(values, 0, 1).reshape(LEN, SEQS, D)
    return (from_batches(results[0]), from_batches(results[1]), from_batches(results[2]), totals[0], totals[1], totals[2], totals[3], totals[4], totals[5], totals[6], totals[7], totals[8])
```

```python
import functools

import jax
import jax.numpy as jnp
from jax import lax
from jax.experimental import pallas as pl
from jax.experimental.pallas import tpu as pltpu
from jax.sharding import PartitionSpec as P

HEADS = 8
HEAD_DIM = 128


def rms_scale(values):
    return lax.rsqrt(jnp.mean(values * values, -1, keepdims=True) + 1e-06)


def norm_back(values, upstream, gain_vec):
    scale_rows = rms_scale(values)
    normal = values * scale_rows
    gain_part = jnp.sum(upstream * normal, 0)
    scaled = upstream * gain_vec
    return (
        scale_rows * (scaled - normal * jnp.mean(scaled * normal, -1, keepdims=True)),
        gain_part,
    )


def rope_table(positions):
    freq = 10000.0 ** (-2.0 * jnp.arange(HEAD_DIM // 2, dtype=jnp.float32) / HEAD_DIM)
    angle = positions.astype(jnp.float32)[:, None] * freq
    return (jnp.cos(angle), jnp.sin(angle))


def rotate(values, cosine, sine):
    half_dim = HEAD_DIM // 2
    first_half = values[..., :half_dim]
    second_half = values[..., half_dim:]
    cos_b = cosine[:, None, None, :]
    sin_b = sine[:, None, None, :]
    return jnp.concatenate(
        [first_half * cos_b - second_half * sin_b, second_half * cos_b + first_half * sin_b], -1
    )


def unrotate(grads, cosine, sine):
    half_dim = HEAD_DIM // 2
    first_half = grads[..., :half_dim]
    second_half = grads[..., half_dim:]
    cos_b = cosine[:, None, None, :]
    sin_b = sine[:, None, None, :]
    return jnp.concatenate(
        [first_half * cos_b + second_half * sin_b, second_half * cos_b - first_half * sin_b], -1
    )


def score_block(queries, keys_in, query_pos, key_pos_in):
    raw = jnp.einsum(
        "qshd,kshd->qshk", queries, keys_in, preferred_element_type=jnp.float32
    ) * HEAD_DIM ** (-0.5)
    causal = key_pos_in[None, :] <= query_pos[:, None]
    return jnp.where(causal[:, None, None, :], raw, -1e30)


def back_block(queries, keys_in, values_in, d_mixed, log_total, delta, query_pos, key_pos_in):
    scores = score_block(queries, keys_in, query_pos, key_pos_in)
    probs = jnp.exp(scores - log_total[..., None])
    d_probs = jnp.einsum("qshd,kshd->qshk", d_mixed, values_in, preferred_element_type=jnp.float32)
    slopes = (probs * (d_probs - delta[..., None])).astype(jnp.bfloat16)
    return (probs.astype(jnp.bfloat16), slopes)


def spread_on_device(
    latents,
    embeds,
    cotangent,
    counts,
    w_adapt,
    w_query,
    w_key,
    w_value,
    w_out,
    w_gate,
    w_up,
    w_down,
    gains,
):
    groups = lax.axis_size("grp")
    ctx_count = lax.axis_size("ctx")
    seq_total = latents.shape[1]
    seq_group = seq_total // groups
    block_len = latents.shape[0]
    model_width = latents.shape[2]
    group_len = groups * block_len
    adapt_w, query_w, key_w, value_w, output_w, gate_w, up_w, down_w, gain_rows = (
        lax.all_gather(w_adapt, ("grp", "ctx"), axis=0, tiled=True),
        lax.all_gather(w_query, ("grp", "ctx"), axis=0, tiled=True),
        lax.all_gather(w_key, ("grp", "ctx"), axis=0, tiled=True),
        lax.all_gather(w_value, ("grp", "ctx"), axis=0, tiled=True),
        lax.all_gather(w_out, ("grp", "ctx"), axis=0, tiled=True),
        lax.all_gather(w_gate, ("grp", "ctx"), axis=0, tiled=True),
        lax.all_gather(w_up, ("grp", "ctx"), axis=0, tiled=True),
        lax.all_gather(w_down, ("grp", "ctx"), axis=0, tiled=True),
        lax.all_gather(gains, ("grp", "ctx"), axis=1, tiled=True),
    )
    gain_float = gain_rows.astype(jnp.float32)
    seq_order = jnp.arange(seq_total, dtype=jnp.int32)
    latent_in, embed_in, slope_in = (
        lax.all_to_all(
            jnp.take(latents, seq_order, axis=1), "grp", split_axis=1, concat_axis=0, tiled=True
        ),
        lax.all_to_all(
            jnp.take(embeds, seq_order, axis=1), "grp", split_axis=1, concat_axis=0, tiled=True
        ),
        lax.all_to_all(
            jnp.take(cotangent, seq_order, axis=1), "grp", split_axis=1, concat_axis=0, tiled=True
        ),
    )
    ctx_index = lax.axis_index("ctx")

    def key_position(flat_index):
        source = flat_index // group_len
        within = flat_index % group_len
        return (within // block_len * ctx_count + source) * block_len + within % block_len

    query_pos = key_position(ctx_index * group_len + jnp.arange(group_len, dtype=jnp.int32))
    cos_query, sin_query = rope_table(query_pos)

    def attend_forward(queries, keys_in, values_in):
        piece = lax.all_gather(keys_in, "ctx", axis=0, tiled=True)
        scores = score_block(
            queries, piece, query_pos, key_position(jnp.arange(piece.shape[0], dtype=jnp.int32))
        )
        log_total = jax.nn.logsumexp(scores, -1)
        probs = jnp.exp(scores - log_total[..., None]).astype(jnp.bfloat16)
        mixed_raw = jnp.einsum(
            "qshk,kshd->qshd",
            probs,
            lax.all_gather(values_in, "ctx", axis=0, tiled=True),
            preferred_element_type=jnp.float32,
        )
        return (mixed_raw.astype(jnp.bfloat16), (queries, keys_in, values_in, log_total, mixed_raw))

    def core_block(latent, embedding):
        seq_batch = latent.shape[1]
        row_count = group_len * seq_batch
        joined = jnp.concatenate([latent.astype(jnp.bfloat16), embedding], -1).reshape(
            row_count, 2 * model_width
        )
        resid = jnp.dot(joined, adapt_w, preferred_element_type=jnp.float32)
        normed = (resid * rms_scale(resid) * gain_float[0]).astype(jnp.bfloat16)

        def heads_of(matrix):
            return jnp.dot(normed, matrix, preferred_element_type=jnp.float32).reshape(
                group_len, seq_batch, HEADS, HEAD_DIM
            )

        queries = rotate(heads_of(query_w), cos_query, sin_query).astype(jnp.bfloat16)
        keys_in = rotate(heads_of(key_w), cos_query, sin_query).astype(jnp.bfloat16)
        values_in = heads_of(value_w).astype(jnp.bfloat16)
        mixed, kept = attend_forward(queries, keys_in, values_in)
        mixed_flat = mixed.reshape(row_count, model_width)
        branch = jnp.dot(mixed_flat, output_w, preferred_element_type=jnp.float32)
        middle = resid + branch * rms_scale(branch) * gain_float[1]
        mlp_in = (middle * rms_scale(middle) * gain_float[2]).astype(jnp.bfloat16)
        gate_pre = jnp.dot(mlp_in, gate_w, preferred_element_type=jnp.float32)
        up_pre = jnp.dot(mlp_in, up_w, preferred_element_type=jnp.float32)
        hidden = (jax.nn.silu(gate_pre) * up_pre).astype(jnp.bfloat16)
        down_out = jnp.dot(hidden, down_w, preferred_element_type=jnp.float32)
        result = middle + down_out * rms_scale(down_out) * gain_float[3]
        flat_saved = tuple(
            (
                stored.reshape(group_len, seq_batch, stored.shape[-1])
                for stored in (
                    joined,
                    resid,
                    normed,
                    mixed_flat,
                    branch,
                    middle,
                    mlp_in,
                    gate_pre,
                    up_pre,
                    hidden,
                    down_out,
                )
            )
        )
        return (result.reshape(group_len, seq_batch, model_width), (flat_saved, kept))

    group_counts = lax.dynamic_slice_in_dim(
        jnp.take(counts, seq_order), lax.axis_index("grp") * seq_group, seq_group
    )
    first_out, first_saved = core_block(latent_in, embed_in)
    last_in = jnp.where(group_counts[None, :, None] == 2, first_out, latent_in.astype(jnp.float32))
    final_out, saved = core_block(last_in, embed_in)
    upstream = slope_in.astype(jnp.float32)
    flat_saved, kept = saved
    (
        joined,
        resid,
        normed,
        mixed_flat,
        branch,
        middle,
        mlp_in,
        gate_pre,
        up_pre,
        hidden,
        down_out,
    ) = tuple((stored.reshape(-1, stored.shape[-1]) for stored in flat_saved))
    seq_batch = upstream.shape[1]
    d_result = upstream.reshape(-1, model_width)
    d_down, gain_four = norm_back(down_out, d_result, gain_float[3])
    d_down = d_down.astype(jnp.bfloat16)
    down_part = jnp.einsum("rf,rd->fd", hidden, d_down, preferred_element_type=jnp.float32)
    d_hidden = jnp.einsum("rd,fd->rf", d_down, down_w, preferred_element_type=jnp.float32)
    sigma = jax.nn.sigmoid(gate_pre)
    d_gate = (d_hidden * up_pre * sigma * (1.0 + gate_pre * (1.0 - sigma))).astype(jnp.bfloat16)
    d_up = (d_hidden * gate_pre * sigma).astype(jnp.bfloat16)
    gate_part = jnp.einsum("rd,rf->df", mlp_in, d_gate, preferred_element_type=jnp.float32)
    up_part = jnp.einsum("rd,rf->df", mlp_in, d_up, preferred_element_type=jnp.float32)
    d_mlp = jnp.einsum(
        "rf,df->rd", d_gate, gate_w, preferred_element_type=jnp.float32
    ) + jnp.einsum("rf,df->rd", d_up, up_w, preferred_element_type=jnp.float32)
    d_middle, gain_three = norm_back(middle, d_mlp, gain_float[2])
    d_middle = d_middle + d_result
    d_branch, gain_two = norm_back(branch, d_middle, gain_float[1])
    d_branch = d_branch.astype(jnp.bfloat16)
    out_part = jnp.einsum("re,rd->ed", mixed_flat, d_branch, preferred_element_type=jnp.float32)
    d_mixed = jnp.einsum(
        "rd,ed->re", d_branch, output_w, preferred_element_type=jnp.float32
    ).astype(jnp.bfloat16)
    attend_d_mixed = d_mixed.reshape(group_len, seq_batch, HEADS, HEAD_DIM)
    queries, keys_in, values_in, log_total, mixed_raw = kept
    delta = jnp.sum(attend_d_mixed.astype(jnp.float32) * mixed_raw, -1)
    key_part = lax.all_gather(keys_in, "ctx", axis=0, tiled=True)
    value_part = lax.all_gather(values_in, "ctx", axis=0, tiled=True)
    key_pos_in = key_position(jnp.arange(key_part.shape[0], dtype=jnp.int32))
    probs_low, slopes = back_block(
        queries, key_part, value_part, attend_d_mixed, log_total, delta, query_pos, key_pos_in
    )
    d_query = HEAD_DIM ** (-0.5) * jnp.einsum(
        "qshk,kshd->qshd", slopes, key_part, preferred_element_type=jnp.float32
    )
    pull_stacked = jnp.stack([probs_low, slopes])
    d_query, stacked = (d_query, pull_stacked)
    d_key = HEAD_DIM ** (-0.5) * jnp.einsum(
        "qshk,qshd->kshd", stacked[1], queries, preferred_element_type=jnp.float32
    )
    d_value = jnp.einsum(
        "qshk,qshd->kshd", stacked[0], attend_d_mixed, preferred_element_type=jnp.float32
    )
    paired = lax.psum_scatter(
        jnp.concatenate([d_key, d_value], -1).astype(jnp.bfloat16),
        "ctx",
        scatter_dimension=0,
        tiled=True,
    ).astype(jnp.float32)
    d_query, d_key, d_value = (
        unrotate(d_query, cos_query, sin_query).astype(jnp.bfloat16),
        unrotate(paired[..., :HEAD_DIM], cos_query, sin_query).astype(jnp.bfloat16),
        paired[..., HEAD_DIM:].astype(jnp.bfloat16),
    )
    d_query = d_query.reshape(-1, model_width)
    d_key = d_key.reshape(-1, model_width)
    d_value = d_value.reshape(-1, model_width)
    query_part = jnp.einsum("rd,re->de", normed, d_query, preferred_element_type=jnp.float32)
    key_part = jnp.einsum("rd,re->de", normed, d_key, preferred_element_type=jnp.float32)
    value_part = jnp.einsum("rd,re->de", normed, d_value, preferred_element_type=jnp.float32)
    d_normed = (
        jnp.einsum("re,de->rd", d_query, query_w, preferred_element_type=jnp.float32)
        + jnp.einsum("re,de->rd", d_key, key_w, preferred_element_type=jnp.float32)
        + jnp.einsum("re,de->rd", d_value, value_w, preferred_element_type=jnp.float32)
    )
    d_resid, gain_one = norm_back(resid, d_normed, gain_float[0])
    d_resid = (d_resid + d_middle).astype(jnp.bfloat16)
    adapt_part = jnp.einsum("rk,rd->kd", joined, d_resid, preferred_element_type=jnp.float32)
    d_joined = jnp.einsum("rd,kd->rk", d_resid, adapt_w, preferred_element_type=jnp.float32)
    gain_part = jnp.stack([gain_one, gain_two, gain_three, gain_four])
    d_joined, grads = (
        d_joined.reshape(group_len, seq_batch, 2 * model_width),
        (
            adapt_part,
            query_part,
            key_part,
            value_part,
            out_part,
            gate_part,
            up_part,
            down_part,
            gain_part,
        ),
    )
    final_back, latent_back, embed_back = (
        lax.all_to_all(
            final_out.astype(jnp.bfloat16), "grp", split_axis=0, concat_axis=1, tiled=True
        ),
        lax.all_to_all(
            d_joined[..., :model_width].astype(jnp.bfloat16),
            "grp",
            split_axis=0,
            concat_axis=1,
            tiled=True,
        ),
        lax.all_to_all(
            d_joined[..., model_width:].astype(jnp.bfloat16),
            "grp",
            split_axis=0,
            concat_axis=1,
            tiled=True,
        ),
    )
    seq_index = jnp.arange(seq_total, dtype=jnp.int32)
    inverse = jnp.sum(jnp.where(seq_order[:, None] == seq_index[None, :], seq_index[:, None], 0), 0)
    (
        adapt_part,
        query_part,
        key_part,
        value_part,
        out_part,
        gate_part,
        up_part,
        down_part,
        gain_part,
    ) = grads
    summed = (
        lax.psum_scatter(adapt_part, ("grp", "ctx"), scatter_dimension=0, tiled=True),
        lax.psum_scatter(query_part, ("grp", "ctx"), scatter_dimension=0, tiled=True),
        lax.psum_scatter(key_part, ("grp", "ctx"), scatter_dimension=0, tiled=True),
        lax.psum_scatter(value_part, ("grp", "ctx"), scatter_dimension=0, tiled=True),
        lax.psum_scatter(out_part, ("grp", "ctx"), scatter_dimension=0, tiled=True),
        lax.psum_scatter(gate_part, ("grp", "ctx"), scatter_dimension=0, tiled=True),
        lax.psum_scatter(up_part, ("grp", "ctx"), scatter_dimension=0, tiled=True),
        lax.psum_scatter(down_part, ("grp", "ctx"), scatter_dimension=0, tiled=True),
        lax.psum_scatter(gain_part, ("grp", "ctx"), scatter_dimension=1, tiled=True),
    )
    return (
        jnp.take(final_back, inverse, axis=1),
        jnp.take(latent_back, inverse, axis=1),
        jnp.take(embed_back, inverse, axis=1),
        summed[0],
        summed[1],
        summed[2],
        summed[3],
        summed[4],
        summed[5],
        summed[6],
        summed[7],
        summed[8],
    )


BOTH = ("grp", "ctx")
LOG2E = 1.4426950408889634
SCALE = HEAD_DIM ** (-0.5)
TILE = 256
NEG = -1e30


def grid_sizes():
    ctx = lax.axis_size("ctx")
    x_size = ctx // 2
    return lax.axis_size("grp") // x_size, x_size, x_size, 2


def grid_place():
    z_size, y_size, x_size, k_size = grid_sizes()
    g, c = lax.axis_index("grp"), lax.axis_index("ctx")
    return g // y_size, g % y_size, c // k_size, c % k_size


def send(values, axis, shift=None, keep=None):
    sizes = grid_sizes()
    pairs = []
    for flat in range(sizes[0] * sizes[1] * sizes[2] * sizes[3]):
        rest, spot = flat, [0, 0, 0, 0]
        for at in (3, 2, 1, 0):
            spot[at] = rest % sizes[at]
            rest //= sizes[at]
        own = spot[axis]
        other = 1 - own if shift is None else own + shift
        if 0 <= other < sizes[axis] and (keep is None or keep(own)):
            spot[axis] = other
            target = ((spot[0] * sizes[1] + spot[1]) * sizes[2] + spot[2]) * sizes[3] + spot[3]
            pairs.append((flat, target))
    return lax.ppermute(values, BOTH, pairs)


def join_pair(values, axis, spot, at):
    other = send(values, axis)
    first = jnp.where(spot == 0, values, other)
    second = jnp.where(spot == 0, other, values)
    return jnp.stack([first, second], at)


def gather_rows(shard):
    z_size = grid_sizes()[0]
    z, y, x, k = grid_place()
    rows, width = shard.shape
    up, down = [shard], [shard]
    for step in range(1, z_size):
        up.append(send(up[-1], 0, 1, lambda own, s=step: own >= s - 1))
        down.append(send(down[-1], 0, -1, lambda own, s=step: own <= z_size - s))
    line = lax.dynamic_update_index_in_dim(jnp.zeros((z_size, rows, width), shard.dtype), shard, z, 0)
    for step in range(1, z_size):
        block = jnp.where(z >= step, up[step], down[z_size - step])
        line = lax.dynamic_update_index_in_dim(line, block, (z - step + z_size) % z_size, 0)
    half = z_size // 2
    low, high = line[:half], line[half:]
    low = join_pair(low, 2, x, 1)
    high = join_pair(high, 1, y, 1)
    low = join_pair(low, 1, y, 1)
    high = join_pair(high, 2, x, 2)
    chip = jnp.concatenate([low, high], 0)
    return join_pair(chip, 3, k, 3).reshape(-1, rows, width)


def fold_pair(values, axis, spot, at):
    leaving = lax.dynamic_index_in_dim(values, 1 - spot, at, keepdims=False).astype(jnp.bfloat16)
    staying = lax.dynamic_index_in_dim(values, spot, at, keepdims=False).astype(jnp.float32)
    return (staying + send(leaving, axis).astype(jnp.float32)).astype(jnp.bfloat16)


def scatter_rows(blocks):
    sizes = grid_sizes()
    z_size = sizes[0]
    z, y, x, k = grid_place()
    chip = fold_pair(blocks.reshape(sizes + blocks.shape[1:]), 3, k, 3)
    half = z_size // 2
    low, high = chip[:half], chip[half:]
    low = fold_pair(low, 1, y, 1)
    high = fold_pair(high, 2, x, 2)
    low = fold_pair(low, 2, x, 1)
    high = fold_pair(high, 1, y, 1)
    line = jnp.concatenate([low, high], 0)
    up = down = jnp.zeros(line.shape[1:], line.dtype)
    for step in range(1, z_size):
        rising = lax.dynamic_index_in_dim(line, (z + z_size - step) % z_size, 0, keepdims=False)
        rising = (rising.astype(jnp.float32) + up.astype(jnp.float32)).astype(jnp.bfloat16)
        up = send(rising, 0, 1, lambda own, s=step: own <= s - 1)
        sinking = lax.dynamic_index_in_dim(line, (z + step) % z_size, 0, keepdims=False)
        sinking = (sinking.astype(jnp.float32) + down.astype(jnp.float32)).astype(jnp.bfloat16)
        down = send(sinking, 0, -1, lambda own, s=step: own >= z_size - s)
    own = lax.dynamic_index_in_dim(line, z, 0, keepdims=False)
    return own.astype(jnp.float32) + up.astype(jnp.float32) + down.astype(jnp.float32)


def dot_t(left, right):
    return lax.dot_general(left, right, (((1,), (1,)), ((), ())), preferred_element_type=jnp.float32)


def dot_n(left, right):
    return jnp.dot(left, right, preferred_element_type=jnp.float32)


def dot_w(left, right):
    return lax.dot_general(left, right, (((0,), (0,)), ((), ())), preferred_element_type=jnp.float32)


def below(rows, columns):
    at_row = lax.broadcasted_iota(jnp.int32, (rows, columns), 0)
    at_column = lax.broadcasted_iota(jnp.int32, (rows, columns), 1)
    return at_column <= at_row


def whole_attend(q_ref, k_ref, v_ref, o_ref, log_ref):
    head = pl.program_id(0)
    length = q_ref.shape[0]
    lane = lax.broadcasted_iota(jnp.int32, (TILE, 128), 1)
    for at in range(length // TILE):
        rows = pl.ds(at * TILE, TILE)
        seen = (at + 1) * TILE
        raw = dot_t(q_ref[rows, :], k_ref[:seen, :]) * (SCALE * LOG2E)
        last = jnp.where(below(TILE, TILE), raw[:, at * TILE :], NEG)
        raw = jnp.concatenate([raw[:, : at * TILE], last], 1) if at else last
        top = jnp.max(raw, 1, keepdims=True)
        weight = jnp.exp2(raw - top)
        total = jnp.sum(weight, 1, keepdims=True)
        mixed = dot_n(weight.astype(jnp.bfloat16), v_ref[:seen, :])
        o_ref[rows, :] = (mixed / total).astype(o_ref.dtype)
        log_total = top + jnp.log2(total)
        log_ref[rows, :] = jnp.where(lane == head, log_total, log_ref[rows, :])


def attend_whole(queries, keys_in, values_in):
    length, width = queries.shape
    head_block = pl.BlockSpec((length, HEAD_DIM), lambda h: (0, h))
    return pl.pallas_call(
        whole_attend,
        grid=(width // HEAD_DIM,),
        in_specs=[head_block] * 3,
        out_specs=[head_block, pl.BlockSpec((length, 128), lambda h: (0, 0))],
        out_shape=[
            jax.ShapeDtypeStruct((length, width), jnp.bfloat16),
            jax.ShapeDtypeStruct((length, 128), jnp.float32),
        ],
        compiler_params=pltpu.CompilerParams(vmem_limit_bytes=32 * 2**20),
        cost_estimate=pl.CostEstimate(
            flops=2 * length * length * width, bytes_accessed=8 * length * width, transcendentals=0
        ),
        name="attend_whole",
    )(queries, keys_in, values_in)


def shared_attend(block_len, core_ref, q_ref, k_ref, v_ref, ok_ref, ov_ref, o_ref):
    core = core_ref[0]
    length = q_ref.shape[0]
    for at in range(length // TILE):
        rows = pl.ds(at * TILE, TILE)
        seen = (at + 1) * TILE
        queries = q_ref[rows, :]
        raw = dot_t(queries, k_ref[:seen, :]) * (SCALE * LOG2E)
        far = dot_t(queries, ok_ref[:seen, :]) * (SCALE * LOG2E)
        at_row = lax.broadcasted_iota(jnp.int32, (TILE, TILE), 0)
        at_column = lax.broadcasted_iota(jnp.int32, (TILE, TILE), 1)
        near_last = jnp.where(at_column <= at_row, raw[:, at * TILE :], NEG)
        far_ok = at_column // block_len < at_row // block_len + core
        far_last = jnp.where(far_ok, far[:, at * TILE :], NEG)
        raw = jnp.concatenate([raw[:, : at * TILE], near_last], 1) if at else near_last
        far = jnp.concatenate([far[:, : at * TILE], far_last], 1) if at else far_last
        top = jnp.maximum(jnp.max(raw, 1, keepdims=True), jnp.max(far, 1, keepdims=True))
        weight = jnp.exp2(raw - top)
        far_weight = jnp.exp2(far - top)
        total = jnp.sum(weight, 1, keepdims=True) + jnp.sum(far_weight, 1, keepdims=True)
        mixed = dot_n(weight.astype(jnp.bfloat16), v_ref[:seen, :])
        mixed = mixed + dot_n(far_weight.astype(jnp.bfloat16), ov_ref[:seen, :])
        o_ref[rows, :] = (mixed / total).astype(o_ref.dtype)


def attend_shared(core, block_len, queries, keys_in, values_in, far_keys, far_values):
    length, width = queries.shape
    head_block = pl.BlockSpec((length, HEAD_DIM), lambda h: (0, h))
    return pl.pallas_call(
        functools.partial(shared_attend, block_len),
        grid=(width // HEAD_DIM,),
        in_specs=[pl.BlockSpec(memory_space=pltpu.SMEM)] + [head_block] * 5,
        out_specs=head_block,
        out_shape=jax.ShapeDtypeStruct((length, width), jnp.bfloat16),
        compiler_params=pltpu.CompilerParams(vmem_limit_bytes=32 * 2**20),
        cost_estimate=pl.CostEstimate(
            flops=4 * length * length * width, bytes_accessed=12 * length * width, transcendentals=0
        ),
        name="attend_shared",
    )(core.reshape(1), queries, keys_in, values_in, far_keys, far_values)


def whole_attend_back(
    q_ref, k_ref, v_ref, o_ref, do_ref, log_ref, cos_ref, sin_ref, dq_ref, dk_ref, dv_ref, dk_sum, dv_sum
):
    head = pl.program_id(0)
    length = q_ref.shape[0]
    lane = lax.broadcasted_iota(jnp.int32, (TILE, 128), 1)

    def unrotated(grads, rows):
        turned = pltpu.roll(grads, HEAD_DIM // 2, 1)
        return grads * cos_ref[rows, :] - turned * sin_ref[rows, :]

    for at in range(length // TILE):
        rows = pl.ds(at * TILE, TILE)
        seen = (at + 1) * TILE
        queries, d_mixed = q_ref[rows, :], do_ref[rows, :]
        log_total = jnp.sum(jnp.where(lane == head, log_ref[rows, :], 0.0), 1, keepdims=True)
        delta = jnp.sum(d_mixed.astype(jnp.float32) * o_ref[rows, :].astype(jnp.float32), 1, keepdims=True)
        raw = dot_t(queries, k_ref[:seen, :]) * (SCALE * LOG2E)
        last = jnp.where(below(TILE, TILE), raw[:, at * TILE :], NEG)
        raw = jnp.concatenate([raw[:, : at * TILE], last], 1) if at else last
        probs = jnp.exp2(raw - log_total)
        d_probs = dot_t(d_mixed, v_ref[:seen, :])
        slopes = (probs * (d_probs - delta)).astype(jnp.bfloat16)
        d_query = dot_n(slopes, k_ref[:seen, :]) * SCALE
        dq_ref[rows, :] = unrotated(d_query, rows).astype(dq_ref.dtype)
        d_value = dot_w(probs.astype(jnp.bfloat16), d_mixed)
        d_key = dot_w(slopes, queries)
        if at:
            before = pl.ds(0, at * TILE)
            dv_sum[before, :] += d_value[: at * TILE]
            dk_sum[before, :] += d_key[: at * TILE]
        dv_sum[rows, :] = d_value[at * TILE :]
        dk_sum[rows, :] = d_key[at * TILE :]
    everything = pl.ds(0, length)
    dk_ref[...] = unrotated(dk_sum[...] * SCALE, everything).astype(dk_ref.dtype)
    dv_ref[...] = dv_sum[...].astype(dv_ref.dtype)


def attend_whole_back(queries, keys_in, values_in, mixed, d_mixed, log_total, cos_full, sin_full):
    length, width = queries.shape
    head_block = pl.BlockSpec((length, HEAD_DIM), lambda h: (0, h))
    fixed = pl.BlockSpec((length, 128), lambda h: (0, 0))
    return pl.pallas_call(
        whole_attend_back,
        grid=(width // HEAD_DIM,),
        in_specs=[head_block] * 5 + [fixed] * 3,
        out_specs=[head_block] * 3,
        out_shape=[jax.ShapeDtypeStruct((length, width), jnp.bfloat16)] * 3,
        scratch_shapes=[pltpu.VMEM((length, HEAD_DIM), jnp.float32)] * 2,
        compiler_params=pltpu.CompilerParams(vmem_limit_bytes=40 * 2**20),
        cost_estimate=pl.CostEstimate(
            flops=5 * length * length * width, bytes_accessed=16 * length * width, transcendentals=0
        ),
        name="attend_whole_back",
    )(queries, keys_in, values_in, mixed, d_mixed, log_total, cos_full, sin_full)


def rope_full(positions):
    cosine, sine = rope_table(positions)
    return jnp.concatenate([cosine, cosine], 1), jnp.concatenate([-sine, sine], 1)


def rotate_rows(values, cos_full, sin_full):
    rows, width = values.shape
    heads = values.reshape(rows, width // HEAD_DIM, HEAD_DIM)
    half = HEAD_DIM // 2
    turned = jnp.concatenate([heads[..., half:], heads[..., :half]], -1)
    return (heads * cos_full[:, None] + turned * sin_full[:, None]).reshape(rows, width)


def paired_on_device(
    latents, embeds, cotangent, counts, w_adapt, w_query, w_key, w_value, w_out, w_gate, w_up, w_down, gains
):
    block_len, seqs, width = latents.shape
    parts = lax.axis_size("grp") * lax.axis_size("ctx")
    length = block_len * parts
    core = grid_place()[3]
    owner = core == 0

    twice = counts == 2
    slot = jnp.where(
        twice,
        2 * (jnp.cumsum(twice.astype(jnp.int32)) - 1),
        2 * (jnp.cumsum((~twice).astype(jnp.int32)) - 1) + 1,
    )
    row_count = block_len * seqs
    target = (slot[None, :] * block_len + jnp.arange(block_len, dtype=jnp.int32)[:, None]).reshape(row_count)
    order = (lax.broadcasted_iota(jnp.int32, (row_count, row_count), 0) == target[None, :]).astype(jnp.bfloat16)

    def to_slots(values):
        return dot_n(order, values.reshape(row_count, width)).astype(jnp.bfloat16)

    def from_slots(values):
        return dot_w(order, values.reshape(row_count, width)).astype(jnp.bfloat16)

    def exchange(values):
        return lax.all_to_all(values, BOTH, split_axis=0, concat_axis=0, tiled=True)

    adapt_w = gather_rows(w_adapt).reshape(-1, width)
    gain_rows = jnp.pad(gains.reshape(1, -1), ((0, 15), (0, width - gains.size)))
    side = w_query.shape[0]
    square = gather_rows(jnp.concatenate([w_query, w_key, w_value, w_out, gain_rows], 0))
    query_w, key_w, value_w, output_w = (
        square[:, at * side : (at + 1) * side].reshape(width, width) for at in range(4)
    )
    gain_float = (
        square[:, 4 * side, : gains.size]
        .reshape(parts, gains.shape[0], gains.shape[1])
        .transpose(1, 0, 2)
        .reshape(gains.shape[0], width)
        .astype(jnp.float32)
    )
    gate_w = gather_rows(w_gate).reshape(width, -1)
    up_w = gather_rows(w_up).reshape(width, -1)
    down_w = gather_rows(w_down).reshape(-1, width)

    latent_slots, embed_slots = to_slots(latents), to_slots(embeds)
    upstream = exchange(to_slots(cotangent).reshape(parts, block_len, width)).reshape(length, width)
    embed_part = dot_n(embed_slots, adapt_w[width:])
    adapted = (dot_n(latent_slots, adapt_w[:width]) + embed_part).reshape(parts, block_len, width)
    embed_part = embed_part.reshape(parts, block_len, width)
    pair_at = lax.broadcasted_iota(jnp.int32, (parts, 1, 1), 0) % 2
    starting = jnp.where(pair_at == 0, embed_part, adapted).astype(jnp.bfloat16)
    shared = adapted.reshape(parts // 2, 2, block_len, width)[:, 0].astype(jnp.bfloat16)
    shared = lax.all_to_all(
        shared,
        BOTH,
        split_axis=0,
        concat_axis=0,
        tiled=True,
        axis_index_groups=[list(range(k, parts, 2)) for k in range(2)],
    )
    starting = exchange(starting).reshape(length, width).astype(jnp.float32)

    def before_attention(resid, cos_full, sin_full):
        normed = (resid * rms_scale(resid) * gain_float[0]).astype(jnp.bfloat16)
        queries = rotate_rows(dot_n(normed, query_w), cos_full, sin_full).astype(jnp.bfloat16)
        keys_in = rotate_rows(dot_n(normed, key_w), cos_full, sin_full).astype(jnp.bfloat16)
        values_in = dot_n(normed, value_w).astype(jnp.bfloat16)
        return normed, queries, keys_in, values_in

    def after_attention(resid, mixed):
        branch = dot_n(mixed, output_w)
        middle = resid + branch * rms_scale(branch) * gain_float[1]
        mlp_in = (middle * rms_scale(middle) * gain_float[2]).astype(jnp.bfloat16)
        gate_pre = dot_n(mlp_in, gate_w)
        up_pre = dot_n(mlp_in, up_w)
        hidden = (jax.nn.silu(gate_pre) * up_pre).astype(jnp.bfloat16)
        down_out = dot_n(hidden, down_w)
        result = middle + down_out * rms_scale(down_out) * gain_float[3]
        return result.astype(jnp.bfloat16), (branch, middle, mlp_in, gate_pre, up_pre, hidden, down_out)

    resid = shared.reshape(length // 2, width).astype(jnp.float32)
    local = jnp.arange(length // 2, dtype=jnp.int32)
    cos_half, sin_half = rope_full((local // block_len * 2 + core) * block_len + local % block_len)
    normed, queries, keys_in, values_in = before_attention(resid, cos_half, sin_half)
    far_keys, far_values = send(keys_in, 3), send(values_in, 3)
    mixed = attend_shared(core, block_len, queries, keys_in, values_in, far_keys, far_values)
    first_out, _ = after_attention(resid, mixed)
    far_out = send(first_out, 3, -1)
    first_out = jnp.stack(
        [first_out.reshape(-1, block_len, width), far_out.reshape(-1, block_len, width)], 1
    ).reshape(length, width)
    first_out = jnp.where(owner, first_out, jnp.zeros_like(first_out))

    cos_full, sin_full = rope_full(jnp.arange(length, dtype=jnp.int32))
    resid = starting + dot_n(first_out, adapt_w[:width])
    normed, queries, keys_in, values_in = before_attention(resid, cos_full, sin_full)
    mixed, log_total = attend_whole(queries, keys_in, values_in)
    result, saved = after_attention(resid, mixed)
    branch, middle, mlp_in, gate_pre, up_pre, hidden, down_out = saved
    final_back = exchange(result.reshape(parts, block_len, width))

    d_result = upstream.astype(jnp.float32)
    d_down, gain_four = norm_back(down_out, d_result, gain_float[3])
    d_down = d_down.astype(jnp.bfloat16)
    down_part = dot_w(hidden, d_down).astype(jnp.bfloat16)
    d_hidden = dot_t(d_down, down_w)
    sigma = jax.nn.sigmoid(gate_pre)
    d_gate = (d_hidden * up_pre * sigma * (1.0 + gate_pre * (1.0 - sigma))).astype(jnp.bfloat16)
    d_up = (d_hidden * gate_pre * sigma).astype(jnp.bfloat16)
    gate_part = dot_w(mlp_in, d_gate).astype(jnp.bfloat16)
    up_part = dot_w(mlp_in, d_up).astype(jnp.bfloat16)
    d_mlp = dot_t(d_gate, gate_w) + dot_t(d_up, up_w)
    d_middle, gain_three = norm_back(middle, d_mlp, gain_float[2])
    d_middle = d_middle + d_result
    d_branch, gain_two = norm_back(branch, d_middle, gain_float[1])
    d_branch = d_branch.astype(jnp.bfloat16)
    out_part = dot_w(mixed, d_branch).astype(jnp.bfloat16)
    d_mixed = dot_t(d_branch, output_w).astype(jnp.bfloat16)
    d_query, d_key, d_value = attend_whole_back(
        queries, keys_in, values_in, mixed, d_mixed, log_total, cos_full, sin_full
    )
    query_part = dot_w(normed, d_query).astype(jnp.bfloat16)
    key_part = dot_w(normed, d_key).astype(jnp.bfloat16)
    value_part = dot_w(normed, d_value).astype(jnp.bfloat16)
    d_normed = dot_t(d_query, query_w) + dot_t(d_key, key_w) + dot_t(d_value, value_w)
    d_resid, gain_one = norm_back(resid, d_normed, gain_float[0])
    d_resid = (d_resid + d_middle).astype(jnp.bfloat16)
    d_home = exchange(d_resid.reshape(parts, block_len, width))
    first_part = dot_w(first_out, d_resid)

    d_home = from_slots(d_home)
    latent_back = dot_t(d_home, adapt_w[:width]).astype(jnp.bfloat16).reshape(latents.shape)
    embed_back = dot_t(d_home, adapt_w[width:]).astype(jnp.bfloat16).reshape(latents.shape)
    once = jnp.where(twice[None, :, None], jnp.zeros_like(latents), latents).reshape(row_count, width)
    latent_part = first_part + dot_w(once, d_home)
    embed_part = dot_w(embeds.reshape(row_count, width), d_home)
    final_back = from_slots(final_back).reshape(latents.shape)

    def blocks(part):
        return part.reshape(parts, -1, part.shape[-1])

    down_grad = scatter_rows(blocks(down_part))
    gate_grad = scatter_rows(blocks(gate_part))
    up_grad = scatter_rows(blocks(up_part))
    gain_part = jnp.stack([gain_one, gain_two, gain_three, gain_four])
    gain_part = gain_part.reshape(gains.shape[0], parts, gains.shape[1]).transpose(1, 0, 2)
    gain_part = jnp.pad(
        gain_part.reshape(parts, 1, gains.size).astype(jnp.bfloat16), ((0, 0), (0, 15), (0, width - gains.size))
    )
    square_grad = scatter_rows(
        jnp.concatenate(
            [blocks(query_part), blocks(key_part), blocks(value_part), blocks(out_part), gain_part], 1
        )
    )
    query_grad, key_grad, value_grad, out_grad = (square_grad[at * side : (at + 1) * side] for at in range(4))
    gain_grad = square_grad[4 * side, : gains.size].reshape(gains.shape)
    adapt_grad = scatter_rows(blocks(jnp.concatenate([latent_part, embed_part], 0).astype(jnp.bfloat16)))
    return (
        final_back,
        latent_back,
        embed_back,
        adapt_grad,
        query_grad,
        key_grad,
        value_grad,
        out_grad,
        gate_grad,
        up_grad,
        down_grad,
        gain_grad,
    )


def on_device(latents, *others):
    ctx = lax.axis_size("ctx")
    parts = lax.axis_size("grp") * ctx
    if latents.shape[1] == parts and ctx == 4 and latents.shape[0] % 16 == 0:
        return paired_on_device(latents, *others)
    return spread_on_device(latents, *others)


def solution(mesh):
    placed = (
        P(("grp", "ctx"), None, None),
        P(("grp", "ctx"), None, None),
        P(("grp", "ctx"), None, None),
        P(),
        P(("grp", "ctx"), None),
        P(("grp", "ctx"), None),
        P(("grp", "ctx"), None),
        P(("grp", "ctx"), None),
        P(("grp", "ctx"), None),
        P(("grp", "ctx"), None),
        P(("grp", "ctx"), None),
        P(("grp", "ctx"), None),
        P(None, ("grp", "ctx")),
    )
    return jax.shard_map(
        on_device,
        mesh=mesh,
        in_specs=placed,
        out_specs=(
            P(("grp", "ctx"), None, None),
            P(("grp", "ctx"), None, None),
            P(("grp", "ctx"), None, None),
            P(("grp", "ctx"), None),
            P(("grp", "ctx"), None),
            P(("grp", "ctx"), None),
            P(("grp", "ctx"), None),
            P(("grp", "ctx"), None),
            P(("grp", "ctx"), None),
            P(("grp", "ctx"), None),
            P(("grp", "ctx"), None),
            P(None, ("grp", "ctx")),
        ),
        check_vma=False,
    )
```

```python
import functools

import jax
import jax.numpy as jnp
from jax import lax
from jax.experimental import pallas as pl
from jax.experimental.pallas import tpu as pltpu
from jax.sharding import PartitionSpec as P

HEADS = 8
HEAD_DIM = 128


def rms_scale(values):
    return lax.rsqrt(jnp.mean(values * values, -1, keepdims=True) + 1e-06)


def norm_back(values, upstream, gain_vec):
    scale_rows = rms_scale(values)
    normal = values * scale_rows
    gain_part = jnp.sum(upstream * normal, 0)
    scaled = upstream * gain_vec
    return (
        scale_rows * (scaled - normal * jnp.mean(scaled * normal, -1, keepdims=True)),
        gain_part,
    )


def rope_table(positions):
    freq = 10000.0 ** (-2.0 * jnp.arange(HEAD_DIM // 2, dtype=jnp.float32) / HEAD_DIM)
    angle = positions.astype(jnp.float32)[:, None] * freq
    return (jnp.cos(angle), jnp.sin(angle))


def rotate(values, cosine, sine):
    half_dim = HEAD_DIM // 2
    first_half = values[..., :half_dim]
    second_half = values[..., half_dim:]
    cos_b = cosine[:, None, None, :]
    sin_b = sine[:, None, None, :]
    return jnp.concatenate(
        [first_half * cos_b - second_half * sin_b, second_half * cos_b + first_half * sin_b], -1
    )


def unrotate(grads, cosine, sine):
    half_dim = HEAD_DIM // 2
    first_half = grads[..., :half_dim]
    second_half = grads[..., half_dim:]
    cos_b = cosine[:, None, None, :]
    sin_b = sine[:, None, None, :]
    return jnp.concatenate(
        [first_half * cos_b + second_half * sin_b, second_half * cos_b - first_half * sin_b], -1
    )


def score_block(queries, keys_in, query_pos, key_pos_in):
    raw = jnp.einsum(
        "qshd,kshd->qshk", queries, keys_in, preferred_element_type=jnp.float32
    ) * HEAD_DIM ** (-0.5)
    causal = key_pos_in[None, :] <= query_pos[:, None]
    return jnp.where(causal[:, None, None, :], raw, -1e30)


def back_block(queries, keys_in, values_in, d_mixed, log_total, delta, query_pos, key_pos_in):
    scores = score_block(queries, keys_in, query_pos, key_pos_in)
    probs = jnp.exp(scores - log_total[..., None])
    d_probs = jnp.einsum("qshd,kshd->qshk", d_mixed, values_in, preferred_element_type=jnp.float32)
    slopes = (probs * (d_probs - delta[..., None])).astype(jnp.bfloat16)
    return (probs.astype(jnp.bfloat16), slopes)


def spread_on_device(
    latents,
    embeds,
    cotangent,
    counts,
    w_adapt,
    w_query,
    w_key,
    w_value,
    w_out,
    w_gate,
    w_up,
    w_down,
    gains,
):
    groups = lax.axis_size("grp")
    ctx_count = lax.axis_size("ctx")
    seq_total = latents.shape[1]
    seq_group = seq_total // groups
    block_len = latents.shape[0]
    model_width = latents.shape[2]
    group_len = groups * block_len
    adapt_w, query_w, key_w, value_w, output_w, gate_w, up_w, down_w, gain_rows = (
        lax.all_gather(w_adapt, ("grp", "ctx"), axis=0, tiled=True),
        lax.all_gather(w_query, ("grp", "ctx"), axis=0, tiled=True),
        lax.all_gather(w_key, ("grp", "ctx"), axis=0, tiled=True),
        lax.all_gather(w_value, ("grp", "ctx"), axis=0, tiled=True),
        lax.all_gather(w_out, ("grp", "ctx"), axis=0, tiled=True),
        lax.all_gather(w_gate, ("grp", "ctx"), axis=0, tiled=True),
        lax.all_gather(w_up, ("grp", "ctx"), axis=0, tiled=True),
        lax.all_gather(w_down, ("grp", "ctx"), axis=0, tiled=True),
        lax.all_gather(gains, ("grp", "ctx"), axis=1, tiled=True),
    )
    gain_float = gain_rows.astype(jnp.float32)
    seq_order = jnp.arange(seq_total, dtype=jnp.int32)
    latent_in, embed_in, slope_in = (
        lax.all_to_all(
            jnp.take(latents, seq_order, axis=1), "grp", split_axis=1, concat_axis=0, tiled=True
        ),
        lax.all_to_all(
            jnp.take(embeds, seq_order, axis=1), "grp", split_axis=1, concat_axis=0, tiled=True
        ),
        lax.all_to_all(
            jnp.take(cotangent, seq_order, axis=1), "grp", split_axis=1, concat_axis=0, tiled=True
        ),
    )
    ctx_index = lax.axis_index("ctx")

    def key_position(flat_index):
        source = flat_index // group_len
        within = flat_index % group_len
        return (within // block_len * ctx_count + source) * block_len + within % block_len

    query_pos = key_position(ctx_index * group_len + jnp.arange(group_len, dtype=jnp.int32))
    cos_query, sin_query = rope_table(query_pos)

    def attend_forward(queries, keys_in, values_in):
        piece = lax.all_gather(keys_in, "ctx", axis=0, tiled=True)
        scores = score_block(
            queries, piece, query_pos, key_position(jnp.arange(piece.shape[0], dtype=jnp.int32))
        )
        log_total = jax.nn.logsumexp(scores, -1)
        probs = jnp.exp(scores - log_total[..., None]).astype(jnp.bfloat16)
        mixed_raw = jnp.einsum(
            "qshk,kshd->qshd",
            probs,
            lax.all_gather(values_in, "ctx", axis=0, tiled=True),
            preferred_element_type=jnp.float32,
        )
        return (mixed_raw.astype(jnp.bfloat16), (queries, keys_in, values_in, log_total, mixed_raw))

    def core_block(latent, embedding):
        seq_batch = latent.shape[1]
        row_count = group_len * seq_batch
        joined = jnp.concatenate([latent.astype(jnp.bfloat16), embedding], -1).reshape(
            row_count, 2 * model_width
        )
        resid = jnp.dot(joined, adapt_w, preferred_element_type=jnp.float32)
        normed = (resid * rms_scale(resid) * gain_float[0]).astype(jnp.bfloat16)

        def heads_of(matrix):
            return jnp.dot(normed, matrix, preferred_element_type=jnp.float32).reshape(
                group_len, seq_batch, HEADS, HEAD_DIM
            )

        queries = rotate(heads_of(query_w), cos_query, sin_query).astype(jnp.bfloat16)
        keys_in = rotate(heads_of(key_w), cos_query, sin_query).astype(jnp.bfloat16)
        values_in = heads_of(value_w).astype(jnp.bfloat16)
        mixed, kept = attend_forward(queries, keys_in, values_in)
        mixed_flat = mixed.reshape(row_count, model_width)
        branch = jnp.dot(mixed_flat, output_w, preferred_element_type=jnp.float32)
        middle = resid + branch * rms_scale(branch) * gain_float[1]
        mlp_in = (middle * rms_scale(middle) * gain_float[2]).astype(jnp.bfloat16)
        gate_pre = jnp.dot(mlp_in, gate_w, preferred_element_type=jnp.float32)
        up_pre = jnp.dot(mlp_in, up_w, preferred_element_type=jnp.float32)
        hidden = (jax.nn.silu(gate_pre) * up_pre).astype(jnp.bfloat16)
        down_out = jnp.dot(hidden, down_w, preferred_element_type=jnp.float32)
        result = middle + down_out * rms_scale(down_out) * gain_float[3]
        flat_saved = tuple(
            (
                stored.reshape(group_len, seq_batch, stored.shape[-1])
                for stored in (
                    joined,
                    resid,
                    normed,
                    mixed_flat,
                    branch,
                    middle,
                    mlp_in,
                    gate_pre,
                    up_pre,
                    hidden,
                    down_out,
                )
            )
        )
        return (result.reshape(group_len, seq_batch, model_width), (flat_saved, kept))

    group_counts = lax.dynamic_slice_in_dim(
        jnp.take(counts, seq_order), lax.axis_index("grp") * seq_group, seq_group
    )
    first_out, first_saved = core_block(latent_in, embed_in)
    last_in = jnp.where(group_counts[None, :, None] == 2, first_out, latent_in.astype(jnp.float32))
    final_out, saved = core_block(last_in, embed_in)
    upstream = slope_in.astype(jnp.float32)
    flat_saved, kept = saved
    (
        joined,
        resid,
        normed,
        mixed_flat,
        branch,
        middle,
        mlp_in,
        gate_pre,
        up_pre,
        hidden,
        down_out,
    ) = tuple((stored.reshape(-1, stored.shape[-1]) for stored in flat_saved))
    seq_batch = upstream.shape[1]
    d_result = upstream.reshape(-1, model_width)
    d_down, gain_four = norm_back(down_out, d_result, gain_float[3])
    d_down = d_down.astype(jnp.bfloat16)
    down_part = jnp.einsum("rf,rd->fd", hidden, d_down, preferred_element_type=jnp.float32)
    d_hidden = jnp.einsum("rd,fd->rf", d_down, down_w, preferred_element_type=jnp.float32)
    sigma = jax.nn.sigmoid(gate_pre)
    d_gate = (d_hidden * up_pre * sigma * (1.0 + gate_pre * (1.0 - sigma))).astype(jnp.bfloat16)
    d_up = (d_hidden * gate_pre * sigma).astype(jnp.bfloat16)
    gate_part = jnp.einsum("rd,rf->df", mlp_in, d_gate, preferred_element_type=jnp.float32)
    up_part = jnp.einsum("rd,rf->df", mlp_in, d_up, preferred_element_type=jnp.float32)
    d_mlp = jnp.einsum(
        "rf,df->rd", d_gate, gate_w, preferred_element_type=jnp.float32
    ) + jnp.einsum("rf,df->rd", d_up, up_w, preferred_element_type=jnp.float32)
    d_middle, gain_three = norm_back(middle, d_mlp, gain_float[2])
    d_middle = d_middle + d_result
    d_branch, gain_two = norm_back(branch, d_middle, gain_float[1])
    d_branch = d_branch.astype(jnp.bfloat16)
    out_part = jnp.einsum("re,rd->ed", mixed_flat, d_branch, preferred_element_type=jnp.float32)
    d_mixed = jnp.einsum(
        "rd,ed->re", d_branch, output_w, preferred_element_type=jnp.float32
    ).astype(jnp.bfloat16)
    attend_d_mixed = d_mixed.reshape(group_len, seq_batch, HEADS, HEAD_DIM)
    queries, keys_in, values_in, log_total, mixed_raw = kept
    delta = jnp.sum(attend_d_mixed.astype(jnp.float32) * mixed_raw, -1)
    key_part = lax.all_gather(keys_in, "ctx", axis=0, tiled=True)
    value_part = lax.all_gather(values_in, "ctx", axis=0, tiled=True)
    key_pos_in = key_position(jnp.arange(key_part.shape[0], dtype=jnp.int32))
    probs_low, slopes = back_block(
        queries, key_part, value_part, attend_d_mixed, log_total, delta, query_pos, key_pos_in
    )
    d_query = HEAD_DIM ** (-0.5) * jnp.einsum(
        "qshk,kshd->qshd", slopes, key_part, preferred_element_type=jnp.float32
    )
    pull_stacked = jnp.stack([probs_low, slopes])
    d_query, stacked = (d_query, pull_stacked)
    d_key = HEAD_DIM ** (-0.5) * jnp.einsum(
        "qshk,qshd->kshd", stacked[1], queries, preferred_element_type=jnp.float32
    )
    d_value = jnp.einsum(
        "qshk,qshd->kshd", stacked[0], attend_d_mixed, preferred_element_type=jnp.float32
    )
    paired = lax.psum_scatter(
        jnp.concatenate([d_key, d_value], -1).astype(jnp.bfloat16),
        "ctx",
        scatter_dimension=0,
        tiled=True,
    ).astype(jnp.float32)
    d_query, d_key, d_value = (
        unrotate(d_query, cos_query, sin_query).astype(jnp.bfloat16),
        unrotate(paired[..., :HEAD_DIM], cos_query, sin_query).astype(jnp.bfloat16),
        paired[..., HEAD_DIM:].astype(jnp.bfloat16),
    )
    d_query = d_query.reshape(-1, model_width)
    d_key = d_key.reshape(-1, model_width)
    d_value = d_value.reshape(-1, model_width)
    query_part = jnp.einsum("rd,re->de", normed, d_query, preferred_element_type=jnp.float32)
    key_part = jnp.einsum("rd,re->de", normed, d_key, preferred_element_type=jnp.float32)
    value_part = jnp.einsum("rd,re->de", normed, d_value, preferred_element_type=jnp.float32)
    d_normed = (
        jnp.einsum("re,de->rd", d_query, query_w, preferred_element_type=jnp.float32)
        + jnp.einsum("re,de->rd", d_key, key_w, preferred_element_type=jnp.float32)
        + jnp.einsum("re,de->rd", d_value, value_w, preferred_element_type=jnp.float32)
    )
    d_resid, gain_one = norm_back(resid, d_normed, gain_float[0])
    d_resid = (d_resid + d_middle).astype(jnp.bfloat16)
    adapt_part = jnp.einsum("rk,rd->kd", joined, d_resid, preferred_element_type=jnp.float32)
    d_joined = jnp.einsum("rd,kd->rk", d_resid, adapt_w, preferred_element_type=jnp.float32)
    gain_part = jnp.stack([gain_one, gain_two, gain_three, gain_four])
    d_joined, grads = (
        d_joined.reshape(group_len, seq_batch, 2 * model_width),
        (
            adapt_part,
            query_part,
            key_part,
            value_part,
            out_part,
            gate_part,
            up_part,
            down_part,
            gain_part,
        ),
    )
    final_back, latent_back, embed_back = (
        lax.all_to_all(
            final_out.astype(jnp.bfloat16), "grp", split_axis=0, concat_axis=1, tiled=True
        ),
        lax.all_to_all(
            d_joined[..., :model_width].astype(jnp.bfloat16),
            "grp",
            split_axis=0,
            concat_axis=1,
            tiled=True,
        ),
        lax.all_to_all(
            d_joined[..., model_width:].astype(jnp.bfloat16),
            "grp",
            split_axis=0,
            concat_axis=1,
            tiled=True,
        ),
    )
    seq_index = jnp.arange(seq_total, dtype=jnp.int32)
    inverse = jnp.sum(jnp.where(seq_order[:, None] == seq_index[None, :], seq_index[:, None], 0), 0)
    (
        adapt_part,
        query_part,
        key_part,
        value_part,
        out_part,
        gate_part,
        up_part,
        down_part,
        gain_part,
    ) = grads
    summed = (
        lax.psum_scatter(adapt_part, ("grp", "ctx"), scatter_dimension=0, tiled=True),
        lax.psum_scatter(query_part, ("grp", "ctx"), scatter_dimension=0, tiled=True),
        lax.psum_scatter(key_part, ("grp", "ctx"), scatter_dimension=0, tiled=True),
        lax.psum_scatter(value_part, ("grp", "ctx"), scatter_dimension=0, tiled=True),
        lax.psum_scatter(out_part, ("grp", "ctx"), scatter_dimension=0, tiled=True),
        lax.psum_scatter(gate_part, ("grp", "ctx"), scatter_dimension=0, tiled=True),
        lax.psum_scatter(up_part, ("grp", "ctx"), scatter_dimension=0, tiled=True),
        lax.psum_scatter(down_part, ("grp", "ctx"), scatter_dimension=0, tiled=True),
        lax.psum_scatter(gain_part, ("grp", "ctx"), scatter_dimension=1, tiled=True),
    )
    return (
        jnp.take(final_back, inverse, axis=1),
        jnp.take(latent_back, inverse, axis=1),
        jnp.take(embed_back, inverse, axis=1),
        summed[0],
        summed[1],
        summed[2],
        summed[3],
        summed[4],
        summed[5],
        summed[6],
        summed[7],
        summed[8],
    )


BOTH = ("grp", "ctx")
LOG2E = 1.4426950408889634
SCALE = HEAD_DIM ** (-0.5)
TILE = 256
NEG = -1e30


def grid_sizes():
    ctx = lax.axis_size("ctx")
    x_size = ctx // 2
    return lax.axis_size("grp") // x_size, x_size, x_size, 2


def grid_place():
    z_size, y_size, x_size, k_size = grid_sizes()
    g, c = lax.axis_index("grp"), lax.axis_index("ctx")
    return g // y_size, g % y_size, c // k_size, c % k_size


def send(values, axis, shift=None, keep=None):
    sizes = grid_sizes()
    pairs = []
    for flat in range(sizes[0] * sizes[1] * sizes[2] * sizes[3]):
        rest, spot = flat, [0, 0, 0, 0]
        for at in (3, 2, 1, 0):
            spot[at] = rest % sizes[at]
            rest //= sizes[at]
        own = spot[axis]
        other = 1 - own if shift is None else own + shift
        if 0 <= other < sizes[axis] and (keep is None or keep(own)):
            spot[axis] = other
            target = ((spot[0] * sizes[1] + spot[1]) * sizes[2] + spot[2]) * sizes[3] + spot[3]
            pairs.append((flat, target))
    return lax.ppermute(values, BOTH, pairs)


MESH = pl.DeviceIdType.MESH


def device_at(z, y, x, k):
    _, y_size, _, k_size = grid_sizes()
    return (z * y_size + y, x * k_size + k)


def order_of(z, y, x, half, slot_z):
    high = slot_z // half
    first = (y + high * (1 - 2 * y), x + (1 - high) * (1 - 2 * x))
    second = (y + (1 - high) * (1 - 2 * y), x + high * (1 - 2 * x))
    return first, second


def greet(devices):
    barrier = pltpu.get_barrier_semaphore()
    for device in devices:
        pl.semaphore_signal(barrier, inc=1, device_id=device, device_id_type=MESH)
    pl.semaphore_wait(barrier, len(devices))


def greet_line(z, y, x, k, z_size):
    barrier = pltpu.get_barrier_semaphore()
    for device in (device_at(z, 1 - y, x, k), device_at(z, y, 1 - x, k), device_at(z, y, x, 1 - k)):
        pl.semaphore_signal(barrier, inc=1, device_id=device, device_id_type=MESH)

    @pl.when(z > 0)
    def _():
        pl.semaphore_signal(barrier, inc=1, device_id=device_at(z - 1, y, x, k), device_id_type=MESH)

    @pl.when(z < z_size - 1)
    def _():
        pl.semaphore_signal(barrier, inc=1, device_id=device_at(z + 1, y, x, k), device_id_type=MESH)

    pl.semaphore_wait(barrier, 3 + jnp.minimum(z, 1) + jnp.minimum(z_size - 1 - z, 1))


def remote(source, target, send_sem, recv_sem, device):
    return pltpu.make_async_remote_copy(
        src_ref=source,
        dst_ref=target,
        send_sem=send_sem,
        recv_sem=recv_sem,
        device_id=device,
        device_id_type=MESH,
    )


def gather_kernel(count, *refs):
    z_size, _, _, _ = grid_sizes()
    z, y, x, k = grid_place()
    half = z_size // 2
    shards, outs = refs[:count], refs[count : 2 * count]
    local_sem, z_send, z_recv, p_send, p_recv, k_send, k_recv = refs[2 * count :]
    greet_line(z, y, x, k, z_size)

    def z_copy(g, slot_z, way):
        spot = outs[g].at[slot_z, y, x, k]
        side = z + 1 - 2 * way
        return remote(spot, spot, z_send.at[g, slot_z, way], z_recv.at[g, slot_z], device_at(side, y, x, k))

    def plane_copy(g, slot_z, kind):
        first, second = order_of(z, y, x, half, slot_z)
        from_at = first if kind == 2 else (y, x)
        to_at = first if kind == 0 else second
        spot = outs[g].at[slot_z, from_at[0], from_at[1], k]
        return remote(
            spot, spot, p_send.at[g, slot_z, kind], p_recv.at[g, slot_z, kind], device_at(z, to_at[0], to_at[1], k)
        )

    def core_copy(g, slot_z):
        spot = outs[g].at[slot_z, :, :, k]
        return remote(spot, spot, k_send.at[g, slot_z], k_recv.at[g, slot_z], device_at(z, y, x, 1 - k))

    def spread_z(g, slot_z, up, down):
        if up:

            @pl.when(z < z_size - 1)
            def _():
                z_copy(g, slot_z, 0).start()

        if down:

            @pl.when(z > 0)
            def _():
                z_copy(g, slot_z, 1).start()

    def at_offsets(step, body):
        if step == 0:
            body(z, True, True)
            return

        @pl.when(z >= step)
        def _():
            body(z - step, True, False)

        @pl.when(z + step < z_size)
        def _():
            body(z + step, False, True)

    own = [pltpu.make_async_copy(shards[g], outs[g].at[z, y, x, k], local_sem.at[g]) for g in range(count)]
    for copy in own:
        copy.start()
    for step in range(z_size):
        for g in range(count):
            if step == 0:
                own[g].wait()

            def arrive(slot_z, up, down, g=g):
                if not (up and down):
                    z_copy(g, slot_z, 1 if up else 0).wait_recv()
                spread_z(g, slot_z, up, down)
                plane_copy(g, slot_z, 0).start()
                plane_copy(g, slot_z, 1).start()

            at_offsets(step, arrive)
        for g in range(count):

            def pass_on(slot_z, up, down, g=g):
                plane_copy(g, slot_z, 0).wait_recv()
                plane_copy(g, slot_z, 2).start()

            at_offsets(step, pass_on)
        if step > 0:
            for g in range(count):

                def cross(slot_z, up, down, g=g):
                    plane_copy(g, slot_z, 1).wait_recv()
                    plane_copy(g, slot_z, 2).wait_recv()
                    core_copy(g, slot_z).start()

                at_offsets(step - 1, cross)
    for g in range(count):

        def cross_last(slot_z, up, down, g=g):
            plane_copy(g, slot_z, 1).wait_recv()
            plane_copy(g, slot_z, 2).wait_recv()
            core_copy(g, slot_z).start()

        at_offsets(z_size - 1, cross_last)
    for g in range(count):
        for slot_z in range(z_size):
            core_copy(g, slot_z).wait()
            for kind in range(3):
                plane_copy(g, slot_z, kind).wait_send()
    for step in range(z_size):
        for g in range(count):

            def settle(slot_z, up, down, g=g):
                if up:

                    @pl.when(z < z_size - 1)
                    def _():
                        z_copy(g, slot_z, 0).wait_send()

                if down:

                    @pl.when(z > 0)
                    def _():
                        z_copy(g, slot_z, 1).wait_send()

            at_offsets(step, settle)


def gather_all(shards, collective_id):
    sizes = grid_sizes()
    count, z_size = len(shards), sizes[0]
    anywhere = pl.BlockSpec(memory_space=pl.ANY)
    dma = pltpu.SemaphoreType.DMA
    return pl.pallas_call(
        functools.partial(gather_kernel, count),
        in_specs=[anywhere] * count,
        out_specs=[anywhere] * count,
        out_shape=[jax.ShapeDtypeStruct(sizes + shard.shape, shard.dtype) for shard in shards],
        scratch_shapes=[
            dma((count,)),
            dma((count, z_size, 2)),
            dma((count, z_size)),
            dma((count, z_size, 3)),
            dma((count, z_size, 3)),
            dma((count, z_size)),
            dma((count, z_size)),
        ],
        compiler_params=pltpu.CompilerParams(collective_id=collective_id, has_side_effects=True),
        name="gather_weights",
    )(*shards)


def scatter_kernel(count, *refs):
    z_size, _, _, _ = grid_sizes()
    z, y, x, k = grid_place()
    half = z_size // 2
    parts, outs = refs[:count], refs[count : 2 * count]
    held, from_core = refs[2 * count : 3 * count], refs[3 * count : 4 * count]
    from_second, from_first = refs[4 * count : 5 * count], refs[5 * count : 6 * count]
    from_z = refs[6 * count : 7 * count]
    local_sem, k_send, k_recv, p_send, p_recv, z_send, z_recv = refs[7 * count :]
    greet_line(z, y, x, k, z_size)

    def core_copy(g, slot_z):
        return remote(
            parts[g].at[slot_z, :, :, 1 - k],
            from_core[g].at[slot_z],
            k_send.at[g, slot_z],
            k_recv.at[g, slot_z],
            device_at(z, y, x, 1 - k),
        )

    def own_copy(g, slot_z):
        return pltpu.make_async_copy(parts[g].at[slot_z, :, :, k], held[g].at[slot_z], local_sem.at[g, slot_z])

    def second_copy(g, slot_z, kind):
        _, second = order_of(z, y, x, half, slot_z)
        at = second if kind == 0 else (1 - y, 1 - x)
        return remote(
            held[g].at[slot_z, at[0], at[1]],
            from_second[g].at[slot_z, kind],
            p_send.at[g, slot_z, kind],
            p_recv.at[g, slot_z, kind],
            device_at(z, second[0], second[1], k),
        )

    def first_copy(g, slot_z):
        first, _ = order_of(z, y, x, half, slot_z)
        return remote(
            held[g].at[slot_z, first[0], first[1]],
            from_first[g].at[slot_z],
            p_send.at[g, slot_z, 2],
            p_recv.at[g, slot_z, 2],
            device_at(z, first[0], first[1], k),
        )

    def z_copy(g, step, way):
        slot_z = z + (1 - 2 * way) * (z_size - step)
        return remote(
            held[g].at[slot_z, y, x],
            from_z[g].at[step - 1, way],
            z_send.at[g, step - 1, way],
            z_recv.at[g, step - 1, way],
            device_at(z + 1 - 2 * way, y, x, k),
        )

    def z_wait(g, step, way):
        remote(
            held[g].at[z, y, x],
            from_z[g].at[step - 1, way],
            z_send.at[g, step - 1, way],
            z_recv.at[g, step - 1, way],
            device_at(z - 1 + 2 * way, y, x, k),
        ).wait_recv()

    def add(ref, at, other, other_at):
        total = ref[at].astype(jnp.float32) + other[other_at].astype(jnp.float32)
        ref[at] = total.astype(ref.dtype)

    for slot_z in range(z_size):
        for g in range(count):
            core_copy(g, slot_z).start()
            own_copy(g, slot_z).start()
    for slot_z in range(z_size):
        first, second = order_of(z, y, x, half, slot_z)
        for g in range(count):
            own_copy(g, slot_z).wait()
            core_copy(g, slot_z).wait_recv()
            for at in (second, (1 - y, 1 - x)):
                add(held[g], (slot_z, at[0], at[1]), from_core[g], (slot_z, at[0], at[1]))
            second_copy(g, slot_z, 0).start()
            second_copy(g, slot_z, 1).start()
            for at in (first, (y, x)):
                add(held[g], (slot_z, at[0], at[1]), from_core[g], (slot_z, at[0], at[1]))
    for slot_z in range(z_size):
        first, second = order_of(z, y, x, half, slot_z)
        for g in range(count):
            second_copy(g, slot_z, 1).wait_recv()
            add(held[g], (slot_z, first[0], first[1]), from_second[g], (slot_z, 1))
            first_copy(g, slot_z).start()
    for slot_z in range(z_size):
        for g in range(count):
            second_copy(g, slot_z, 0).wait_recv()
            add(held[g], (slot_z, y, x), from_second[g], (slot_z, 0))
            first_copy(g, slot_z).wait_recv()
            add(held[g], (slot_z, y, x), from_first[g], (slot_z,))
    for step in range(1, z_size):
        for way in range(2):
            for g in range(count):
                goes = z <= step - 1 if way == 0 else z >= z_size - step
                came = (z >= 1) & (z <= step - 1) if way == 0 else (z <= z_size - 2) & (z >= z_size - step)

                @pl.when(goes)
                def _(g=g, step=step, way=way, came=came):
                    slot_z = z + (1 - 2 * way) * (z_size - step)
                    if step > 1:

                        @pl.when(came)
                        def _():
                            z_wait(g, step - 1, way)
                            add(held[g], (slot_z, y, x), from_z[g], (step - 2, way))

                    z_copy(g, step, way).start()

    for g in range(count):
        total = held[g][z, y, x].astype(jnp.float32)
        outs[g][...] = total
        for way in range(2):

            @pl.when(z > 0 if way == 0 else z < z_size - 1)
            def _(g=g, way=way):
                z_wait(g, z_size - 1, way)
                outs[g][...] += from_z[g][z_size - 2, way].astype(jnp.float32)

    for g in range(count):
        for slot_z in range(z_size):
            core_copy(g, slot_z).wait_send()
            second_copy(g, slot_z, 0).wait_send()
            second_copy(g, slot_z, 1).wait_send()
            first_copy(g, slot_z).wait_send()
        for step in range(1, z_size):
            for way in range(2):

                @pl.when(z <= step - 1 if way == 0 else z >= z_size - step)
                def _(g=g, step=step, way=way):
                    z_copy(g, step, way).wait_send()


def scatter_all(parts, collective_id):
    sizes = grid_sizes()
    count, (z_size, y_size, x_size, _) = len(parts), sizes
    shapes = [part.shape[1:] for part in parts]
    dma = pltpu.SemaphoreType.DMA
    plane = (z_size, y_size, x_size)

    def buffers(lead):
        return [pltpu.VMEM(lead + shape, jnp.bfloat16) for shape in shapes]

    return pl.pallas_call(
        functools.partial(scatter_kernel, count),
        in_specs=[pl.BlockSpec(memory_space=pl.ANY)] * count,
        out_specs=[pl.BlockSpec(memory_space=pltpu.VMEM)] * count,
        out_shape=[jax.ShapeDtypeStruct(shape, jnp.float32) for shape in shapes],
        scratch_shapes=buffers(plane)
        + buffers(plane)
        + buffers((z_size, 2))
        + buffers((z_size,))
        + buffers((z_size - 1, 2))
        + [
            dma((count, z_size)),
            dma((count, z_size)),
            dma((count, z_size)),
            dma((count, z_size, 3)),
            dma((count, z_size, 3)),
            dma((count, z_size - 1, 2)),
            dma((count, z_size - 1, 2)),
        ],
        compiler_params=pltpu.CompilerParams(
            collective_id=collective_id, has_side_effects=True, vmem_limit_bytes=56 * 2**20
        ),
        name="scatter_sums",
    )(*(part.reshape(sizes + part.shape[1:]) for part in parts))


def dot_t(left, right):
    return lax.dot_general(left, right, (((1,), (1,)), ((), ())), preferred_element_type=jnp.float32)


def dot_n(left, right):
    return jnp.dot(left, right, preferred_element_type=jnp.float32)


def dot_w(left, right):
    return lax.dot_general(left, right, (((0,), (0,)), ((), ())), preferred_element_type=jnp.float32)


def below(rows, columns):
    at_row = lax.broadcasted_iota(jnp.int32, (rows, columns), 0)
    at_column = lax.broadcasted_iota(jnp.int32, (rows, columns), 1)
    return at_column <= at_row


def whole_attend(q_ref, k_ref, v_ref, o_ref, log_ref):
    head = pl.program_id(0)
    length = q_ref.shape[0]
    lane = lax.broadcasted_iota(jnp.int32, (TILE, 128), 1)
    for at in range(length // TILE):
        rows = pl.ds(at * TILE, TILE)
        seen = (at + 1) * TILE
        raw = dot_t(q_ref[rows, :], k_ref[:seen, :]) * (SCALE * LOG2E)
        last = jnp.where(below(TILE, TILE), raw[:, at * TILE :], NEG)
        raw = jnp.concatenate([raw[:, : at * TILE], last], 1) if at else last
        top = jnp.max(raw, 1, keepdims=True)
        weight = jnp.exp2(raw - top)
        total = jnp.sum(weight, 1, keepdims=True)
        mixed = dot_n(weight.astype(jnp.bfloat16), v_ref[:seen, :])
        o_ref[rows, :] = (mixed / total).astype(o_ref.dtype)
        log_total = top + jnp.log2(total)
        log_ref[rows, :] = jnp.where(lane == head, log_total, log_ref[rows, :])


def attend_whole(queries, keys_in, values_in):
    length, width = queries.shape
    head_block = pl.BlockSpec((length, HEAD_DIM), lambda h: (0, h))
    return pl.pallas_call(
        whole_attend,
        grid=(width // HEAD_DIM,),
        in_specs=[head_block] * 3,
        out_specs=[head_block, pl.BlockSpec((length, 128), lambda h: (0, 0))],
        out_shape=[
            jax.ShapeDtypeStruct((length, width), jnp.bfloat16),
            jax.ShapeDtypeStruct((length, 128), jnp.float32),
        ],
        compiler_params=pltpu.CompilerParams(vmem_limit_bytes=32 * 2**20),
        cost_estimate=pl.CostEstimate(
            flops=2 * length * length * width, bytes_accessed=8 * length * width, transcendentals=0
        ),
        name="attend_whole",
    )(queries, keys_in, values_in)


def shared_attend(block_len, core_ref, q_ref, k_ref, v_ref, ok_ref, ov_ref, o_ref):
    core = core_ref[0]
    length = q_ref.shape[0]
    for at in range(length // TILE):
        rows = pl.ds(at * TILE, TILE)
        seen = (at + 1) * TILE
        queries = q_ref[rows, :]
        raw = dot_t(queries, k_ref[:seen, :]) * (SCALE * LOG2E)
        far = dot_t(queries, ok_ref[:seen, :]) * (SCALE * LOG2E)
        at_row = lax.broadcasted_iota(jnp.int32, (TILE, TILE), 0)
        at_column = lax.broadcasted_iota(jnp.int32, (TILE, TILE), 1)
        near_last = jnp.where(at_column <= at_row, raw[:, at * TILE :], NEG)
        far_ok = at_column // block_len < at_row // block_len + core
        far_last = jnp.where(far_ok, far[:, at * TILE :], NEG)
        raw = jnp.concatenate([raw[:, : at * TILE], near_last], 1) if at else near_last
        far = jnp.concatenate([far[:, : at * TILE], far_last], 1) if at else far_last
        top = jnp.maximum(jnp.max(raw, 1, keepdims=True), jnp.max(far, 1, keepdims=True))
        weight = jnp.exp2(raw - top)
        far_weight = jnp.exp2(far - top)
        total = jnp.sum(weight, 1, keepdims=True) + jnp.sum(far_weight, 1, keepdims=True)
        mixed = dot_n(weight.astype(jnp.bfloat16), v_ref[:seen, :])
        mixed = mixed + dot_n(far_weight.astype(jnp.bfloat16), ov_ref[:seen, :])
        o_ref[rows, :] = (mixed / total).astype(o_ref.dtype)


def attend_shared(core, block_len, queries, keys_in, values_in, far_keys, far_values):
    length, width = queries.shape
    head_block = pl.BlockSpec((length, HEAD_DIM), lambda h: (0, h))
    return pl.pallas_call(
        functools.partial(shared_attend, block_len),
        grid=(width // HEAD_DIM,),
        in_specs=[pl.BlockSpec(memory_space=pltpu.SMEM)] + [head_block] * 5,
        out_specs=head_block,
        out_shape=jax.ShapeDtypeStruct((length, width), jnp.bfloat16),
        compiler_params=pltpu.CompilerParams(vmem_limit_bytes=32 * 2**20),
        cost_estimate=pl.CostEstimate(
            flops=4 * length * length * width, bytes_accessed=12 * length * width, transcendentals=0
        ),
        name="attend_shared",
    )(core.reshape(1), queries, keys_in, values_in, far_keys, far_values)


def whole_attend_back(
    q_ref, k_ref, v_ref, o_ref, do_ref, log_ref, cos_ref, sin_ref, dq_ref, dk_ref, dv_ref, dk_sum, dv_sum
):
    head = pl.program_id(0)
    length = q_ref.shape[0]
    lane = lax.broadcasted_iota(jnp.int32, (TILE, 128), 1)

    def unrotated(grads, rows):
        turned = pltpu.roll(grads, HEAD_DIM // 2, 1)
        return grads * cos_ref[rows, :] - turned * sin_ref[rows, :]

    for at in range(length // TILE):
        rows = pl.ds(at * TILE, TILE)
        seen = (at + 1) * TILE
        queries, d_mixed = q_ref[rows, :], do_ref[rows, :]
        log_total = jnp.sum(jnp.where(lane == head, log_ref[rows, :], 0.0), 1, keepdims=True)
        delta = jnp.sum(d_mixed.astype(jnp.float32) * o_ref[rows, :].astype(jnp.float32), 1, keepdims=True)
        raw = dot_t(queries, k_ref[:seen, :]) * (SCALE * LOG2E)
        last = jnp.where(below(TILE, TILE), raw[:, at * TILE :], NEG)
        raw = jnp.concatenate([raw[:, : at * TILE], last], 1) if at else last
        probs = jnp.exp2(raw - log_total)
        d_probs = dot_t(d_mixed, v_ref[:seen, :])
        slopes = (probs * (d_probs - delta)).astype(jnp.bfloat16)
        d_query = dot_n(slopes, k_ref[:seen, :]) * SCALE
        dq_ref[rows, :] = unrotated(d_query, rows).astype(dq_ref.dtype)
        d_value = dot_w(probs.astype(jnp.bfloat16), d_mixed)
        d_key = dot_w(slopes, queries)
        if at:
            before = pl.ds(0, at * TILE)
            dv_sum[before, :] += d_value[: at * TILE]
            dk_sum[before, :] += d_key[: at * TILE]
        dv_sum[rows, :] = d_value[at * TILE :]
        dk_sum[rows, :] = d_key[at * TILE :]
    everything = pl.ds(0, length)
    dk_ref[...] = unrotated(dk_sum[...] * SCALE, everything).astype(dk_ref.dtype)
    dv_ref[...] = dv_sum[...].astype(dv_ref.dtype)


def attend_whole_back(queries, keys_in, values_in, mixed, d_mixed, log_total, cos_full, sin_full):
    length, width = queries.shape
    head_block = pl.BlockSpec((length, HEAD_DIM), lambda h: (0, h))
    fixed = pl.BlockSpec((length, 128), lambda h: (0, 0))
    return pl.pallas_call(
        whole_attend_back,
        grid=(width // HEAD_DIM,),
        in_specs=[head_block] * 5 + [fixed] * 3,
        out_specs=[head_block] * 3,
        out_shape=[jax.ShapeDtypeStruct((length, width), jnp.bfloat16)] * 3,
        scratch_shapes=[pltpu.VMEM((length, HEAD_DIM), jnp.float32)] * 2,
        compiler_params=pltpu.CompilerParams(vmem_limit_bytes=40 * 2**20),
        cost_estimate=pl.CostEstimate(
            flops=5 * length * length * width, bytes_accessed=16 * length * width, transcendentals=0
        ),
        name="attend_whole_back",
    )(queries, keys_in, values_in, mixed, d_mixed, log_total, cos_full, sin_full)


def rope_full(positions):
    cosine, sine = rope_table(positions)
    return jnp.concatenate([cosine, cosine], 1), jnp.concatenate([-sine, sine], 1)


def rotate_rows(values, cos_full, sin_full):
    rows, width = values.shape
    heads = values.reshape(rows, width // HEAD_DIM, HEAD_DIM)
    half = HEAD_DIM // 2
    turned = jnp.concatenate([heads[..., half:], heads[..., :half]], -1)
    return (heads * cos_full[:, None] + turned * sin_full[:, None]).reshape(rows, width)


def paired_on_device(
    latents, embeds, cotangent, counts, w_adapt, w_query, w_key, w_value, w_out, w_gate, w_up, w_down, gains
):
    block_len, seqs, width = latents.shape
    parts = lax.axis_size("grp") * lax.axis_size("ctx")
    length = block_len * parts
    core = grid_place()[3]
    owner = core == 0

    twice = counts == 2
    slot = jnp.where(
        twice,
        2 * (jnp.cumsum(twice.astype(jnp.int32)) - 1),
        2 * (jnp.cumsum((~twice).astype(jnp.int32)) - 1) + 1,
    )
    row_count = block_len * seqs
    target = (slot[None, :] * block_len + jnp.arange(block_len, dtype=jnp.int32)[:, None]).reshape(row_count)
    order = (lax.broadcasted_iota(jnp.int32, (row_count, row_count), 0) == target[None, :]).astype(jnp.bfloat16)

    def to_slots(values):
        return dot_n(order, values.reshape(row_count, width)).astype(jnp.bfloat16)

    def from_slots(values):
        return dot_w(order, values.reshape(row_count, width)).astype(jnp.bfloat16)

    def exchange(values):
        return lax.all_to_all(values, BOTH, split_axis=0, concat_axis=0, tiled=True)

    adapt_w = gather_all([w_adapt], 0)[0].reshape(-1, width)
    latent_slots, embed_slots = to_slots(latents), to_slots(embeds)
    upstream = to_slots(cotangent).reshape(parts, block_len, width)
    embed_part = dot_n(embed_slots, adapt_w[width:])
    adapted = (dot_n(latent_slots, adapt_w[:width]) + embed_part).reshape(parts, block_len, width)
    embed_part = embed_part.reshape(parts, block_len, width)
    pair_at = lax.broadcasted_iota(jnp.int32, (parts, 1, 1), 0) % 2
    starting = jnp.where(pair_at == 0, embed_part, adapted).astype(jnp.bfloat16)
    shared = adapted.reshape(parts // 2, 2, block_len, width)[:, 0].astype(jnp.bfloat16)
    gain_rows = jnp.pad(gains.reshape(1, -1), ((0, 15), (0, 0)))
    shared, *shards = lax.optimization_barrier(
        (shared, w_query, w_key, w_value, w_out, w_gate, w_up, w_down, gain_rows)
    )
    shared = lax.all_to_all(
        shared,
        BOTH,
        split_axis=0,
        concat_axis=0,
        tiled=True,
        axis_index_groups=[list(range(k, parts, 2)) for k in range(2)],
    )
    *matrices, gain_float = gather_all(shards, 1)
    query_w, key_w, value_w, output_w, gate_w, up_w, down_w = (
        matrix.reshape(-1, matrix.shape[-1]) for matrix in matrices
    )
    gain_float = gain_float.reshape((parts,) + gain_rows.shape)[:, 0].reshape((parts,) + gains.shape)
    gain_float = gain_float.transpose(1, 0, 2).reshape(gains.shape[0], width).astype(jnp.float32)
    gate_w, starting, upstream = lax.optimization_barrier((gate_w, starting, upstream))
    starting = exchange(starting).reshape(length, width).astype(jnp.float32)
    upstream = exchange(upstream).reshape(length, width)

    def before_attention(resid, cos_full, sin_full):
        normed = (resid * rms_scale(resid) * gain_float[0]).astype(jnp.bfloat16)
        queries = rotate_rows(dot_n(normed, query_w), cos_full, sin_full).astype(jnp.bfloat16)
        keys_in = rotate_rows(dot_n(normed, key_w), cos_full, sin_full).astype(jnp.bfloat16)
        values_in = dot_n(normed, value_w).astype(jnp.bfloat16)
        return normed, queries, keys_in, values_in

    def after_attention(resid, mixed):
        branch = dot_n(mixed, output_w)
        middle = resid + branch * rms_scale(branch) * gain_float[1]
        mlp_in = (middle * rms_scale(middle) * gain_float[2]).astype(jnp.bfloat16)
        gate_pre = dot_n(mlp_in, gate_w)
        up_pre = dot_n(mlp_in, up_w)
        hidden = (jax.nn.silu(gate_pre) * up_pre).astype(jnp.bfloat16)
        down_out = dot_n(hidden, down_w)
        result = middle + down_out * rms_scale(down_out) * gain_float[3]
        return result.astype(jnp.bfloat16), (branch, middle, mlp_in, gate_pre, up_pre, hidden, down_out)

    resid = shared.reshape(length // 2, width).astype(jnp.float32)
    local = jnp.arange(length // 2, dtype=jnp.int32)
    cos_half, sin_half = rope_full((local // block_len * 2 + core) * block_len + local % block_len)
    normed, queries, keys_in, values_in = before_attention(resid, cos_half, sin_half)
    far_keys, far_values = send(keys_in, 3), send(values_in, 3)
    mixed = attend_shared(core, block_len, queries, keys_in, values_in, far_keys, far_values)
    first_out, _ = after_attention(resid, mixed)
    far_out = send(first_out, 3, -1)
    first_out = jnp.stack(
        [first_out.reshape(-1, block_len, width), far_out.reshape(-1, block_len, width)], 1
    ).reshape(length, width)
    first_out = jnp.where(owner, first_out, jnp.zeros_like(first_out))

    cos_full, sin_full = rope_full(jnp.arange(length, dtype=jnp.int32))
    resid = starting + dot_n(first_out, adapt_w[:width])
    normed, queries, keys_in, values_in = before_attention(resid, cos_full, sin_full)
    mixed, log_total = attend_whole(queries, keys_in, values_in)
    result, saved = after_attention(resid, mixed)
    branch, middle, mlp_in, gate_pre, up_pre, hidden, down_out = saved
    final_back = exchange(result.reshape(parts, block_len, width))

    d_result = upstream.astype(jnp.float32)
    d_down, gain_four = norm_back(down_out, d_result, gain_float[3])
    d_down = d_down.astype(jnp.bfloat16)
    down_part = dot_w(hidden, d_down).astype(jnp.bfloat16)
    d_hidden = dot_t(d_down, down_w)
    sigma = jax.nn.sigmoid(gate_pre)
    d_gate = (d_hidden * up_pre * sigma * (1.0 + gate_pre * (1.0 - sigma))).astype(jnp.bfloat16)
    d_up = (d_hidden * gate_pre * sigma).astype(jnp.bfloat16)
    gate_part = dot_w(mlp_in, d_gate).astype(jnp.bfloat16)
    up_part = dot_w(mlp_in, d_up).astype(jnp.bfloat16)
    d_mlp = dot_t(d_gate, gate_w) + dot_t(d_up, up_w)
    d_middle, gain_three = norm_back(middle, d_mlp, gain_float[2])
    d_middle = d_middle + d_result
    d_branch, gain_two = norm_back(branch, d_middle, gain_float[1])
    d_branch = d_branch.astype(jnp.bfloat16)
    out_part = dot_w(mixed, d_branch).astype(jnp.bfloat16)
    d_mixed = dot_t(d_branch, output_w).astype(jnp.bfloat16)
    d_query, d_key, d_value = attend_whole_back(
        queries, keys_in, values_in, mixed, d_mixed, log_total, cos_full, sin_full
    )
    query_part = dot_w(normed, d_query).astype(jnp.bfloat16)
    key_part = dot_w(normed, d_key).astype(jnp.bfloat16)
    value_part = dot_w(normed, d_value).astype(jnp.bfloat16)
    d_normed = dot_t(d_query, query_w) + dot_t(d_key, key_w) + dot_t(d_value, value_w)
    d_resid, gain_one = norm_back(resid, d_normed, gain_float[0])
    d_resid = (d_resid + d_middle).astype(jnp.bfloat16)
    d_home = exchange(d_resid.reshape(parts, block_len, width))
    first_part = dot_w(first_out, d_resid)

    def blocks(part):
        return part.reshape(parts, -1, part.shape[-1])

    gain_part = jnp.stack([gain_one, gain_two, gain_three, gain_four])
    gain_part = gain_part.reshape(gains.shape[0], parts, gains.shape[1]).transpose(1, 0, 2)
    gain_part = jnp.pad(
        gain_part.reshape(parts, 1, gains.size).astype(jnp.bfloat16), ((0, 0), (0, 15), (0, 0))
    )
    sums = scatter_all(
        [
            blocks(part)
            for part in (query_part, key_part, value_part, out_part, gate_part, up_part, down_part)
        ]
        + [gain_part],
        2,
    )
    query_grad, key_grad, value_grad, out_grad, gate_grad, up_grad, down_grad, gain_grad = sums
    gain_grad = gain_grad[0].reshape(gains.shape)
    d_home, gate_grad = lax.optimization_barrier((d_home, gate_grad))

    d_home = from_slots(d_home)
    latent_back = dot_t(d_home, adapt_w[:width]).astype(jnp.bfloat16).reshape(latents.shape)
    embed_back = dot_t(d_home, adapt_w[width:]).astype(jnp.bfloat16).reshape(latents.shape)
    once = jnp.where(twice[None, :, None], jnp.zeros_like(latents), latents).reshape(row_count, width)
    latent_part = first_part + dot_w(once, d_home)
    embed_part = dot_w(embeds.reshape(row_count, width), d_home)
    final_back = from_slots(final_back).reshape(latents.shape)

    adapt_part = jnp.concatenate([latent_part, embed_part], 0).astype(jnp.bfloat16)
    (adapt_grad,) = scatter_all([blocks(adapt_part)], 3)
    return (
        final_back,
        latent_back,
        embed_back,
        adapt_grad,
        query_grad,
        key_grad,
        value_grad,
        out_grad,
        gate_grad,
        up_grad,
        down_grad,
        gain_grad,
    )


def on_device(latents, *others):
    ctx = lax.axis_size("ctx")
    parts = lax.axis_size("grp") * ctx
    if latents.shape[1] == parts and ctx == 4 and latents.shape[0] % 16 == 0:
        return paired_on_device(latents, *others)
    return spread_on_device(latents, *others)


def solution(mesh):
    placed = (
        P(("grp", "ctx"), None, None),
        P(("grp", "ctx"), None, None),
        P(("grp", "ctx"), None, None),
        P(),
        P(("grp", "ctx"), None),
        P(("grp", "ctx"), None),
        P(("grp", "ctx"), None),
        P(("grp", "ctx"), None),
        P(("grp", "ctx"), None),
        P(("grp", "ctx"), None),
        P(("grp", "ctx"), None),
        P(("grp", "ctx"), None),
        P(None, ("grp", "ctx")),
    )
    return jax.shard_map(
        on_device,
        mesh=mesh,
        in_specs=placed,
        out_specs=(
            P(("grp", "ctx"), None, None),
            P(("grp", "ctx"), None, None),
            P(("grp", "ctx"), None, None),
            P(("grp", "ctx"), None),
            P(("grp", "ctx"), None),
            P(("grp", "ctx"), None),
            P(("grp", "ctx"), None),
            P(("grp", "ctx"), None),
            P(("grp", "ctx"), None),
            P(("grp", "ctx"), None),
            P(("grp", "ctx"), None),
            P(None, ("grp", "ctx")),
        ),
        check_vma=False,
    )
```

```python
import functools

import jax
import jax.numpy as jnp
from jax import lax
from jax.experimental import pallas as pl
from jax.experimental.pallas import tpu as pltpu
from jax.sharding import PartitionSpec as P

HEADS = 8
HEAD_DIM = 128


def rms_scale(values):
    return lax.rsqrt(jnp.mean(values * values, -1, keepdims=True) + 1e-06)


def norm_back(values, upstream, gain_vec):
    scale_rows = rms_scale(values)
    normal = values * scale_rows
    gain_part = jnp.sum(upstream * normal, 0)
    scaled = upstream * gain_vec
    return (
        scale_rows * (scaled - normal * jnp.mean(scaled * normal, -1, keepdims=True)),
        gain_part,
    )


def rope_table(positions):
    freq = 10000.0 ** (-2.0 * jnp.arange(HEAD_DIM // 2, dtype=jnp.float32) / HEAD_DIM)
    angle = positions.astype(jnp.float32)[:, None] * freq
    return (jnp.cos(angle), jnp.sin(angle))


def rotate(values, cosine, sine):
    half_dim = HEAD_DIM // 2
    first_half = values[..., :half_dim]
    second_half = values[..., half_dim:]
    cos_b = cosine[:, None, None, :]
    sin_b = sine[:, None, None, :]
    return jnp.concatenate(
        [first_half * cos_b - second_half * sin_b, second_half * cos_b + first_half * sin_b], -1
    )


def unrotate(grads, cosine, sine):
    half_dim = HEAD_DIM // 2
    first_half = grads[..., :half_dim]
    second_half = grads[..., half_dim:]
    cos_b = cosine[:, None, None, :]
    sin_b = sine[:, None, None, :]
    return jnp.concatenate(
        [first_half * cos_b + second_half * sin_b, second_half * cos_b - first_half * sin_b], -1
    )


def score_block(queries, keys_in, query_pos, key_pos_in):
    raw = jnp.einsum(
        "qshd,kshd->qshk", queries, keys_in, preferred_element_type=jnp.float32
    ) * HEAD_DIM ** (-0.5)
    causal = key_pos_in[None, :] <= query_pos[:, None]
    return jnp.where(causal[:, None, None, :], raw, -1e30)


def back_block(queries, keys_in, values_in, d_mixed, log_total, delta, query_pos, key_pos_in):
    scores = score_block(queries, keys_in, query_pos, key_pos_in)
    probs = jnp.exp(scores - log_total[..., None])
    d_probs = jnp.einsum("qshd,kshd->qshk", d_mixed, values_in, preferred_element_type=jnp.float32)
    slopes = (probs * (d_probs - delta[..., None])).astype(jnp.bfloat16)
    return (probs.astype(jnp.bfloat16), slopes)


def spread_on_device(
    latents,
    embeds,
    cotangent,
    counts,
    w_adapt,
    w_query,
    w_key,
    w_value,
    w_out,
    w_gate,
    w_up,
    w_down,
    gains,
):
    groups = lax.axis_size("grp")
    ctx_count = lax.axis_size("ctx")
    seq_total = latents.shape[1]
    seq_group = seq_total // groups
    block_len = latents.shape[0]
    model_width = latents.shape[2]
    group_len = groups * block_len
    adapt_w, query_w, key_w, value_w, output_w, gate_w, up_w, down_w, gain_rows = (
        lax.all_gather(w_adapt, ("grp", "ctx"), axis=0, tiled=True),
        lax.all_gather(w_query, ("grp", "ctx"), axis=0, tiled=True),
        lax.all_gather(w_key, ("grp", "ctx"), axis=0, tiled=True),
        lax.all_gather(w_value, ("grp", "ctx"), axis=0, tiled=True),
        lax.all_gather(w_out, ("grp", "ctx"), axis=0, tiled=True),
        lax.all_gather(w_gate, ("grp", "ctx"), axis=0, tiled=True),
        lax.all_gather(w_up, ("grp", "ctx"), axis=0, tiled=True),
        lax.all_gather(w_down, ("grp", "ctx"), axis=0, tiled=True),
        lax.all_gather(gains, ("grp", "ctx"), axis=1, tiled=True),
    )
    gain_float = gain_rows.astype(jnp.float32)
    seq_order = jnp.arange(seq_total, dtype=jnp.int32)
    latent_in, embed_in, slope_in = (
        lax.all_to_all(
            jnp.take(latents, seq_order, axis=1), "grp", split_axis=1, concat_axis=0, tiled=True
        ),
        lax.all_to_all(
            jnp.take(embeds, seq_order, axis=1), "grp", split_axis=1, concat_axis=0, tiled=True
        ),
        lax.all_to_all(
            jnp.take(cotangent, seq_order, axis=1), "grp", split_axis=1, concat_axis=0, tiled=True
        ),
    )
    ctx_index = lax.axis_index("ctx")

    def key_position(flat_index):
        source = flat_index // group_len
        within = flat_index % group_len
        return (within // block_len * ctx_count + source) * block_len + within % block_len

    query_pos = key_position(ctx_index * group_len + jnp.arange(group_len, dtype=jnp.int32))
    cos_query, sin_query = rope_table(query_pos)

    def attend_forward(queries, keys_in, values_in):
        piece = lax.all_gather(keys_in, "ctx", axis=0, tiled=True)
        scores = score_block(
            queries, piece, query_pos, key_position(jnp.arange(piece.shape[0], dtype=jnp.int32))
        )
        log_total = jax.nn.logsumexp(scores, -1)
        probs = jnp.exp(scores - log_total[..., None]).astype(jnp.bfloat16)
        mixed_raw = jnp.einsum(
            "qshk,kshd->qshd",
            probs,
            lax.all_gather(values_in, "ctx", axis=0, tiled=True),
            preferred_element_type=jnp.float32,
        )
        return (mixed_raw.astype(jnp.bfloat16), (queries, keys_in, values_in, log_total, mixed_raw))

    def core_block(latent, embedding):
        seq_batch = latent.shape[1]
        row_count = group_len * seq_batch
        joined = jnp.concatenate([latent.astype(jnp.bfloat16), embedding], -1).reshape(
            row_count, 2 * model_width
        )
        resid = jnp.dot(joined, adapt_w, preferred_element_type=jnp.float32)
        normed = (resid * rms_scale(resid) * gain_float[0]).astype(jnp.bfloat16)

        def heads_of(matrix):
            return jnp.dot(normed, matrix, preferred_element_type=jnp.float32).reshape(
                group_len, seq_batch, HEADS, HEAD_DIM
            )

        queries = rotate(heads_of(query_w), cos_query, sin_query).astype(jnp.bfloat16)
        keys_in = rotate(heads_of(key_w), cos_query, sin_query).astype(jnp.bfloat16)
        values_in = heads_of(value_w).astype(jnp.bfloat16)
        mixed, kept = attend_forward(queries, keys_in, values_in)
        mixed_flat = mixed.reshape(row_count, model_width)
        branch = jnp.dot(mixed_flat, output_w, preferred_element_type=jnp.float32)
        middle = resid + branch * rms_scale(branch) * gain_float[1]
        mlp_in = (middle * rms_scale(middle) * gain_float[2]).astype(jnp.bfloat16)
        gate_pre = jnp.dot(mlp_in, gate_w, preferred_element_type=jnp.float32)
        up_pre = jnp.dot(mlp_in, up_w, preferred_element_type=jnp.float32)
        hidden = (jax.nn.silu(gate_pre) * up_pre).astype(jnp.bfloat16)
        down_out = jnp.dot(hidden, down_w, preferred_element_type=jnp.float32)
        result = middle + down_out * rms_scale(down_out) * gain_float[3]
        flat_saved = tuple(
            (
                stored.reshape(group_len, seq_batch, stored.shape[-1])
                for stored in (
                    joined,
                    resid,
                    normed,
                    mixed_flat,
                    branch,
                    middle,
                    mlp_in,
                    gate_pre,
                    up_pre,
                    hidden,
                    down_out,
                )
            )
        )
        return (result.reshape(group_len, seq_batch, model_width), (flat_saved, kept))

    group_counts = lax.dynamic_slice_in_dim(
        jnp.take(counts, seq_order), lax.axis_index("grp") * seq_group, seq_group
    )
    first_out, first_saved = core_block(latent_in, embed_in)
    last_in = jnp.where(group_counts[None, :, None] == 2, first_out, latent_in.astype(jnp.float32))
    final_out, saved = core_block(last_in, embed_in)
    upstream = slope_in.astype(jnp.float32)
    flat_saved, kept = saved
    (
        joined,
        resid,
        normed,
        mixed_flat,
        branch,
        middle,
        mlp_in,
        gate_pre,
        up_pre,
        hidden,
        down_out,
    ) = tuple((stored.reshape(-1, stored.shape[-1]) for stored in flat_saved))
    seq_batch = upstream.shape[1]
    d_result = upstream.reshape(-1, model_width)
    d_down, gain_four = norm_back(down_out, d_result, gain_float[3])
    d_down = d_down.astype(jnp.bfloat16)
    down_part = jnp.einsum("rf,rd->fd", hidden, d_down, preferred_element_type=jnp.float32)
    d_hidden = jnp.einsum("rd,fd->rf", d_down, down_w, preferred_element_type=jnp.float32)
    sigma = jax.nn.sigmoid(gate_pre)
    d_gate = (d_hidden * up_pre * sigma * (1.0 + gate_pre * (1.0 - sigma))).astype(jnp.bfloat16)
    d_up = (d_hidden * gate_pre * sigma).astype(jnp.bfloat16)
    gate_part = jnp.einsum("rd,rf->df", mlp_in, d_gate, preferred_element_type=jnp.float32)
    up_part = jnp.einsum("rd,rf->df", mlp_in, d_up, preferred_element_type=jnp.float32)
    d_mlp = jnp.einsum(
        "rf,df->rd", d_gate, gate_w, preferred_element_type=jnp.float32
    ) + jnp.einsum("rf,df->rd", d_up, up_w, preferred_element_type=jnp.float32)
    d_middle, gain_three = norm_back(middle, d_mlp, gain_float[2])
    d_middle = d_middle + d_result
    d_branch, gain_two = norm_back(branch, d_middle, gain_float[1])
    d_branch = d_branch.astype(jnp.bfloat16)
    out_part = jnp.einsum("re,rd->ed", mixed_flat, d_branch, preferred_element_type=jnp.float32)
    d_mixed = jnp.einsum(
        "rd,ed->re", d_branch, output_w, preferred_element_type=jnp.float32
    ).astype(jnp.bfloat16)
    attend_d_mixed = d_mixed.reshape(group_len, seq_batch, HEADS, HEAD_DIM)
    queries, keys_in, values_in, log_total, mixed_raw = kept
    delta = jnp.sum(attend_d_mixed.astype(jnp.float32) * mixed_raw, -1)
    key_part = lax.all_gather(keys_in, "ctx", axis=0, tiled=True)
    value_part = lax.all_gather(values_in, "ctx", axis=0, tiled=True)
    key_pos_in = key_position(jnp.arange(key_part.shape[0], dtype=jnp.int32))
    probs_low, slopes = back_block(
        queries, key_part, value_part, attend_d_mixed, log_total, delta, query_pos, key_pos_in
    )
    d_query = HEAD_DIM ** (-0.5) * jnp.einsum(
        "qshk,kshd->qshd", slopes, key_part, preferred_element_type=jnp.float32
    )
    pull_stacked = jnp.stack([probs_low, slopes])
    d_query, stacked = (d_query, pull_stacked)
    d_key = HEAD_DIM ** (-0.5) * jnp.einsum(
        "qshk,qshd->kshd", stacked[1], queries, preferred_element_type=jnp.float32
    )
    d_value = jnp.einsum(
        "qshk,qshd->kshd", stacked[0], attend_d_mixed, preferred_element_type=jnp.float32
    )
    paired = lax.psum_scatter(
        jnp.concatenate([d_key, d_value], -1).astype(jnp.bfloat16),
        "ctx",
        scatter_dimension=0,
        tiled=True,
    ).astype(jnp.float32)
    d_query, d_key, d_value = (
        unrotate(d_query, cos_query, sin_query).astype(jnp.bfloat16),
        unrotate(paired[..., :HEAD_DIM], cos_query, sin_query).astype(jnp.bfloat16),
        paired[..., HEAD_DIM:].astype(jnp.bfloat16),
    )
    d_query = d_query.reshape(-1, model_width)
    d_key = d_key.reshape(-1, model_width)
    d_value = d_value.reshape(-1, model_width)
    query_part = jnp.einsum("rd,re->de", normed, d_query, preferred_element_type=jnp.float32)
    key_part = jnp.einsum("rd,re->de", normed, d_key, preferred_element_type=jnp.float32)
    value_part = jnp.einsum("rd,re->de", normed, d_value, preferred_element_type=jnp.float32)
    d_normed = (
        jnp.einsum("re,de->rd", d_query, query_w, preferred_element_type=jnp.float32)
        + jnp.einsum("re,de->rd", d_key, key_w, preferred_element_type=jnp.float32)
        + jnp.einsum("re,de->rd", d_value, value_w, preferred_element_type=jnp.float32)
    )
    d_resid, gain_one = norm_back(resid, d_normed, gain_float[0])
    d_resid = (d_resid + d_middle).astype(jnp.bfloat16)
    adapt_part = jnp.einsum("rk,rd->kd", joined, d_resid, preferred_element_type=jnp.float32)
    d_joined = jnp.einsum("rd,kd->rk", d_resid, adapt_w, preferred_element_type=jnp.float32)
    gain_part = jnp.stack([gain_one, gain_two, gain_three, gain_four])
    d_joined, grads = (
        d_joined.reshape(group_len, seq_batch, 2 * model_width),
        (
            adapt_part,
            query_part,
            key_part,
            value_part,
            out_part,
            gate_part,
            up_part,
            down_part,
            gain_part,
        ),
    )
    final_back, latent_back, embed_back = (
        lax.all_to_all(
            final_out.astype(jnp.bfloat16), "grp", split_axis=0, concat_axis=1, tiled=True
        ),
        lax.all_to_all(
            d_joined[..., :model_width].astype(jnp.bfloat16),
            "grp",
            split_axis=0,
            concat_axis=1,
            tiled=True,
        ),
        lax.all_to_all(
            d_joined[..., model_width:].astype(jnp.bfloat16),
            "grp",
            split_axis=0,
            concat_axis=1,
            tiled=True,
        ),
    )
    seq_index = jnp.arange(seq_total, dtype=jnp.int32)
    inverse = jnp.sum(jnp.where(seq_order[:, None] == seq_index[None, :], seq_index[:, None], 0), 0)
    (
        adapt_part,
        query_part,
        key_part,
        value_part,
        out_part,
        gate_part,
        up_part,
        down_part,
        gain_part,
    ) = grads
    summed = (
        lax.psum_scatter(adapt_part, ("grp", "ctx"), scatter_dimension=0, tiled=True),
        lax.psum_scatter(query_part, ("grp", "ctx"), scatter_dimension=0, tiled=True),
        lax.psum_scatter(key_part, ("grp", "ctx"), scatter_dimension=0, tiled=True),
        lax.psum_scatter(value_part, ("grp", "ctx"), scatter_dimension=0, tiled=True),
        lax.psum_scatter(out_part, ("grp", "ctx"), scatter_dimension=0, tiled=True),
        lax.psum_scatter(gate_part, ("grp", "ctx"), scatter_dimension=0, tiled=True),
        lax.psum_scatter(up_part, ("grp", "ctx"), scatter_dimension=0, tiled=True),
        lax.psum_scatter(down_part, ("grp", "ctx"), scatter_dimension=0, tiled=True),
        lax.psum_scatter(gain_part, ("grp", "ctx"), scatter_dimension=1, tiled=True),
    )
    return (
        jnp.take(final_back, inverse, axis=1),
        jnp.take(latent_back, inverse, axis=1),
        jnp.take(embed_back, inverse, axis=1),
        summed[0],
        summed[1],
        summed[2],
        summed[3],
        summed[4],
        summed[5],
        summed[6],
        summed[7],
        summed[8],
    )


BOTH = ("grp", "ctx")
LOG2E = 1.4426950408889634
SCALE = HEAD_DIM ** (-0.5)
TILE = 256
NEG = -1e30


def grid_sizes():
    ctx = lax.axis_size("ctx")
    x_size = ctx // 2
    return lax.axis_size("grp") // x_size, x_size, x_size, 2


def grid_place():
    z_size, y_size, x_size, k_size = grid_sizes()
    g, c = lax.axis_index("grp"), lax.axis_index("ctx")
    return g // y_size, g % y_size, c // k_size, c % k_size


def send(values, axis, shift=None, keep=None):
    sizes = grid_sizes()
    pairs = []
    for flat in range(sizes[0] * sizes[1] * sizes[2] * sizes[3]):
        rest, spot = flat, [0, 0, 0, 0]
        for at in (3, 2, 1, 0):
            spot[at] = rest % sizes[at]
            rest //= sizes[at]
        own = spot[axis]
        other = 1 - own if shift is None else own + shift
        if 0 <= other < sizes[axis] and (keep is None or keep(own)):
            spot[axis] = other
            target = ((spot[0] * sizes[1] + spot[1]) * sizes[2] + spot[2]) * sizes[3] + spot[3]
            pairs.append((flat, target))
    return lax.ppermute(values, BOTH, pairs)


MESH = pl.DeviceIdType.MESH


def device_at(z, y, x, k):
    _, y_size, _, k_size = grid_sizes()
    return (z * y_size + y, x * k_size + k)


def order_of(y, x, turn):
    first = (y + turn * (1 - 2 * y), x + (1 - turn) * (1 - 2 * x))
    second = (y + (1 - turn) * (1 - 2 * y), x + turn * (1 - 2 * x))
    return first, second


def greet_line(z, y, x, k, z_size):
    barrier = pltpu.get_barrier_semaphore()
    for device in (device_at(z, 1 - y, x, k), device_at(z, y, 1 - x, k), device_at(z, y, x, 1 - k)):
        pl.semaphore_signal(barrier, inc=1, device_id=device, device_id_type=MESH)

    @pl.when(z > 0)
    def _():
        pl.semaphore_signal(barrier, inc=1, device_id=device_at(z - 1, y, x, k), device_id_type=MESH)

    @pl.when(z < z_size - 1)
    def _():
        pl.semaphore_signal(barrier, inc=1, device_id=device_at(z + 1, y, x, k), device_id_type=MESH)

    pl.semaphore_wait(barrier, 3 + jnp.minimum(z, 1) + jnp.minimum(z_size - 1 - z, 1))


def remote(source, target, send_sem, recv_sem, device):
    return pltpu.make_async_remote_copy(
        src_ref=source,
        dst_ref=target,
        send_sem=send_sem,
        recv_sem=recv_sem,
        device_id=device,
        device_id_type=MESH,
    )


def row_views(shapes):
    views = []
    for at, (rows, width) in enumerate(shapes):
        if rows % 32 == 0 and rows * width >= 2**16:
            views += [(at, 0, rows // 2, 0), (at, rows // 2, rows // 2, 1)]
        else:
            views.append((at, 0, rows, at % 2))
    return views


def at_offsets(z, z_size, step, body):
    if step == 0:
        body(z, True, True)
        return

    @pl.when(z >= step)
    def _():
        body(z - step, True, False)

    @pl.when(z + step < z_size)
    def _():
        body(z + step, False, True)


def gather_kernel(views, count, *refs):
    z_size, _, _, _ = grid_sizes()
    z, y, x, k = grid_place()
    shards, outs = refs[:count], refs[count : 2 * count]
    local_sem, z_send, z_recv, p_send, p_recv, k_send, k_recv = refs[2 * count :]
    greet_line(z, y, x, k, z_size)
    everyone = range(len(views))

    def spot(g, slot_z, at_y, at_x):
        at, first_row, rows, _ = views[g]
        return outs[at].at[slot_z, at_y, at_x, k, pl.ds(first_row, rows)]

    def z_copy(g, slot_z, way):
        block = spot(g, slot_z, y, x)
        side = z + 1 - 2 * way
        return remote(block, block, z_send.at[g, slot_z, way], z_recv.at[g, slot_z], device_at(side, y, x, k))

    def plane_copy(g, slot_z, kind):
        first, second = order_of(y, x, (views[g][3] + slot_z) % 2)
        from_at = first if kind == 2 else (y, x)
        to_at = first if kind == 0 else second
        block = spot(g, slot_z, from_at[0], from_at[1])
        device = device_at(z, to_at[0], to_at[1], k)
        return remote(block, block, p_send.at[g, slot_z, kind], p_recv.at[g, slot_z, kind], device)

    def core_copy(at, slot_z):
        block = outs[at].at[slot_z, :, :, k]
        return remote(block, block, k_send.at[at, slot_z], k_recv.at[at, slot_z], device_at(z, y, x, 1 - k))

    def each_way(g, slot_z, up, down, act):
        if up:

            @pl.when(z < z_size - 1)
            def _():
                act(z_copy(g, slot_z, 0))

        if down:

            @pl.when(z > 0)
            def _():
                act(z_copy(g, slot_z, 1))

    own = [pltpu.make_async_copy(shards[at], outs[at].at[z, y, x, k], local_sem.at[at]) for at in range(count)]
    for copy in own:
        copy.start()
    for copy in own:
        copy.wait()

    def arrive(slot_z, up, down):
        for g in everyone:
            if not (up and down):
                z_copy(g, slot_z, 1 if up else 0).wait_recv()
            each_way(g, slot_z, up, down, lambda copy: copy.start())
            plane_copy(g, slot_z, 0).start()
            plane_copy(g, slot_z, 1).start()

    def pass_on(slot_z, up, down):
        for g in everyone:
            plane_copy(g, slot_z, 0).wait_recv()
            plane_copy(g, slot_z, 2).start()

    def cross(slot_z, up, down):
        for g in everyone:
            plane_copy(g, slot_z, 1).wait_recv()
            plane_copy(g, slot_z, 2).wait_recv()
        for at in range(count):
            core_copy(at, slot_z).start()

    def settle(slot_z, up, down):
        for g in everyone:
            each_way(g, slot_z, up, down, lambda copy: copy.wait_send())
            for kind in range(3):
                plane_copy(g, slot_z, kind).wait_send()

    for step in range(z_size + 1):
        if step < z_size:
            at_offsets(z, z_size, step, arrive)
            at_offsets(z, z_size, step, pass_on)
        if step > 0:
            at_offsets(z, z_size, step - 1, cross)
    for step in range(z_size):
        at_offsets(z, z_size, step, settle)
    for slot_z in range(z_size):
        for at in range(count):
            core_copy(at, slot_z).wait()


def gather_all(shards, collective_id):
    sizes = grid_sizes()
    count, z_size = len(shards), sizes[0]
    views = row_views([shard.shape for shard in shards])
    series = len(views)
    anywhere = pl.BlockSpec(memory_space=pl.ANY)
    dma = pltpu.SemaphoreType.DMA
    return pl.pallas_call(
        functools.partial(gather_kernel, views, count),
        in_specs=[anywhere] * count,
        out_specs=[anywhere] * count,
        out_shape=[jax.ShapeDtypeStruct(sizes + shard.shape, shard.dtype) for shard in shards],
        scratch_shapes=[
            dma((count,)),
            dma((series, z_size, 2)),
            dma((series, z_size)),
            dma((series, z_size, 3)),
            dma((series, z_size, 3)),
            dma((count, z_size)),
            dma((count, z_size)),
        ],
        compiler_params=pltpu.CompilerParams(collective_id=collective_id, has_side_effects=True),
        name="gather_weights",
    )(*shards)


def scatter_kernel(views, count, *refs):
    z_size, _, _, _ = grid_sizes()
    z, y, x, k = grid_place()
    parts, outs = refs[:count], refs[count : 2 * count]
    held, from_core = refs[2 * count : 3 * count], refs[3 * count : 4 * count]
    from_second, from_first = refs[4 * count : 5 * count], refs[5 * count : 6 * count]
    from_z = refs[6 * count : 7 * count]
    local_sem, k_send, k_recv, p_send, p_recv, z_send, z_recv = refs[7 * count :]
    greet_line(z, y, x, k, z_size)
    everyone = range(len(views))

    def rows_of(g):
        return pl.ds(views[g][1], views[g][2])

    def core_copy(at, slot_z):
        return remote(
            parts[at].at[slot_z, :, :, 1 - k],
            from_core[at].at[slot_z],
            k_send.at[at, slot_z],
            k_recv.at[at, slot_z],
            device_at(z, y, x, 1 - k),
        )

    def own_copy(at, slot_z):
        return pltpu.make_async_copy(parts[at].at[slot_z, :, :, k], held[at].at[slot_z], local_sem.at[at, slot_z])

    def turns(g, slot_z):
        return order_of(y, x, (views[g][3] + slot_z) % 2)

    def second_copy(g, slot_z, kind):
        at, (_, second) = views[g][0], turns(g, slot_z)
        block = second if kind == 0 else (1 - y, 1 - x)
        return remote(
            held[at].at[slot_z, block[0], block[1], rows_of(g)],
            from_second[at].at[slot_z, kind, rows_of(g)],
            p_send.at[g, slot_z, kind],
            p_recv.at[g, slot_z, kind],
            device_at(z, second[0], second[1], k),
        )

    def first_copy(g, slot_z):
        at, (first, _) = views[g][0], turns(g, slot_z)
        return remote(
            held[at].at[slot_z, first[0], first[1], rows_of(g)],
            from_first[at].at[slot_z, rows_of(g)],
            p_send.at[g, slot_z, 2],
            p_recv.at[g, slot_z, 2],
            device_at(z, first[0], first[1], k),
        )

    def z_copy(at, slot_z, way, here=None):
        side = z + 1 - 2 * way if here is None else here
        return remote(
            held[at].at[slot_z, y, x],
            from_z[at].at[slot_z, way],
            z_send.at[at, slot_z, way],
            z_recv.at[at, slot_z, way],
            device_at(side, y, x, k),
        )

    def add(ref, at, other, other_at):
        ref[at] = ref[at] + other[other_at]

    def begin(slot_z, below, above):
        for at in range(count):
            core_copy(at, slot_z).start()
            own_copy(at, slot_z).start()

    def fold_core(slot_z, below, above):
        for at in range(count):
            own_copy(at, slot_z).wait()
            core_copy(at, slot_z).wait_recv()
        for g in everyone:
            at, rows = views[g][0], rows_of(g)
            first, second = turns(g, slot_z)
            for spot in (second, (1 - y, 1 - x)):
                add(held[at], (slot_z, spot[0], spot[1], rows), from_core[at], (slot_z, spot[0], spot[1], rows))
            second_copy(g, slot_z, 0).start()
            second_copy(g, slot_z, 1).start()
            for spot in (first, (y, x)):
                add(held[at], (slot_z, spot[0], spot[1], rows), from_core[at], (slot_z, spot[0], spot[1], rows))

    def fold_second(slot_z, below, above):
        for g in everyone:
            at, rows = views[g][0], rows_of(g)
            first, _ = turns(g, slot_z)
            second_copy(g, slot_z, 1).wait_recv()
            add(held[at], (slot_z, first[0], first[1], rows), from_second[at], (slot_z, 1, rows))
            first_copy(g, slot_z).start()

    def fold_first(slot_z, below, above):
        for g in everyone:
            at, rows = views[g][0], rows_of(g)
            second_copy(g, slot_z, 0).wait_recv()
            add(held[at], (slot_z, y, x, rows), from_second[at], (slot_z, 0, rows))
            first_copy(g, slot_z).wait_recv()
            add(held[at], (slot_z, y, x, rows), from_first[at], (slot_z, rows))
        if below and above:
            for at in range(count):
                outs[at][...] = held[at][slot_z, y, x].astype(jnp.float32)
        for way, use in ((0, above), (1, below)):
            if not use:
                continue
            came, source = (z > 0, z - 1) if way == 0 else (z < z_size - 1, z + 1)

            @pl.when(came)
            def _(way=way, source=source):
                for at in range(count):
                    z_copy(at, slot_z, way, source).wait_recv()
                    if below and above:
                        outs[at][...] += from_z[at][slot_z, way].astype(jnp.float32)
                    else:
                        add(held[at], (slot_z, y, x), from_z[at], (slot_z, way))

            if not (below and above):
                for at in range(count):
                    z_copy(at, slot_z, way).start()

    def settle(slot_z, below, above):
        for at in range(count):
            core_copy(at, slot_z).wait_send()
            if not (below and above):
                z_copy(at, slot_z, 0 if above else 1).wait_send()
        for g in everyone:
            second_copy(g, slot_z, 0).wait_send()
            second_copy(g, slot_z, 1).wait_send()
            first_copy(g, slot_z).wait_send()

    far = z_size - 1
    for step in range(far, -1, -1):
        at_offsets(z, z_size, step, begin)
    for step in range(far, -3, -1):
        if step >= 0:
            at_offsets(z, z_size, step, fold_core)
        if 0 <= step + 1 <= far:
            at_offsets(z, z_size, step + 1, fold_second)
        if 0 <= step + 2 <= far:
            at_offsets(z, z_size, step + 2, fold_first)
    for step in range(z_size):
        at_offsets(z, z_size, step, settle)


def scatter_all(parts, collective_id):
    sizes = grid_sizes()
    count, (z_size, y_size, x_size, _) = len(parts), sizes
    shapes = [part.shape[1:] for part in parts]
    views = row_views(shapes)
    series = len(views)
    dma = pltpu.SemaphoreType.DMA
    plane = (z_size, y_size, x_size)

    def buffers(lead):
        return [pltpu.VMEM(lead + shape, jnp.bfloat16) for shape in shapes]

    return pl.pallas_call(
        functools.partial(scatter_kernel, views, count),
        in_specs=[pl.BlockSpec(memory_space=pl.ANY)] * count,
        out_specs=[pl.BlockSpec(memory_space=pltpu.VMEM)] * count,
        out_shape=[jax.ShapeDtypeStruct(shape, jnp.float32) for shape in shapes],
        scratch_shapes=buffers(plane)
        + buffers(plane)
        + buffers((z_size, 2))
        + buffers((z_size,))
        + buffers((z_size, 2))
        + [
            dma((count, z_size)),
            dma((count, z_size)),
            dma((count, z_size)),
            dma((series, z_size, 3)),
            dma((series, z_size, 3)),
            dma((count, z_size, 2)),
            dma((count, z_size, 2)),
        ],
        compiler_params=pltpu.CompilerParams(
            collective_id=collective_id, has_side_effects=True, vmem_limit_bytes=56 * 2**20
        ),
        name="scatter_sums",
    )(*(part.reshape(sizes + part.shape[1:]) for part in parts))


def dot_t(left, right):
    return lax.dot_general(left, right, (((1,), (1,)), ((), ())), preferred_element_type=jnp.float32)


def dot_n(left, right):
    return jnp.dot(left, right, preferred_element_type=jnp.float32)


def dot_w(left, right):
    return lax.dot_general(left, right, (((0,), (0,)), ((), ())), preferred_element_type=jnp.float32)


def below(rows, columns):
    at_row = lax.broadcasted_iota(jnp.int32, (rows, columns), 0)
    at_column = lax.broadcasted_iota(jnp.int32, (rows, columns), 1)
    return at_column <= at_row


def whole_attend(q_ref, k_ref, v_ref, o_ref, log_ref):
    head = pl.program_id(0)
    length = q_ref.shape[0]
    lane = lax.broadcasted_iota(jnp.int32, (TILE, 128), 1)
    for at in range(length // TILE):
        rows = pl.ds(at * TILE, TILE)
        seen = (at + 1) * TILE
        raw = dot_t(q_ref[rows, :], k_ref[:seen, :]) * (SCALE * LOG2E)
        last = jnp.where(below(TILE, TILE), raw[:, at * TILE :], NEG)
        raw = jnp.concatenate([raw[:, : at * TILE], last], 1) if at else last
        top = jnp.max(raw, 1, keepdims=True)
        weight = jnp.exp2(raw - top)
        total = jnp.sum(weight, 1, keepdims=True)
        mixed = dot_n(weight.astype(jnp.bfloat16), v_ref[:seen, :])
        o_ref[rows, :] = (mixed / total).astype(o_ref.dtype)
        log_total = top + jnp.log2(total)
        log_ref[rows, :] = jnp.where(lane == head, log_total, log_ref[rows, :])


def attend_whole(queries, keys_in, values_in):
    length, width = queries.shape
    head_block = pl.BlockSpec((length, HEAD_DIM), lambda h: (0, h))
    return pl.pallas_call(
        whole_attend,
        grid=(width // HEAD_DIM,),
        in_specs=[head_block] * 3,
        out_specs=[head_block, pl.BlockSpec((length, 128), lambda h: (0, 0))],
        out_shape=[
            jax.ShapeDtypeStruct((length, width), jnp.bfloat16),
            jax.ShapeDtypeStruct((length, 128), jnp.float32),
        ],
        compiler_params=pltpu.CompilerParams(vmem_limit_bytes=32 * 2**20),
        cost_estimate=pl.CostEstimate(
            flops=2 * length * length * width, bytes_accessed=8 * length * width, transcendentals=0
        ),
        name="attend_whole",
    )(queries, keys_in, values_in)


def shared_attend(block_len, core_ref, q_ref, k_ref, v_ref, ok_ref, ov_ref, o_ref):
    core = core_ref[0]
    length = q_ref.shape[0]
    for at in range(length // TILE):
        rows = pl.ds(at * TILE, TILE)
        seen = (at + 1) * TILE
        queries = q_ref[rows, :]
        raw = dot_t(queries, k_ref[:seen, :]) * (SCALE * LOG2E)
        far = dot_t(queries, ok_ref[:seen, :]) * (SCALE * LOG2E)
        at_row = lax.broadcasted_iota(jnp.int32, (TILE, TILE), 0)
        at_column = lax.broadcasted_iota(jnp.int32, (TILE, TILE), 1)
        near_last = jnp.where(at_column <= at_row, raw[:, at * TILE :], NEG)
        far_ok = at_column // block_len < at_row // block_len + core
        far_last = jnp.where(far_ok, far[:, at * TILE :], NEG)
        raw = jnp.concatenate([raw[:, : at * TILE], near_last], 1) if at else near_last
        far = jnp.concatenate([far[:, : at * TILE], far_last], 1) if at else far_last
        top = jnp.maximum(jnp.max(raw, 1, keepdims=True), jnp.max(far, 1, keepdims=True))
        weight = jnp.exp2(raw - top)
        far_weight = jnp.exp2(far - top)
        total = jnp.sum(weight, 1, keepdims=True) + jnp.sum(far_weight, 1, keepdims=True)
        mixed = dot_n(weight.astype(jnp.bfloat16), v_ref[:seen, :])
        mixed = mixed + dot_n(far_weight.astype(jnp.bfloat16), ov_ref[:seen, :])
        o_ref[rows, :] = (mixed / total).astype(o_ref.dtype)


def attend_shared(core, block_len, queries, keys_in, values_in, far_keys, far_values):
    length, width = queries.shape
    head_block = pl.BlockSpec((length, HEAD_DIM), lambda h: (0, h))
    return pl.pallas_call(
        functools.partial(shared_attend, block_len),
        grid=(width // HEAD_DIM,),
        in_specs=[pl.BlockSpec(memory_space=pltpu.SMEM)] + [head_block] * 5,
        out_specs=head_block,
        out_shape=jax.ShapeDtypeStruct((length, width), jnp.bfloat16),
        compiler_params=pltpu.CompilerParams(vmem_limit_bytes=32 * 2**20),
        cost_estimate=pl.CostEstimate(
            flops=4 * length * length * width, bytes_accessed=12 * length * width, transcendentals=0
        ),
        name="attend_shared",
    )(core.reshape(1), queries, keys_in, values_in, far_keys, far_values)


def whole_attend_back(
    q_ref, k_ref, v_ref, o_ref, do_ref, log_ref, cos_ref, sin_ref, dq_ref, dk_ref, dv_ref, dk_sum, dv_sum
):
    head = pl.program_id(0)
    length = q_ref.shape[0]
    lane = lax.broadcasted_iota(jnp.int32, (TILE, 128), 1)

    def unrotated(grads, rows):
        turned = pltpu.roll(grads, HEAD_DIM // 2, 1)
        return grads * cos_ref[rows, :] - turned * sin_ref[rows, :]

    for at in range(length // TILE):
        rows = pl.ds(at * TILE, TILE)
        seen = (at + 1) * TILE
        queries, d_mixed = q_ref[rows, :], do_ref[rows, :]
        log_total = jnp.sum(jnp.where(lane == head, log_ref[rows, :], 0.0), 1, keepdims=True)
        delta = jnp.sum(d_mixed.astype(jnp.float32) * o_ref[rows, :].astype(jnp.float32), 1, keepdims=True)
        raw = dot_t(queries, k_ref[:seen, :]) * (SCALE * LOG2E)
        last = jnp.where(below(TILE, TILE), raw[:, at * TILE :], NEG)
        raw = jnp.concatenate([raw[:, : at * TILE], last], 1) if at else last
        probs = jnp.exp2(raw - log_total)
        d_probs = dot_t(d_mixed, v_ref[:seen, :])
        slopes = (probs * (d_probs - delta)).astype(jnp.bfloat16)
        d_query = dot_n(slopes, k_ref[:seen, :]) * SCALE
        dq_ref[rows, :] = unrotated(d_query, rows).astype(dq_ref.dtype)
        d_value = dot_w(probs.astype(jnp.bfloat16), d_mixed)
        d_key = dot_w(slopes, queries)
        if at:
            before = pl.ds(0, at * TILE)
            dv_sum[before, :] += d_value[: at * TILE]
            dk_sum[before, :] += d_key[: at * TILE]
        dv_sum[rows, :] = d_value[at * TILE :]
        dk_sum[rows, :] = d_key[at * TILE :]
    everything = pl.ds(0, length)
    dk_ref[...] = unrotated(dk_sum[...] * SCALE, everything).astype(dk_ref.dtype)
    dv_ref[...] = dv_sum[...].astype(dv_ref.dtype)


def attend_whole_back(queries, keys_in, values_in, mixed, d_mixed, log_total, cos_full, sin_full):
    length, width = queries.shape
    head_block = pl.BlockSpec((length, HEAD_DIM), lambda h: (0, h))
    fixed = pl.BlockSpec((length, 128), lambda h: (0, 0))
    return pl.pallas_call(
        whole_attend_back,
        grid=(width // HEAD_DIM,),
        in_specs=[head_block] * 5 + [fixed] * 3,
        out_specs=[head_block] * 3,
        out_shape=[jax.ShapeDtypeStruct((length, width), jnp.bfloat16)] * 3,
        scratch_shapes=[pltpu.VMEM((length, HEAD_DIM), jnp.float32)] * 2,
        compiler_params=pltpu.CompilerParams(vmem_limit_bytes=40 * 2**20),
        cost_estimate=pl.CostEstimate(
            flops=5 * length * length * width, bytes_accessed=16 * length * width, transcendentals=0
        ),
        name="attend_whole_back",
    )(queries, keys_in, values_in, mixed, d_mixed, log_total, cos_full, sin_full)


def rope_full(positions):
    cosine, sine = rope_table(positions)
    return jnp.concatenate([cosine, cosine], 1), jnp.concatenate([-sine, sine], 1)


def whole_block(array):
    return pl.BlockSpec(array.shape, lambda *_: (0,) * array.ndim, pipeline_mode=pl.Buffered(1))


def row_block(rows, width):
    return pl.BlockSpec((rows, width), lambda i: (i, 0))


def compute_params(megabytes=58):
    return pltpu.CompilerParams(vmem_limit_bytes=megabytes * 2**20)


def cost(flops, nbytes):
    return pl.CostEstimate(flops=int(flops), bytes_accessed=int(nbytes), transcendentals=0)


def unit_rows(values):
    scale_rows = rms_scale(values)
    return scale_rows, values * scale_rows


def pull_norm(values, upstream, gain_row):
    scale_rows, normal = unit_rows(values)
    gain_part = jnp.sum(upstream * normal, 0, keepdims=True)
    scaled = upstream * gain_row
    return scale_rows * (scaled - normal * jnp.mean(scaled * normal, -1, keepdims=True)), gain_part


def home_kernel(block_len, target_ref, s_ref, e_ref, c_ref, w_ref, start_ref, shared_ref, up_ref):
    rows, width = start_ref.shape
    count = s_ref.shape[0]
    at_row = lax.broadcasted_iota(jnp.int32, (rows, count), 0) + pl.program_id(0) * rows
    order = (at_row == target_ref[...]).astype(jnp.bfloat16)
    up_ref[...] = dot_n(order, c_ref[...]).astype(jnp.bfloat16)
    latent = dot_n(order, s_ref[...]).astype(jnp.bfloat16)
    embed = dot_n(order, e_ref[...]).astype(jnp.bfloat16)
    embed_part = dot_n(embed, w_ref[width:, :])
    adapted = dot_n(jnp.concatenate([latent, embed], 1), w_ref[...])
    shared_ref[...] = adapted.astype(jnp.bfloat16)
    pair_at = lax.broadcasted_iota(jnp.int32, (rows, 1), 0) // block_len % 2
    start_ref[...] = jnp.where(pair_at == 0, embed_part, adapted).astype(jnp.bfloat16)


def adapt_at_home(target, latents, embeds, cotangent, adapt_w, block_len):
    count, width = latents.shape
    like = jax.ShapeDtypeStruct((count, width), jnp.bfloat16)
    return pl.pallas_call(
        functools.partial(home_kernel, block_len),
        grid=(count // TILE,),
        in_specs=[whole_block(a) for a in (target, latents, embeds, cotangent, adapt_w)],
        out_specs=[
            row_block(TILE, width),
            row_block(TILE, width),
            row_block(TILE, width),
        ],
        out_shape=[like, like, like],
        compiler_params=compute_params(),
        cost_estimate=cost(10 * count * width * width, 14 * count * width),
        name="adapt_at_home",
    )(target, latents, embeds, cotangent, adapt_w)


def turned_heads(values, cos, sin):
    parts = []
    for head in range(values.shape[1] // HEAD_DIM):
        one = values[:, head * HEAD_DIM : (head + 1) * HEAD_DIM]
        parts.append(one * cos + pltpu.roll(one, HEAD_DIM // 2, 1) * sin)
    return jnp.concatenate(parts, 1)


def project_heads(resid, gain_ref, wq_ref, wk_ref, wv_ref, cos_ref, sin_ref, q_ref, k_ref, v_ref):
    normed = (unit_rows(resid)[1] * gain_ref[0:1, :]).astype(jnp.bfloat16)
    cos, sin = cos_ref[...], sin_ref[...]
    q_ref[...] = turned_heads(dot_n(normed, wq_ref[...]), cos, sin).astype(jnp.bfloat16)
    k_ref[...] = turned_heads(dot_n(normed, wk_ref[...]), cos, sin).astype(jnp.bfloat16)
    v_ref[...] = dot_n(normed, wv_ref[...]).astype(jnp.bfloat16)
    return normed


def first_heads_kernel(r_ref, gain_ref, wq_ref, wk_ref, wv_ref, cos_ref, sin_ref, q_ref, k_ref, v_ref):
    resid = r_ref[...].astype(jnp.float32)
    project_heads(resid, gain_ref, wq_ref, wk_ref, wv_ref, cos_ref, sin_ref, q_ref, k_ref, v_ref)


def first_heads(resid, gain_float, query_w, key_w, value_w, cos, sin):
    rows, width = resid.shape
    tile = min(TILE, rows)
    fixed = (gain_float, query_w, key_w, value_w)
    return pl.pallas_call(
        first_heads_kernel,
        grid=(rows // tile,),
        in_specs=[row_block(tile, width)] + [whole_block(a) for a in fixed] + [row_block(tile, HEAD_DIM)] * 2,
        out_specs=[row_block(tile, width)] * 3,
        out_shape=[jax.ShapeDtypeStruct((rows, width), jnp.bfloat16)] * 3,
        compiler_params=compute_params(),
        cost_estimate=cost(6 * rows * width * width, 8 * rows * width + 6 * width * width),
        name="first_heads",
    )(resid, *fixed, cos, sin)


def last_heads_kernel(
    start_ref, first_ref, wa_ref, gain_ref, wq_ref, wk_ref, wv_ref, cos_ref, sin_ref, r_ref, n_ref, q_ref, k_ref, v_ref
):
    resid = start_ref[...].astype(jnp.float32) + dot_n(first_ref[...], wa_ref[...])
    r_ref[...] = resid
    n_ref[...] = project_heads(resid, gain_ref, wq_ref, wk_ref, wv_ref, cos_ref, sin_ref, q_ref, k_ref, v_ref)


def last_heads(starting, first_out, adapt_w, gain_float, query_w, key_w, value_w, cos, sin):
    rows, width = starting.shape
    upper = pl.BlockSpec((width, width), lambda i: (0, 0), pipeline_mode=pl.Buffered(1))
    fixed = (gain_float, query_w, key_w, value_w)
    like = jax.ShapeDtypeStruct((rows, width), jnp.bfloat16)
    return pl.pallas_call(
        last_heads_kernel,
        grid=(rows // TILE,),
        in_specs=[row_block(TILE, width)] * 2
        + [upper]
        + [whole_block(a) for a in fixed]
        + [row_block(TILE, HEAD_DIM)] * 2,
        out_specs=[row_block(TILE, width)] * 5,
        out_shape=[jax.ShapeDtypeStruct((rows, width), jnp.float32)] + [like] * 4,
        compiler_params=compute_params(),
        cost_estimate=cost(8 * rows * width * width, 16 * rows * width + 8 * width * width),
        name="last_heads",
    )(starting, first_out, adapt_w, *fixed, cos, sin)


def column_chunks(total, chunk=768):
    return [(at, min(chunk, total - at)) for at in range(0, total, chunk)]


def forward_rows(resid, mixed, gain_ref, wo_ref, wg_ref, wu_ref, wd_ref, keep):
    branch = dot_n(mixed, wo_ref[...])
    middle = resid + unit_rows(branch)[1] * gain_ref[1:2, :]
    mlp_in = (unit_rows(middle)[1] * gain_ref[2:3, :]).astype(jnp.bfloat16)
    down_out = None
    for at, size in column_chunks(wg_ref.shape[1]):
        columns = slice(at, at + size)
        gate_pre = dot_n(mlp_in, wg_ref[:, columns])
        up_pre = dot_n(mlp_in, wu_ref[:, columns])
        sigma = 1.0 / (1.0 + jnp.exp(-gate_pre))
        hidden = (gate_pre * sigma * up_pre).astype(jnp.bfloat16)
        keep(columns, gate_pre, up_pre, hidden)
        part = dot_n(hidden, wd_ref[columns, :])
        down_out = part if down_out is None else down_out + part
    return branch, middle, mlp_in, down_out


def first_rows_kernel(r_ref, mixed_ref, gain_ref, wo_ref, wg_ref, wu_ref, wd_ref, out_ref):
    resid = r_ref[...].astype(jnp.float32)
    _, middle, _, down_out = forward_rows(
        resid, mixed_ref[...], gain_ref, wo_ref, wg_ref, wu_ref, wd_ref, lambda *_: None
    )
    out_ref[...] = (middle + unit_rows(down_out)[1] * gain_ref[3:4, :]).astype(jnp.bfloat16)


def first_rows(resid, mixed, gain_float, output_w, gate_w, up_w, down_w):
    rows, width = resid.shape
    tile = min(TILE, rows)
    fixed = (gain_float, output_w, gate_w, up_w, down_w)
    weights = output_w.size + gate_w.size + up_w.size + down_w.size
    return pl.pallas_call(
        first_rows_kernel,
        grid=(rows // tile,),
        in_specs=[row_block(tile, width)] * 2 + [whole_block(a) for a in fixed],
        out_specs=row_block(tile, width),
        out_shape=jax.ShapeDtypeStruct((rows, width), jnp.bfloat16),
        compiler_params=compute_params(),
        cost_estimate=cost(2 * rows * weights, 6 * rows * width + 2 * weights),
        name="first_rows",
    )(resid, mixed, *fixed)


def last_rows_kernel(
    r_ref,
    mixed_ref,
    up_ref,
    gain_ref,
    wo_ref,
    wg_ref,
    wu_ref,
    wd_ref,
    out_ref,
    hidden_ref,
    dd_ref,
    mlp_ref,
    dg_ref,
    du_ref,
    dmid_ref,
    db_ref,
    dmix_ref,
    gains_ref,
    gate_sc,
    up_sc,
):
    def keep(columns, gate_pre, up_pre, hidden):
        gate_sc[:, columns] = gate_pre
        up_sc[:, columns] = up_pre
        hidden_ref[:, columns] = hidden

    branch, middle, mlp_in, down_out = forward_rows(
        r_ref[...], mixed_ref[...], gain_ref, wo_ref, wg_ref, wu_ref, wd_ref, keep
    )
    mlp_ref[...] = mlp_in
    out_ref[...] = (middle + unit_rows(down_out)[1] * gain_ref[3:4, :]).astype(jnp.bfloat16)
    d_result = up_ref[...].astype(jnp.float32)
    d_down, gain_four = pull_norm(down_out, d_result, gain_ref[3:4, :])
    d_down = d_down.astype(jnp.bfloat16)
    dd_ref[...] = d_down
    d_mlp = None
    for at, size in column_chunks(wg_ref.shape[1]):
        columns = slice(at, at + size)
        d_hidden = dot_t(d_down, wd_ref[columns, :])
        gate_pre, up_pre = gate_sc[:, columns], up_sc[:, columns]
        sigma = 1.0 / (1.0 + jnp.exp(-gate_pre))
        d_gate = (d_hidden * up_pre * sigma * (1.0 + gate_pre * (1.0 - sigma))).astype(jnp.bfloat16)
        d_up = (d_hidden * gate_pre * sigma).astype(jnp.bfloat16)
        dg_ref[:, columns] = d_gate
        du_ref[:, columns] = d_up
        part = dot_t(d_gate, wg_ref[:, columns]) + dot_t(d_up, wu_ref[:, columns])
        d_mlp = part if d_mlp is None else d_mlp + part
    d_middle, gain_three = pull_norm(middle, d_mlp, gain_ref[2:3, :])
    d_middle = d_middle + d_result
    dmid_ref[...] = d_middle
    d_branch, gain_two = pull_norm(branch, d_middle, gain_ref[1:2, :])
    d_branch = d_branch.astype(jnp.bfloat16)
    db_ref[...] = d_branch
    dmix_ref[...] = dot_t(d_branch, wo_ref[...]).astype(jnp.bfloat16)

    @pl.when(pl.program_id(0) == 0)
    def _():
        gains_ref[...] = jnp.zeros_like(gains_ref)

    gains_ref[0:1, :] += gain_two
    gains_ref[1:2, :] += gain_three
    gains_ref[2:3, :] += gain_four


def last_rows(resid, mixed, upstream, gain_float, output_w, gate_w, up_w, down_w):
    rows, width = resid.shape
    inner = gate_w.shape[1]
    fixed = (gain_float, output_w, gate_w, up_w, down_w)
    weights = output_w.size + gate_w.size + up_w.size + down_w.size
    narrow, wide = (jax.ShapeDtypeStruct((rows, w), jnp.bfloat16) for w in (width, inner))
    tall = jax.ShapeDtypeStruct((rows, width), jnp.float32)
    outs = [narrow, wide, narrow, narrow, wide, wide, tall, narrow, narrow]
    return pl.pallas_call(
        last_rows_kernel,
        grid=(rows // TILE,),
        in_specs=[row_block(TILE, width)] * 3 + [whole_block(a) for a in fixed],
        out_specs=[row_block(TILE, one.shape[1]) for one in outs]
        + [pl.BlockSpec((8, width), lambda i: (0, 0))],
        out_shape=outs + [jax.ShapeDtypeStruct((8, width), jnp.float32)],
        scratch_shapes=[pltpu.VMEM((TILE, inner), jnp.float32)] * 2,
        compiler_params=compute_params(),
        cost_estimate=cost(4 * rows * weights, 30 * rows * width + 2 * weights),
        name="last_rows",
    )(resid, mixed, upstream, *fixed)


def weight_grad_kernel(left_ref, right_ref, out_ref):
    out_ref[...] = dot_w(left_ref[...], right_ref[...]).astype(out_ref.dtype)


def weight_grad(left, right, tile=256):
    rows, height = left.shape
    width = right.shape[1]
    return pl.pallas_call(
        weight_grad_kernel,
        grid=(height // tile,),
        in_specs=[pl.BlockSpec((rows, tile), lambda i: (0, i)), whole_block(right)],
        out_specs=row_block(tile, width),
        out_shape=jax.ShapeDtypeStruct((height, width), jnp.bfloat16),
        compiler_params=compute_params(),
        cost_estimate=cost(2 * rows * height * width, 2 * (rows * (height + width) + height * width)),
        name="weight_grad",
    )(left, right)


def back_heads_kernel(dq_ref, dk_ref, dv_ref, r_ref, dmid_ref, gain_ref, wq_ref, wk_ref, wv_ref, out_ref, gains_ref):
    d_normed = dot_t(dq_ref[...], wq_ref[...]) + dot_t(dk_ref[...], wk_ref[...]) + dot_t(dv_ref[...], wv_ref[...])
    d_resid, gain_one = pull_norm(r_ref[...], d_normed, gain_ref[0:1, :])
    out_ref[...] = (d_resid + dmid_ref[...]).astype(jnp.bfloat16)

    @pl.when(pl.program_id(0) == 0)
    def _():
        gains_ref[...] = jnp.zeros_like(gains_ref)

    gains_ref[0:1, :] += gain_one


def back_heads(d_query, d_key, d_value, resid, d_middle, gain_float, query_w, key_w, value_w):
    rows, width = resid.shape
    fixed = (gain_float, query_w, key_w, value_w)
    return pl.pallas_call(
        back_heads_kernel,
        grid=(rows // TILE,),
        in_specs=[row_block(TILE, width)] * 5 + [whole_block(a) for a in fixed],
        out_specs=[row_block(TILE, width), pl.BlockSpec((8, width), lambda i: (0, 0))],
        out_shape=[
            jax.ShapeDtypeStruct((rows, width), jnp.bfloat16),
            jax.ShapeDtypeStruct((8, width), jnp.float32),
        ],
        compiler_params=compute_params(),
        cost_estimate=cost(6 * rows * width * width, 16 * rows * width + 6 * width * width),
        name="back_heads",
    )(d_query, d_key, d_value, resid, d_middle, *fixed)


def home_back_kernel(
    target_ref, d_ref, final_ref, s_ref, e_ref, w_ref, first_ref, out_ref, ds_ref, de_ref, grad_ref, sum_ref
):
    step = pl.program_id(0)
    rows, width = ds_ref.shape
    count = d_ref.shape[0]
    at_column = lax.broadcasted_iota(jnp.int32, (rows, count), 1)
    order = (at_column == target_ref[...]).astype(jnp.bfloat16)
    out_ref[...] = dot_n(order, final_ref[...]).astype(jnp.bfloat16)
    d_home = dot_n(order, d_ref[...]).astype(jnp.bfloat16)
    ds_ref[...] = dot_t(d_home, w_ref[:width, :]).astype(jnp.bfloat16)
    de_ref[...] = dot_t(d_home, w_ref[width:, :]).astype(jnp.bfloat16)
    upper, lower = dot_w(s_ref[...], d_home), dot_w(e_ref[...], d_home)

    @pl.when(step == 0)
    def _():
        sum_ref[:width, :] = upper + first_ref[...]
        sum_ref[width:, :] = lower

    @pl.when(step > 0)
    def _():
        sum_ref[:width, :] += upper
        sum_ref[width:, :] += lower

    @pl.when(step == pl.num_programs(0) - 1)
    def _():
        grad_ref[...] = sum_ref[...].astype(jnp.bfloat16)


def back_at_home(target, d_home, final_slots, once, embeds, adapt_w, first_part):
    count, width = d_home.shape
    like = jax.ShapeDtypeStruct((count, width), jnp.bfloat16)
    return pl.pallas_call(
        home_back_kernel,
        grid=(count // TILE,),
        in_specs=[row_block(TILE, 1), whole_block(d_home), whole_block(final_slots)]
        + [row_block(TILE, width)] * 2
        + [whole_block(adapt_w), whole_block(first_part)],
        out_specs=[row_block(TILE, width)] * 3 + [pl.BlockSpec(adapt_w.shape, lambda i: (0, 0))],
        out_shape=[like] * 3 + [jax.ShapeDtypeStruct(adapt_w.shape, jnp.bfloat16)],
        scratch_shapes=[pltpu.VMEM(adapt_w.shape, jnp.float32)],
        compiler_params=compute_params(),
        cost_estimate=cost(12 * count * width * width, 20 * count * width),
        name="back_at_home",
    )(target, d_home, final_slots, once, embeds, adapt_w, first_part)


def paired_on_device(
    latents, embeds, cotangent, counts, w_adapt, w_query, w_key, w_value, w_out, w_gate, w_up, w_down, gains
):
    block_len, seqs, width = latents.shape
    parts = lax.axis_size("grp") * lax.axis_size("ctx")
    length = block_len * parts
    core = grid_place()[3]
    owner = core == 0

    twice = counts == 2
    slot = jnp.where(
        twice,
        2 * (jnp.cumsum(twice.astype(jnp.int32)) - 1),
        2 * (jnp.cumsum((~twice).astype(jnp.int32)) - 1) + 1,
    )
    row_count = block_len * seqs
    target = (slot[None, :] * block_len + jnp.arange(block_len, dtype=jnp.int32)[:, None]).reshape(row_count)
    latent_rows, embed_rows, slope_rows = (a.reshape(row_count, width) for a in (latents, embeds, cotangent))

    def exchange(values):
        return lax.all_to_all(values, BOTH, split_axis=0, concat_axis=0, tiled=True)

    adapt_w = gather_all([w_adapt], 0)[0].reshape(-1, width)
    starting, shared, upstream = adapt_at_home(
        target.reshape(1, row_count), latent_rows, embed_rows, slope_rows, adapt_w, block_len
    )

    half = block_len // 2
    shared = shared.reshape(parts // 2, 2, block_len, width)[:, 0].reshape(parts, half, width)
    leaving = jnp.concatenate([starting.reshape(parts, block_len, width), shared], 1)
    gain_rows = jnp.pad(gains.reshape(1, -1), ((0, 15), (0, 0)))
    leaving, *shards = lax.optimization_barrier(
        (leaving, w_query, w_key, w_value, w_out, w_gate, w_up, w_down, gain_rows)
    )
    arrived = exchange(leaving)
    *matrices, gain_float = gather_all(shards, 1)
    query_w, key_w, value_w, output_w, gate_w, up_w, down_w = (
        matrix.reshape(-1, matrix.shape[-1]) for matrix in matrices
    )
    gain_float = gain_float.reshape((parts,) + gain_rows.shape)[:, 0].reshape((parts,) + gains.shape)
    gain_float = gain_float.transpose(1, 0, 2).reshape(gains.shape[0], width).astype(jnp.float32)
    gate_w, arrived, upstream = lax.optimization_barrier((gate_w, arrived, upstream))
    starting = arrived[:, :block_len].reshape(length, width)
    shared = arrived[:, block_len:].reshape(length // 2, width)
    upstream = exchange(upstream.reshape(parts, block_len, width)).reshape(length, width)

    resid = shared
    local = jnp.arange(length // 2, dtype=jnp.int32)
    cos_half, sin_half = rope_full((local // half * 2 + core) * half + local % half)
    queries, keys_in, values_in = first_heads(resid, gain_float, query_w, key_w, value_w, cos_half, sin_half)
    far_keys, far_values = send(keys_in, 3), send(values_in, 3)
    mixed = attend_shared(core, half, queries, keys_in, values_in, far_keys, far_values)
    first_out = first_rows(resid, mixed, gain_float, output_w, gate_w, up_w, down_w)
    far_out = send(first_out, 3, -1)
    first_out = jnp.stack(
        [first_out.reshape(-1, half, width), far_out.reshape(-1, half, width)], 1
    ).reshape(length, width)
    first_out = jnp.where(owner, first_out, jnp.zeros_like(first_out))

    cos_full, sin_full = rope_full(jnp.arange(length, dtype=jnp.int32))
    resid, normed, queries, keys_in, values_in = last_heads(
        starting, first_out, adapt_w, gain_float, query_w, key_w, value_w, cos_full, sin_full
    )
    mixed, log_total = attend_whole(queries, keys_in, values_in)
    result, hidden, d_down, mlp_in, d_gate, d_up, d_middle, d_branch, d_mixed, gain_rest = last_rows(
        resid, mixed, upstream, gain_float, output_w, gate_w, up_w, down_w
    )
    final_back = exchange(result.reshape(parts, block_len, width))
    d_query, d_key, d_value = attend_whole_back(
        queries, keys_in, values_in, mixed, d_mixed, log_total, cos_full, sin_full
    )
    d_resid, gain_one = back_heads(
        d_query, d_key, d_value, resid, d_middle, gain_float, query_w, key_w, value_w
    )
    final_back, d_resid = lax.optimization_barrier((final_back, d_resid))
    d_home = exchange(d_resid.reshape(parts, block_len, width))
    down_part = weight_grad(hidden, d_down)
    gate_part = weight_grad(mlp_in, d_gate)
    up_part = weight_grad(mlp_in, d_up)
    out_part = weight_grad(mixed, d_branch)
    query_part = weight_grad(normed, d_query)
    key_part = weight_grad(normed, d_key)
    value_part = weight_grad(normed, d_value)
    first_part = dot_w(first_out, d_resid)

    def blocks(part):
        return part.reshape(parts, -1, part.shape[-1])

    gain_part = jnp.concatenate([gain_one[:1], gain_rest[:3]], 0)
    gain_part = gain_part.reshape(gains.shape[0], parts, gains.shape[1]).transpose(1, 0, 2)
    gain_part = jnp.pad(
        gain_part.reshape(parts, 1, gains.size).astype(jnp.bfloat16), ((0, 0), (0, 15), (0, 0))
    )
    sums = scatter_all(
        [
            blocks(part)
            for part in (query_part, key_part, value_part, out_part, gate_part, up_part, down_part)
        ]
        + [gain_part],
        2,
    )
    query_grad, key_grad, value_grad, out_grad, gate_grad, up_grad, down_grad, gain_grad = sums
    gain_grad = gain_grad[0].reshape(gains.shape)
    d_home, gate_grad = lax.optimization_barrier((d_home, gate_grad))

    once = jnp.where(twice[None, :, None], jnp.zeros_like(latents), latents).reshape(row_count, width)
    final_back, latent_back, embed_back, adapt_part = back_at_home(
        target.reshape(row_count, 1),
        d_home.reshape(row_count, width),
        final_back.reshape(row_count, width),
        once,
        embed_rows,
        adapt_w,
        first_part,
    )
    (adapt_grad,) = scatter_all([blocks(adapt_part)], 3)
    return (
        final_back.reshape(latents.shape),
        latent_back.reshape(latents.shape),
        embed_back.reshape(latents.shape),
        adapt_grad,
        query_grad,
        key_grad,
        value_grad,
        out_grad,
        gate_grad,
        up_grad,
        down_grad,
        gain_grad,
    )


def on_device(latents, *others):
    ctx = lax.axis_size("ctx")
    parts = lax.axis_size("grp") * ctx
    if latents.shape[1] == parts and ctx == 4 and latents.shape[0] % 16 == 0:
        return paired_on_device(latents, *others)
    return spread_on_device(latents, *others)


def solution(mesh):
    placed = (
        P(("grp", "ctx"), None, None),
        P(("grp", "ctx"), None, None),
        P(("grp", "ctx"), None, None),
        P(),
        P(("grp", "ctx"), None),
        P(("grp", "ctx"), None),
        P(("grp", "ctx"), None),
        P(("grp", "ctx"), None),
        P(("grp", "ctx"), None),
        P(("grp", "ctx"), None),
        P(("grp", "ctx"), None),
        P(("grp", "ctx"), None),
        P(None, ("grp", "ctx")),
    )
    return jax.shard_map(
        on_device,
        mesh=mesh,
        in_specs=placed,
        out_specs=(
            P(("grp", "ctx"), None, None),
            P(("grp", "ctx"), None, None),
            P(("grp", "ctx"), None, None),
            P(("grp", "ctx"), None),
            P(("grp", "ctx"), None),
            P(("grp", "ctx"), None),
            P(("grp", "ctx"), None),
            P(("grp", "ctx"), None),
            P(("grp", "ctx"), None),
            P(("grp", "ctx"), None),
            P(("grp", "ctx"), None),
            P(None, ("grp", "ctx")),
        ),
        check_vma=False,
    )
```

```python
import functools

import jax
import jax.numpy as jnp
from jax import lax
from jax.experimental import pallas as pl
from jax.experimental.pallas import tpu as pltpu
from jax.sharding import PartitionSpec as P

HEADS = 8
HEAD_DIM = 128


def rms_scale(values):
    return lax.rsqrt(jnp.mean(values * values, -1, keepdims=True) + 1e-06)


def norm_back(values, upstream, gain_vec):
    scale_rows = rms_scale(values)
    normal = values * scale_rows
    gain_part = jnp.sum(upstream * normal, 0)
    scaled = upstream * gain_vec
    return (
        scale_rows * (scaled - normal * jnp.mean(scaled * normal, -1, keepdims=True)),
        gain_part,
    )


def rope_table(positions):
    freq = 10000.0 ** (-2.0 * jnp.arange(HEAD_DIM // 2, dtype=jnp.float32) / HEAD_DIM)
    angle = positions.astype(jnp.float32)[:, None] * freq
    return (jnp.cos(angle), jnp.sin(angle))


def rotate(values, cosine, sine):
    half_dim = HEAD_DIM // 2
    first_half = values[..., :half_dim]
    second_half = values[..., half_dim:]
    cos_b = cosine[:, None, None, :]
    sin_b = sine[:, None, None, :]
    return jnp.concatenate(
        [first_half * cos_b - second_half * sin_b, second_half * cos_b + first_half * sin_b], -1
    )


def unrotate(grads, cosine, sine):
    half_dim = HEAD_DIM // 2
    first_half = grads[..., :half_dim]
    second_half = grads[..., half_dim:]
    cos_b = cosine[:, None, None, :]
    sin_b = sine[:, None, None, :]
    return jnp.concatenate(
        [first_half * cos_b + second_half * sin_b, second_half * cos_b - first_half * sin_b], -1
    )


def score_block(queries, keys_in, query_pos, key_pos_in):
    raw = jnp.einsum(
        "qshd,kshd->qshk", queries, keys_in, preferred_element_type=jnp.float32
    ) * HEAD_DIM ** (-0.5)
    causal = key_pos_in[None, :] <= query_pos[:, None]
    return jnp.where(causal[:, None, None, :], raw, -1e30)


def back_block(queries, keys_in, values_in, d_mixed, log_total, delta, query_pos, key_pos_in):
    scores = score_block(queries, keys_in, query_pos, key_pos_in)
    probs = jnp.exp(scores - log_total[..., None])
    d_probs = jnp.einsum("qshd,kshd->qshk", d_mixed, values_in, preferred_element_type=jnp.float32)
    slopes = (probs * (d_probs - delta[..., None])).astype(jnp.bfloat16)
    return (probs.astype(jnp.bfloat16), slopes)


def spread_on_device(
    latents,
    embeds,
    cotangent,
    counts,
    w_adapt,
    w_query,
    w_key,
    w_value,
    w_out,
    w_gate,
    w_up,
    w_down,
    gains,
):
    groups = lax.axis_size("grp")
    ctx_count = lax.axis_size("ctx")
    seq_total = latents.shape[1]
    seq_group = seq_total // groups
    block_len = latents.shape[0]
    model_width = latents.shape[2]
    group_len = groups * block_len
    adapt_w, query_w, key_w, value_w, output_w, gate_w, up_w, down_w, gain_rows = (
        lax.all_gather(w_adapt, ("grp", "ctx"), axis=0, tiled=True),
        lax.all_gather(w_query, ("grp", "ctx"), axis=0, tiled=True),
        lax.all_gather(w_key, ("grp", "ctx"), axis=0, tiled=True),
        lax.all_gather(w_value, ("grp", "ctx"), axis=0, tiled=True),
        lax.all_gather(w_out, ("grp", "ctx"), axis=0, tiled=True),
        lax.all_gather(w_gate, ("grp", "ctx"), axis=0, tiled=True),
        lax.all_gather(w_up, ("grp", "ctx"), axis=0, tiled=True),
        lax.all_gather(w_down, ("grp", "ctx"), axis=0, tiled=True),
        lax.all_gather(gains, ("grp", "ctx"), axis=1, tiled=True),
    )
    gain_float = gain_rows.astype(jnp.float32)
    seq_order = jnp.arange(seq_total, dtype=jnp.int32)
    latent_in, embed_in, slope_in = (
        lax.all_to_all(
            jnp.take(latents, seq_order, axis=1), "grp", split_axis=1, concat_axis=0, tiled=True
        ),
        lax.all_to_all(
            jnp.take(embeds, seq_order, axis=1), "grp", split_axis=1, concat_axis=0, tiled=True
        ),
        lax.all_to_all(
            jnp.take(cotangent, seq_order, axis=1), "grp", split_axis=1, concat_axis=0, tiled=True
        ),
    )
    ctx_index = lax.axis_index("ctx")

    def key_position(flat_index):
        source = flat_index // group_len
        within = flat_index % group_len
        return (within // block_len * ctx_count + source) * block_len + within % block_len

    query_pos = key_position(ctx_index * group_len + jnp.arange(group_len, dtype=jnp.int32))
    cos_query, sin_query = rope_table(query_pos)

    def attend_forward(queries, keys_in, values_in):
        piece = lax.all_gather(keys_in, "ctx", axis=0, tiled=True)
        scores = score_block(
            queries, piece, query_pos, key_position(jnp.arange(piece.shape[0], dtype=jnp.int32))
        )
        log_total = jax.nn.logsumexp(scores, -1)
        probs = jnp.exp(scores - log_total[..., None]).astype(jnp.bfloat16)
        mixed_raw = jnp.einsum(
            "qshk,kshd->qshd",
            probs,
            lax.all_gather(values_in, "ctx", axis=0, tiled=True),
            preferred_element_type=jnp.float32,
        )
        return (mixed_raw.astype(jnp.bfloat16), (queries, keys_in, values_in, log_total, mixed_raw))

    def core_block(latent, embedding):
        seq_batch = latent.shape[1]
        row_count = group_len * seq_batch
        joined = jnp.concatenate([latent.astype(jnp.bfloat16), embedding], -1).reshape(
            row_count, 2 * model_width
        )
        resid = jnp.dot(joined, adapt_w, preferred_element_type=jnp.float32)
        normed = (resid * rms_scale(resid) * gain_float[0]).astype(jnp.bfloat16)

        def heads_of(matrix):
            return jnp.dot(normed, matrix, preferred_element_type=jnp.float32).reshape(
                group_len, seq_batch, HEADS, HEAD_DIM
            )

        queries = rotate(heads_of(query_w), cos_query, sin_query).astype(jnp.bfloat16)
        keys_in = rotate(heads_of(key_w), cos_query, sin_query).astype(jnp.bfloat16)
        values_in = heads_of(value_w).astype(jnp.bfloat16)
        mixed, kept = attend_forward(queries, keys_in, values_in)
        mixed_flat = mixed.reshape(row_count, model_width)
        branch = jnp.dot(mixed_flat, output_w, preferred_element_type=jnp.float32)
        middle = resid + branch * rms_scale(branch) * gain_float[1]
        mlp_in = (middle * rms_scale(middle) * gain_float[2]).astype(jnp.bfloat16)
        gate_pre = jnp.dot(mlp_in, gate_w, preferred_element_type=jnp.float32)
        up_pre = jnp.dot(mlp_in, up_w, preferred_element_type=jnp.float32)
        hidden = (jax.nn.silu(gate_pre) * up_pre).astype(jnp.bfloat16)
        down_out = jnp.dot(hidden, down_w, preferred_element_type=jnp.float32)
        result = middle + down_out * rms_scale(down_out) * gain_float[3]
        flat_saved = tuple(
            (
                stored.reshape(group_len, seq_batch, stored.shape[-1])
                for stored in (
                    joined,
                    resid,
                    normed,
                    mixed_flat,
                    branch,
                    middle,
                    mlp_in,
                    gate_pre,
                    up_pre,
                    hidden,
                    down_out,
                )
            )
        )
        return (result.reshape(group_len, seq_batch, model_width), (flat_saved, kept))

    group_counts = lax.dynamic_slice_in_dim(
        jnp.take(counts, seq_order), lax.axis_index("grp") * seq_group, seq_group
    )
    first_out, first_saved = core_block(latent_in, embed_in)
    last_in = jnp.where(group_counts[None, :, None] == 2, first_out, latent_in.astype(jnp.float32))
    final_out, saved = core_block(last_in, embed_in)
    upstream = slope_in.astype(jnp.float32)
    flat_saved, kept = saved
    (
        joined,
        resid,
        normed,
        mixed_flat,
        branch,
        middle,
        mlp_in,
        gate_pre,
        up_pre,
        hidden,
        down_out,
    ) = tuple((stored.reshape(-1, stored.shape[-1]) for stored in flat_saved))
    seq_batch = upstream.shape[1]
    d_result = upstream.reshape(-1, model_width)
    d_down, gain_four = norm_back(down_out, d_result, gain_float[3])
    d_down = d_down.astype(jnp.bfloat16)
    down_part = jnp.einsum("rf,rd->fd", hidden, d_down, preferred_element_type=jnp.float32)
    d_hidden = jnp.einsum("rd,fd->rf", d_down, down_w, preferred_element_type=jnp.float32)
    sigma = jax.nn.sigmoid(gate_pre)
    d_gate = (d_hidden * up_pre * sigma * (1.0 + gate_pre * (1.0 - sigma))).astype(jnp.bfloat16)
    d_up = (d_hidden * gate_pre * sigma).astype(jnp.bfloat16)
    gate_part = jnp.einsum("rd,rf->df", mlp_in, d_gate, preferred_element_type=jnp.float32)
    up_part = jnp.einsum("rd,rf->df", mlp_in, d_up, preferred_element_type=jnp.float32)
    d_mlp = jnp.einsum(
        "rf,df->rd", d_gate, gate_w, preferred_element_type=jnp.float32
    ) + jnp.einsum("rf,df->rd", d_up, up_w, preferred_element_type=jnp.float32)
    d_middle, gain_three = norm_back(middle, d_mlp, gain_float[2])
    d_middle = d_middle + d_result
    d_branch, gain_two = norm_back(branch, d_middle, gain_float[1])
    d_branch = d_branch.astype(jnp.bfloat16)
    out_part = jnp.einsum("re,rd->ed", mixed_flat, d_branch, preferred_element_type=jnp.float32)
    d_mixed = jnp.einsum(
        "rd,ed->re", d_branch, output_w, preferred_element_type=jnp.float32
    ).astype(jnp.bfloat16)
    attend_d_mixed = d_mixed.reshape(group_len, seq_batch, HEADS, HEAD_DIM)
    queries, keys_in, values_in, log_total, mixed_raw = kept
    delta = jnp.sum(attend_d_mixed.astype(jnp.float32) * mixed_raw, -1)
    key_part = lax.all_gather(keys_in, "ctx", axis=0, tiled=True)
    value_part = lax.all_gather(values_in, "ctx", axis=0, tiled=True)
    key_pos_in = key_position(jnp.arange(key_part.shape[0], dtype=jnp.int32))
    probs_low, slopes = back_block(
        queries, key_part, value_part, attend_d_mixed, log_total, delta, query_pos, key_pos_in
    )
    d_query = HEAD_DIM ** (-0.5) * jnp.einsum(
        "qshk,kshd->qshd", slopes, key_part, preferred_element_type=jnp.float32
    )
    pull_stacked = jnp.stack([probs_low, slopes])
    d_query, stacked = (d_query, pull_stacked)
    d_key = HEAD_DIM ** (-0.5) * jnp.einsum(
        "qshk,qshd->kshd", stacked[1], queries, preferred_element_type=jnp.float32
    )
    d_value = jnp.einsum(
        "qshk,qshd->kshd", stacked[0], attend_d_mixed, preferred_element_type=jnp.float32
    )
    paired = lax.psum_scatter(
        jnp.concatenate([d_key, d_value], -1).astype(jnp.bfloat16),
        "ctx",
        scatter_dimension=0,
        tiled=True,
    ).astype(jnp.float32)
    d_query, d_key, d_value = (
        unrotate(d_query, cos_query, sin_query).astype(jnp.bfloat16),
        unrotate(paired[..., :HEAD_DIM], cos_query, sin_query).astype(jnp.bfloat16),
        paired[..., HEAD_DIM:].astype(jnp.bfloat16),
    )
    d_query = d_query.reshape(-1, model_width)
    d_key = d_key.reshape(-1, model_width)
    d_value = d_value.reshape(-1, model_width)
    query_part = jnp.einsum("rd,re->de", normed, d_query, preferred_element_type=jnp.float32)
    key_part = jnp.einsum("rd,re->de", normed, d_key, preferred_element_type=jnp.float32)
    value_part = jnp.einsum("rd,re->de", normed, d_value, preferred_element_type=jnp.float32)
    d_normed = (
        jnp.einsum("re,de->rd", d_query, query_w, preferred_element_type=jnp.float32)
        + jnp.einsum("re,de->rd", d_key, key_w, preferred_element_type=jnp.float32)
        + jnp.einsum("re,de->rd", d_value, value_w, preferred_element_type=jnp.float32)
    )
    d_resid, gain_one = norm_back(resid, d_normed, gain_float[0])
    d_resid = (d_resid + d_middle).astype(jnp.bfloat16)
    adapt_part = jnp.einsum("rk,rd->kd", joined, d_resid, preferred_element_type=jnp.float32)
    d_joined = jnp.einsum("rd,kd->rk", d_resid, adapt_w, preferred_element_type=jnp.float32)
    gain_part = jnp.stack([gain_one, gain_two, gain_three, gain_four])
    d_joined, grads = (
        d_joined.reshape(group_len, seq_batch, 2 * model_width),
        (
            adapt_part,
            query_part,
            key_part,
            value_part,
            out_part,
            gate_part,
            up_part,
            down_part,
            gain_part,
        ),
    )
    final_back, latent_back, embed_back = (
        lax.all_to_all(
            final_out.astype(jnp.bfloat16), "grp", split_axis=0, concat_axis=1, tiled=True
        ),
        lax.all_to_all(
            d_joined[..., :model_width].astype(jnp.bfloat16),
            "grp",
            split_axis=0,
            concat_axis=1,
            tiled=True,
        ),
        lax.all_to_all(
            d_joined[..., model_width:].astype(jnp.bfloat16),
            "grp",
            split_axis=0,
            concat_axis=1,
            tiled=True,
        ),
    )
    seq_index = jnp.arange(seq_total, dtype=jnp.int32)
    inverse = jnp.sum(jnp.where(seq_order[:, None] == seq_index[None, :], seq_index[:, None], 0), 0)
    (
        adapt_part,
        query_part,
        key_part,
        value_part,
        out_part,
        gate_part,
        up_part,
        down_part,
        gain_part,
    ) = grads
    summed = (
        lax.psum_scatter(adapt_part, ("grp", "ctx"), scatter_dimension=0, tiled=True),
        lax.psum_scatter(query_part, ("grp", "ctx"), scatter_dimension=0, tiled=True),
        lax.psum_scatter(key_part, ("grp", "ctx"), scatter_dimension=0, tiled=True),
        lax.psum_scatter(value_part, ("grp", "ctx"), scatter_dimension=0, tiled=True),
        lax.psum_scatter(out_part, ("grp", "ctx"), scatter_dimension=0, tiled=True),
        lax.psum_scatter(gate_part, ("grp", "ctx"), scatter_dimension=0, tiled=True),
        lax.psum_scatter(up_part, ("grp", "ctx"), scatter_dimension=0, tiled=True),
        lax.psum_scatter(down_part, ("grp", "ctx"), scatter_dimension=0, tiled=True),
        lax.psum_scatter(gain_part, ("grp", "ctx"), scatter_dimension=1, tiled=True),
    )
    return (
        jnp.take(final_back, inverse, axis=1),
        jnp.take(latent_back, inverse, axis=1),
        jnp.take(embed_back, inverse, axis=1),
        summed[0],
        summed[1],
        summed[2],
        summed[3],
        summed[4],
        summed[5],
        summed[6],
        summed[7],
        summed[8],
    )


BOTH = ("grp", "ctx")
LOG2E = 1.4426950408889634
SCALE = HEAD_DIM ** (-0.5)
TILE = 256
NEG = -1e30


def grid_sizes():
    ctx = lax.axis_size("ctx")
    x_size = ctx // 2
    return lax.axis_size("grp") // x_size, x_size, x_size, 2


def grid_place():
    z_size, y_size, x_size, k_size = grid_sizes()
    g, c = lax.axis_index("grp"), lax.axis_index("ctx")
    return g // y_size, g % y_size, c // k_size, c % k_size


def send(values, axis, shift=None, keep=None):
    sizes = grid_sizes()
    pairs = []
    for flat in range(sizes[0] * sizes[1] * sizes[2] * sizes[3]):
        rest, spot = flat, [0, 0, 0, 0]
        for at in (3, 2, 1, 0):
            spot[at] = rest % sizes[at]
            rest //= sizes[at]
        own = spot[axis]
        other = 1 - own if shift is None else own + shift
        if 0 <= other < sizes[axis] and (keep is None or keep(own)):
            spot[axis] = other
            target = ((spot[0] * sizes[1] + spot[1]) * sizes[2] + spot[2]) * sizes[3] + spot[3]
            pairs.append((flat, target))
    return lax.ppermute(values, BOTH, pairs)


MESH = pl.DeviceIdType.MESH


def device_at(z, y, x, k):
    _, y_size, _, k_size = grid_sizes()
    return (z * y_size + y, x * k_size + k)


def order_of(y, x, turn):
    first = (y + turn * (1 - 2 * y), x + (1 - turn) * (1 - 2 * x))
    second = (y + (1 - turn) * (1 - 2 * y), x + turn * (1 - 2 * x))
    return first, second


def greet_line(z, y, x, k, z_size):
    barrier = pltpu.get_barrier_semaphore()
    for device in (device_at(z, 1 - y, x, k), device_at(z, y, 1 - x, k), device_at(z, y, x, 1 - k)):
        pl.semaphore_signal(barrier, inc=1, device_id=device, device_id_type=MESH)

    @pl.when(z > 0)
    def _():
        pl.semaphore_signal(barrier, inc=1, device_id=device_at(z - 1, y, x, k), device_id_type=MESH)

    @pl.when(z < z_size - 1)
    def _():
        pl.semaphore_signal(barrier, inc=1, device_id=device_at(z + 1, y, x, k), device_id_type=MESH)

    pl.semaphore_wait(barrier, 3 + jnp.minimum(z, 1) + jnp.minimum(z_size - 1 - z, 1))


def remote(source, target, send_sem, recv_sem, device):
    return pltpu.make_async_remote_copy(
        src_ref=source,
        dst_ref=target,
        send_sem=send_sem,
        recv_sem=recv_sem,
        device_id=device,
        device_id_type=MESH,
    )


def row_views(shapes):
    views = []
    for at, (rows, width) in enumerate(shapes):
        if rows % 32 == 0 and rows * width >= 2**16:
            views += [(at, 0, rows // 2, 0), (at, rows // 2, rows // 2, 1)]
        else:
            views.append((at, 0, rows, at % 2))
    return views


def at_offsets(z, z_size, step, body):
    if step == 0:
        body(z, True, True)
        return

    @pl.when(z >= step)
    def _():
        body(z - step, True, False)

    @pl.when(z + step < z_size)
    def _():
        body(z + step, False, True)


def flat_device(at, ctx):
    return (at // ctx, at % ctx)


class Gather:
    def __init__(self, views, count, shards, outs, sems):
        self.z_size = grid_sizes()[0]
        self.place = grid_place()
        self.views, self.count, self.shards, self.outs = views, count, shards, outs
        self.local_sem, self.z_send, self.z_recv, self.p_send, self.p_recv, self.k_send, self.k_recv = sems

    def at(self, step, body):
        at_offsets(self.place[0], self.z_size, step, body)

    def spot(self, g, slot_z, at_y, at_x):
        at, first_row, rows, _ = self.views[g]
        return self.outs[at].at[slot_z, at_y, at_x, self.place[3], pl.ds(first_row, rows)]

    def z_copy(self, g, slot_z, way):
        z, y, x, k = self.place
        block = self.spot(g, slot_z, y, x)
        device = device_at(z + 1 - 2 * way, y, x, k)
        return remote(block, block, self.z_send.at[g, slot_z, way], self.z_recv.at[g, slot_z], device)

    def plane_copy(self, g, slot_z, kind):
        z, y, x, k = self.place
        first, second = order_of(y, x, (self.views[g][3] + slot_z) % 2)
        from_at = first if kind == 2 else (y, x)
        to_at = first if kind == 0 else second
        block = self.spot(g, slot_z, from_at[0], from_at[1])
        device = device_at(z, to_at[0], to_at[1], k)
        return remote(block, block, self.p_send.at[g, slot_z, kind], self.p_recv.at[g, slot_z, kind], device)

    def core_copy(self, at, slot_z):
        z, y, x, k = self.place
        block = self.outs[at].at[slot_z, :, :, k]
        return remote(block, block, self.k_send.at[at, slot_z], self.k_recv.at[at, slot_z], device_at(z, y, x, 1 - k))

    def own_copy(self, at):
        z, y, x, k = self.place
        return pltpu.make_async_copy(self.shards[at], self.outs[at].at[z, y, x, k], self.local_sem.at[at])

    def each_way(self, g, slot_z, up, down, act):
        z = self.place[0]
        if up:

            @pl.when(z < self.z_size - 1)
            def _():
                act(self.z_copy(g, slot_z, 0))

        if down:

            @pl.when(z > 0)
            def _():
                act(self.z_copy(g, slot_z, 1))

    def series(self, arrays):
        return [g for g, view in enumerate(self.views) if view[0] in arrays]

    def arrive(self, arrays, step):
        def body(slot_z, up, down):
            for g in self.series(arrays):
                if step > 0:
                    self.z_copy(g, slot_z, 1 if up else 0).wait_recv()
                self.each_way(g, slot_z, up, down, lambda copy: copy.start())

        self.at(step, body)

    def spread(self, arrays, step):
        def body(slot_z, up, down):
            for g in self.series(arrays):
                self.plane_copy(g, slot_z, 0).start()
                self.plane_copy(g, slot_z, 1).start()

        self.at(step, body)

    def pass_on(self, arrays, step):
        def body(slot_z, up, down):
            for g in self.series(arrays):
                self.plane_copy(g, slot_z, 0).wait_recv()
                self.plane_copy(g, slot_z, 2).start()

        self.at(step, body)

    def cross(self, arrays, step):
        def body(slot_z, up, down):
            for g in self.series(arrays):
                self.plane_copy(g, slot_z, 1).wait_recv()
                self.plane_copy(g, slot_z, 2).wait_recv()
            for at in arrays:
                self.core_copy(at, slot_z).start()

        self.at(step, body)

    def complete(self, arrays):
        for slot_z in range(self.z_size):
            for at in arrays:
                self.core_copy(at, slot_z).wait_recv()

    def settle(self, arrays):
        def body(slot_z, up, down):
            for g in self.series(arrays):
                self.each_way(g, slot_z, up, down, lambda copy: copy.wait_send())
                for kind in range(3):
                    self.plane_copy(g, slot_z, kind).wait_send()

        for step in range(self.z_size):
            self.at(step, body)
        for slot_z in range(self.z_size):
            for at in arrays:
                self.core_copy(at, slot_z).wait_send()


def open_kernel(views, count, block_len, *refs):
    z_size, _, x_size, k_size = grid_sizes()
    z, y, x, k = grid_place()
    ctx = x_size * k_size
    parts = lax.axis_size("grp") * ctx
    me = lax.axis_index("grp") * ctx + lax.axis_index("ctx")
    target_ref, s_ref, e_ref, c_ref = refs[:4]
    shards, refs = refs[4 : 4 + count], refs[4 + count :]
    outs, refs = refs[:count], refs[count:]
    shared_out, start_ref, up_ref, joined, shared_held = refs[:5]
    gather = Gather(views, count, shards, outs, refs[5:12])
    send_sem, recv_sem, own_sem = refs[12:]
    width = s_ref.shape[1]
    count_rows = s_ref.shape[0]
    half = block_len // 2
    tiles = count_rows // TILE
    slots = TILE // block_len
    adapt, early, late = (0,), (1, 2, 3, 4, 8), (5, 6, 7)

    barrier = pltpu.get_barrier_semaphore()

    def greet(at, carry):
        @pl.when(at != me)
        def _():
            pl.semaphore_signal(barrier, inc=1, device_id=flat_device(at, ctx), device_id_type=MESH)

        return carry

    lax.fori_loop(0, parts, greet, 0)
    pl.semaphore_wait(barrier, parts - 1)

    def half_copy(at):
        device = flat_device(at, ctx)
        return remote(shared_held.at[at], shared_out.at[me], send_sem.at[at], recv_sem.at[me], device)

    own_half = pltpu.make_async_copy(shared_held.at[me], shared_out.at[me], own_sem)

    def reorder(tile):
        rows = pl.ds(pl.multiple_of(tile * TILE, TILE), TILE)
        at_row = lax.broadcasted_iota(jnp.int32, (TILE, count_rows), 0) + tile * TILE
        order = (at_row == target_ref[...]).astype(jnp.bfloat16)
        joined[rows, :width] = dot_n(order, s_ref[...]).astype(jnp.bfloat16)
        joined[rows, width:] = dot_n(order, e_ref[...]).astype(jnp.bfloat16)
        up_ref[rows, :] = dot_n(order, c_ref[...]).astype(jnp.bfloat16)

    def apply(tile):
        rows = pl.ds(pl.multiple_of(tile * TILE, TILE), TILE)
        weight = outs[0][...].reshape(2 * width, width)
        embed_part = dot_n(joined[rows, width:], weight[width:]).astype(jnp.bfloat16)
        adapted = dot_n(joined[rows, :], weight).astype(jnp.bfloat16)
        for pair in range(slots // 2):
            at = tile * slots + 2 * pair
            even = slice(2 * pair * block_len, (2 * pair + 1) * block_len)
            odd = slice((2 * pair + 1) * block_len, (2 * pair + 2) * block_len)
            start_ref[at] = embed_part[even]
            start_ref[at + 1] = adapted[odd]
            shared_held[at] = adapted[even][:half]
            shared_held[at + 1] = adapted[even][half:]

        def leave(at, carry):
            @pl.when(at != me)
            def _():
                half_copy(at).start()

            return carry

        lax.fori_loop(tile * slots, (tile + 1) * slots, leave, 0)

    for at in range(count):
        gather.own_copy(at).start()
    gather.own_copy(0).wait()
    for step in range(z_size):
        gather.arrive(adapt, step)
        gather.spread(adapt, step)
        if step == 0:
            for at in early + late:
                gather.own_copy(at).wait()
        gather.arrive(early, step)
        if step < tiles:
            reorder(step)
        gather.spread(early, step)
        gather.pass_on(adapt, step)
        if step > 0:
            gather.cross(adapt, step - 1)
            gather.pass_on(early, step - 1)
        if step == z_size - 2:
            gather.arrive(late, 0)
    gather.spread(late, 0)
    gather.cross(adapt, z_size - 1)
    for tile in range(z_size, tiles):
        reorder(tile)
    gather.arrive(late, 1)
    gather.pass_on(early, z_size - 1)
    gather.spread(late, 1)
    gather.complete(adapt)
    for tile in range(tiles):
        apply(tile)
        if tile == 0:
            gather.pass_on(late, 0)
        if tile == 1:
            gather.arrive(late, 2)
            gather.spread(late, 2)
        if tile == 2:
            gather.pass_on(late, 1)
    own_half.start()
    gather.arrive(late, 3)
    gather.spread(late, 3)
    for step in range(z_size):
        gather.cross(early, step)
    gather.cross(late, 0)
    gather.pass_on(late, 2)
    gather.cross(late, 1)
    gather.pass_on(late, 3)
    gather.cross(late, 2)
    gather.cross(late, 3)
    gather.complete(early + late)
    gather.settle(adapt + early + late)

    def finish(at, carry):
        @pl.when(at != me)
        def _():
            device = flat_device(at, ctx)
            remote(shared_held.at[at], shared_out.at[at], send_sem.at[at], recv_sem.at[at], device).wait()

        return carry

    lax.fori_loop(0, parts, finish, 0)
    own_half.wait()


def open_all(target, latents, embeds, cotangent, shards, block_len, collective_id):
    sizes = grid_sizes()
    parts = lax.axis_size("grp") * lax.axis_size("ctx")
    count, z_size = len(shards), sizes[0]
    rows, width = latents.shape
    views = row_views([shard.shape for shard in shards])
    series = len(views)
    anywhere = pl.BlockSpec(memory_space=pl.ANY)
    near = pl.BlockSpec(memory_space=pltpu.VMEM)
    dma = pltpu.SemaphoreType.DMA
    half = block_len // 2
    return pl.pallas_call(
        functools.partial(open_kernel, views, count, block_len),
        in_specs=[near] * 4 + [anywhere] * count,
        out_specs=[near] + [anywhere] * count + [near] * 2,
        out_shape=[jax.ShapeDtypeStruct(sizes + shard.shape, shard.dtype) for shard in shards]
        + [
            jax.ShapeDtypeStruct((parts, half, width), jnp.bfloat16),
            jax.ShapeDtypeStruct((parts, block_len, width), jnp.bfloat16),
            jax.ShapeDtypeStruct((rows, width), jnp.bfloat16),
        ],
        scratch_shapes=[
            pltpu.VMEM((rows, 2 * width), jnp.bfloat16),
            pltpu.VMEM((parts, half, width), jnp.bfloat16),
            dma((count,)),
            dma((series, z_size, 2)),
            dma((series, z_size)),
            dma((series, z_size, 3)),
            dma((series, z_size, 3)),
            dma((count, z_size)),
            dma((count, z_size)),
            dma((parts,)),
            dma((parts,)),
            dma,
        ],
        compiler_params=pltpu.CompilerParams(
            collective_id=collective_id, has_side_effects=True, vmem_limit_bytes=56 * 2**20
        ),
        name="open_all",
    )(target, latents, embeds, cotangent, *shards)


class Scatter:
    def __init__(self, views, parts, outs, buffers, sems):
        self.z_size = grid_sizes()[0]
        self.place = grid_place()
        self.views, self.parts, self.outs = views, parts, outs
        count = len(parts)
        self.held, self.mine, self.from_second, self.from_first, self.from_z = (
            buffers[at * count : (at + 1) * count] for at in range(5)
        )
        self.local_sem, self.k_send, self.k_recv, self.p_send, self.p_recv, self.z_send, self.z_recv = sems

    def at(self, step, body):
        if 0 <= step < self.z_size:
            at_offsets(self.place[0], self.z_size, step, body)

    def series(self, arrays):
        return [g for g, view in enumerate(self.views) if view[0] in arrays]

    def rows_of(self, g):
        return pl.ds(self.views[g][1], self.views[g][2])

    def turns(self, g, slot_z):
        return order_of(self.place[1], self.place[2], (self.views[g][3] + slot_z) % 2)

    def core_copy(self, at, slot_z):
        z, y, x, k = self.place
        return remote(
            self.parts[at].at[slot_z, :, :, 1 - k],
            self.held[at].at[slot_z],
            self.k_send.at[at, slot_z],
            self.k_recv.at[at, slot_z],
            device_at(z, y, x, 1 - k),
        )

    def own_copy(self, at, slot_z, side):
        return pltpu.make_async_copy(
            self.parts[at].at[slot_z, :, :, self.place[3]], self.mine[at].at[side], self.local_sem.at[at, side]
        )

    def second_copy(self, g, slot_z, kind):
        z, y, x, k = self.place
        at, (_, second) = self.views[g][0], self.turns(g, slot_z)
        block = second if kind == 0 else (1 - y, 1 - x)
        return remote(
            self.held[at].at[slot_z, block[0], block[1], self.rows_of(g)],
            self.from_second[at].at[slot_z, kind, self.rows_of(g)],
            self.p_send.at[g, slot_z, kind],
            self.p_recv.at[g, slot_z, kind],
            device_at(z, second[0], second[1], k),
        )

    def first_copy(self, g, slot_z):
        z, y, x, k = self.place
        at, (first, _) = self.views[g][0], self.turns(g, slot_z)
        return remote(
            self.held[at].at[slot_z, first[0], first[1], self.rows_of(g)],
            self.from_first[at].at[slot_z, self.rows_of(g)],
            self.p_send.at[g, slot_z, 2],
            self.p_recv.at[g, slot_z, 2],
            device_at(z, first[0], first[1], k),
        )

    def z_copy(self, at, slot_z, way, lands_home, here=None):
        z, y, x, k = self.place
        side = z + 1 - 2 * way if here is None else here
        buffer = self.z_size if way == 1 and lands_home else slot_z
        return remote(
            self.held[at].at[slot_z, y, x],
            self.from_z[at].at[buffer],
            self.z_send.at[at, slot_z, way],
            self.z_recv.at[at, slot_z, way],
            device_at(side, y, x, k),
        )

    def begin(self, arrays):
        def body(slot_z, below, above):
            for at in arrays:
                self.core_copy(at, slot_z).start()

        for step in range(self.z_size - 1, -1, -1):
            self.at(step, body)

    def fold_core(self, arrays, step):
        def fetch(slot_z, below, above):
            for at in arrays:
                self.own_copy(at, slot_z, 0 if below else 1).start()

        def body(slot_z, below, above):
            _, y, x, _ = self.place
            side = 0 if below else 1
            for at in arrays:
                self.own_copy(at, slot_z, side).wait()
                self.core_copy(at, slot_z).wait_recv()
            for g in self.series(arrays):
                at, rows = self.views[g][0], self.rows_of(g)
                held, mine = self.held[at], self.mine[at]
                first, second = self.turns(g, slot_z)
                for spot in (second, (1 - y, 1 - x)):
                    here = (slot_z, spot[0], spot[1], rows)
                    held[here] = held[here] + mine[(side,) + here[1:]]
                self.second_copy(g, slot_z, 0).start()
                self.second_copy(g, slot_z, 1).start()
                for spot in (first, (y, x)):
                    here = (slot_z, spot[0], spot[1], rows)
                    held[here] = held[here] + mine[(side,) + here[1:]]

        self.at(step, fetch)
        self.at(step, body)

    def fold_second(self, arrays, step):
        def body(slot_z, below, above):
            for g in self.series(arrays):
                at, rows = self.views[g][0], self.rows_of(g)
                held, come = self.held[at], self.from_second[at]
                first, _ = self.turns(g, slot_z)
                self.second_copy(g, slot_z, 1).wait_recv()
                here = (slot_z, first[0], first[1], rows)
                held[here] = held[here] + come[slot_z, 1, rows]
                self.first_copy(g, slot_z).start()

        self.at(step, body)

    def fold_first(self, arrays, step):
        z, y, x, _ = self.place
        home = step == 0

        def body(slot_z, below, above):
            for g in self.series(arrays):
                at, rows = self.views[g][0], self.rows_of(g)
                held = self.held[at]
                here = (slot_z, y, x, rows)
                self.second_copy(g, slot_z, 0).wait_recv()
                self.first_copy(g, slot_z).wait_recv()
                held[here] = held[here] + self.from_second[at][slot_z, 0, rows] + self.from_first[at][slot_z, rows]
            if home:
                for at in arrays:
                    self.outs[at][...] = self.held[at][slot_z, y, x].astype(jnp.float32)
            for way, use in ((0, above), (1, below)):
                if not use:
                    continue
                came, source = (z > 0, z - 1) if way == 0 else (z < self.z_size - 1, z + 1)

                @pl.when(came)
                def _(way=way, source=source):
                    for at in arrays:
                        self.z_copy(at, slot_z, way, home, source).wait_recv()
                        come = self.from_z[at][self.z_size if way == 1 and home else slot_z]
                        if home:
                            self.outs[at][...] += come.astype(jnp.float32)
                        else:
                            self.held[at][slot_z, y, x] = self.held[at][slot_z, y, x] + come

                if not home:
                    for at in arrays:
                        self.z_copy(at, slot_z, way, step == 1).start()

        self.at(step, body)

    def settle(self, arrays):
        for step in range(self.z_size):

            def body(slot_z, below, above, step=step):
                for at in arrays:
                    self.core_copy(at, slot_z).wait_send()
                    if step > 0:
                        self.z_copy(at, slot_z, 0 if above else 1, step == 1).wait_send()
                for g in self.series(arrays):
                    self.second_copy(g, slot_z, 0).wait_send()
                    self.second_copy(g, slot_z, 1).wait_send()
                    self.first_copy(g, slot_z).wait_send()

            self.at(step, body)

    def stage(self, arrays, number):
        far = self.z_size - 1
        self.fold_core(arrays, far - number)
        self.fold_second(arrays, far - number + 1)
        self.fold_first(arrays, far - number + 2)

    def stages(self):
        return self.z_size + 2


def scatter_scratch(shapes):
    z_size, y_size, x_size, _ = grid_sizes()
    count, series = len(shapes), len(row_views(shapes))
    leads = ((z_size, y_size, x_size), (2, y_size, x_size), (z_size, 2), (z_size,), (z_size + 1,))
    dma = pltpu.SemaphoreType.DMA
    return [pltpu.VMEM(lead + shape, jnp.bfloat16) for lead in leads for shape in shapes] + [
        dma((count, 2)),
        dma((count, z_size)),
        dma((count, z_size)),
        dma((series, z_size, 3)),
        dma((series, z_size, 3)),
        dma((count, z_size, 2)),
        dma((count, z_size, 2)),
    ]


def dot_t(left, right):
    return lax.dot_general(left, right, (((1,), (1,)), ((), ())), preferred_element_type=jnp.float32)


def dot_n(left, right):
    return jnp.dot(left, right, preferred_element_type=jnp.float32)


def dot_w(left, right):
    return lax.dot_general(left, right, (((0,), (0,)), ((), ())), preferred_element_type=jnp.float32)


def below(rows, columns):
    at_row = lax.broadcasted_iota(jnp.int32, (rows, columns), 0)
    at_column = lax.broadcasted_iota(jnp.int32, (rows, columns), 1)
    return at_column <= at_row


def whole_attend(q_ref, k_ref, v_ref, o_ref, log_ref):
    head = pl.program_id(0)
    length = q_ref.shape[0]
    lane = lax.broadcasted_iota(jnp.int32, (TILE, 128), 1)
    for at in range(length // TILE):
        rows = pl.ds(at * TILE, TILE)
        seen = (at + 1) * TILE
        raw = dot_t(q_ref[rows, :], k_ref[:seen, :]) * (SCALE * LOG2E)
        last = jnp.where(below(TILE, TILE), raw[:, at * TILE :], NEG)
        raw = jnp.concatenate([raw[:, : at * TILE], last], 1) if at else last
        top = jnp.max(raw, 1, keepdims=True)
        weight = jnp.exp2(raw - top)
        total = jnp.sum(weight, 1, keepdims=True)
        mixed = dot_n(weight.astype(jnp.bfloat16), v_ref[:seen, :])
        o_ref[rows, :] = (mixed / total).astype(o_ref.dtype)
        log_total = top + jnp.log2(total)
        log_ref[rows, :] = jnp.where(lane == head, log_total, log_ref[rows, :])


def attend_whole(queries, keys_in, values_in):
    length, width = queries.shape
    head_block = pl.BlockSpec((length, HEAD_DIM), lambda h: (0, h))
    return pl.pallas_call(
        whole_attend,
        grid=(width // HEAD_DIM,),
        in_specs=[head_block] * 3,
        out_specs=[head_block, pl.BlockSpec((length, 128), lambda h: (0, 0))],
        out_shape=[
            jax.ShapeDtypeStruct((length, width), jnp.bfloat16),
            jax.ShapeDtypeStruct((length, 128), jnp.float32),
        ],
        compiler_params=pltpu.CompilerParams(vmem_limit_bytes=32 * 2**20),
        cost_estimate=pl.CostEstimate(
            flops=2 * length * length * width, bytes_accessed=8 * length * width, transcendentals=0
        ),
        name="attend_whole",
    )(queries, keys_in, values_in)


def shared_attend(block_len, core_ref, q_ref, k_ref, v_ref, ok_ref, ov_ref, o_ref):
    core = core_ref[0]
    length = q_ref.shape[0]
    for at in range(length // TILE):
        rows = pl.ds(at * TILE, TILE)
        seen = (at + 1) * TILE
        queries = q_ref[rows, :]
        raw = dot_t(queries, k_ref[:seen, :]) * (SCALE * LOG2E)
        far = dot_t(queries, ok_ref[:seen, :]) * (SCALE * LOG2E)
        at_row = lax.broadcasted_iota(jnp.int32, (TILE, TILE), 0)
        at_column = lax.broadcasted_iota(jnp.int32, (TILE, TILE), 1)
        near_last = jnp.where(at_column <= at_row, raw[:, at * TILE :], NEG)
        far_ok = at_column // block_len < at_row // block_len + core
        far_last = jnp.where(far_ok, far[:, at * TILE :], NEG)
        raw = jnp.concatenate([raw[:, : at * TILE], near_last], 1) if at else near_last
        far = jnp.concatenate([far[:, : at * TILE], far_last], 1) if at else far_last
        top = jnp.maximum(jnp.max(raw, 1, keepdims=True), jnp.max(far, 1, keepdims=True))
        weight = jnp.exp2(raw - top)
        far_weight = jnp.exp2(far - top)
        total = jnp.sum(weight, 1, keepdims=True) + jnp.sum(far_weight, 1, keepdims=True)
        mixed = dot_n(weight.astype(jnp.bfloat16), v_ref[:seen, :])
        mixed = mixed + dot_n(far_weight.astype(jnp.bfloat16), ov_ref[:seen, :])
        o_ref[rows, :] = (mixed / total).astype(o_ref.dtype)


def attend_shared(core, block_len, queries, keys_in, values_in, far_keys, far_values):
    length, width = queries.shape
    head_block = pl.BlockSpec((length, HEAD_DIM), lambda h: (0, h))
    return pl.pallas_call(
        functools.partial(shared_attend, block_len),
        grid=(width // HEAD_DIM,),
        in_specs=[pl.BlockSpec(memory_space=pltpu.SMEM)] + [head_block] * 5,
        out_specs=head_block,
        out_shape=jax.ShapeDtypeStruct((length, width), jnp.bfloat16),
        compiler_params=pltpu.CompilerParams(vmem_limit_bytes=32 * 2**20),
        cost_estimate=pl.CostEstimate(
            flops=4 * length * length * width, bytes_accessed=12 * length * width, transcendentals=0
        ),
        name="attend_shared",
    )(core.reshape(1), queries, keys_in, values_in, far_keys, far_values)


def middle_kernel(
    shapes,
    heads,
    q_ref,
    k_ref,
    v_ref,
    o_ref,
    do_ref,
    log_ref,
    cos_ref,
    sin_ref,
    r_ref,
    dmid_ref,
    gain_ref,
    wq_ref,
    wk_ref,
    wv_ref,
    normed_ref,
    mixed_ref,
    first_ref,
    db_ref,
    *refs,
):
    count = len(shapes)
    parts, refs = refs[:count], refs[count:]
    dr_ref, gains_ref, grad_ref = refs[:3]
    outs, refs = refs[3 : 3 + count], refs[3 + count :]
    dq_all, dk_all, dv_all, dk_sum, dv_sum = refs[:5]
    scatter = Scatter(row_views(shapes), parts, outs, refs[5 : 5 + 5 * count], refs[5 + 5 * count :])
    arrays = tuple(range(count))
    step = pl.program_id(0)
    length = q_ref.shape[0]
    tiles = length // TILE
    rest = heads + tiles
    total = rest + 5 * tiles

    @pl.when(step == 0)
    def _():
        greet_line(*scatter.place, scatter.z_size)
        scatter.begin(arrays)
        gains_ref[...] = jnp.zeros_like(gains_ref)

    for number in range(scatter.stages()):

        @pl.when(step == 2 + number * (total - 3) // scatter.stages())
        def _(number=number):
            scatter.stage(arrays, number)

    @pl.when(step < heads)
    def _():
        head = step
        columns = pl.ds(pl.multiple_of(head * HEAD_DIM, HEAD_DIM), HEAD_DIM)
        lane = lax.broadcasted_iota(jnp.int32, (TILE, 128), 1)

        def unrotated(grads, rows):
            turned = pltpu.roll(grads, HEAD_DIM // 2, 1)
            return grads * cos_ref[rows, :] - turned * sin_ref[rows, :]

        for at in range(tiles):
            rows = pl.ds(at * TILE, TILE)
            seen = (at + 1) * TILE
            queries, d_mixed = q_ref[rows, :], do_ref[rows, :]
            log_total = jnp.sum(jnp.where(lane == head, log_ref[rows, :], 0.0), 1, keepdims=True)
            delta = jnp.sum(d_mixed.astype(jnp.float32) * o_ref[rows, :].astype(jnp.float32), 1, keepdims=True)
            raw = dot_t(queries, k_ref[:seen, :]) * (SCALE * LOG2E)
            last = jnp.where(below(TILE, TILE), raw[:, at * TILE :], NEG)
            raw = jnp.concatenate([raw[:, : at * TILE], last], 1) if at else last
            probs = jnp.exp2(raw - log_total)
            d_probs = dot_t(d_mixed, v_ref[:seen, :])
            slopes = (probs * (d_probs - delta)).astype(jnp.bfloat16)
            d_query = dot_n(slopes, k_ref[:seen, :]) * SCALE
            dq_all[rows, columns] = unrotated(d_query, rows).astype(dq_all.dtype)
            d_value = dot_w(probs.astype(jnp.bfloat16), d_mixed)
            d_key = dot_w(slopes, queries)
            if at:
                before = pl.ds(0, at * TILE)
                dv_sum[before, :] += d_value[: at * TILE]
                dk_sum[before, :] += d_key[: at * TILE]
            dv_sum[rows, :] = d_value[at * TILE :]
            dk_sum[rows, :] = d_key[at * TILE :]
        dk_all[:, columns] = unrotated(dk_sum[...] * SCALE, pl.ds(0, length)).astype(dk_all.dtype)
        dv_all[:, columns] = dv_sum[...].astype(dv_all.dtype)

    @pl.when((step >= heads) & (step < rest))
    def _():
        rows = pl.ds(pl.multiple_of((step - heads) * TILE, TILE), TILE)
        d_normed = (
            dot_t(dq_all[rows, :], wq_ref[...])
            + dot_t(dk_all[rows, :], wk_ref[...])
            + dot_t(dv_all[rows, :], wv_ref[...])
        )
        d_resid, gain_one = pull_norm(r_ref[...], d_normed, gain_ref[0:1, :])
        dr_ref[rows, :] = (d_resid + dmid_ref[...]).astype(jnp.bfloat16)
        gains_ref[0:1, :] += gain_one

    pairs = (
        (normed_ref, dq_all),
        (normed_ref, dk_all),
        (normed_ref, dv_all),
        (mixed_ref, db_ref),
        (first_ref, dr_ref),
    )
    for at, (left, right) in enumerate(pairs):

        @pl.when((step >= rest + at * tiles) & (step < rest + (at + 1) * tiles))
        def _(left=left, right=right):
            grad_ref[...] = dot_w(left[...], right[...]).astype(grad_ref.dtype)

    @pl.when(step == total - 1)
    def _():
        scatter.settle(arrays)


def middle_all(
    queries,
    keys_in,
    values_in,
    mixed,
    d_mixed,
    log_total,
    cos_full,
    sin_full,
    resid,
    d_middle,
    gain_float,
    query_w,
    key_w,
    value_w,
    normed,
    first_out,
    d_branch,
    sums,
    collective_id,
):
    sizes = grid_sizes()
    length, width = queries.shape
    heads, tiles = width // HEAD_DIM, length // TILE
    rest = heads + tiles
    shapes = [part.shape[1:] for part in sums]
    head_block = pl.BlockSpec((length, HEAD_DIM), lambda i: (0, jnp.minimum(i, heads - 1)))
    tall_block = pl.BlockSpec((TILE, width), lambda i: (jnp.clip(i - heads, 0, tiles - 1), 0))

    def left_block(first, repeats=1):
        def place(i):
            inside = jnp.clip(i - rest - first * tiles, 0, repeats * tiles - 1)
            return (0, inside % tiles)

        return pl.BlockSpec((length, TILE), place)

    fixed = pl.BlockSpec((length, 128), lambda i: (0, 0), pipeline_mode=pl.Buffered(1))
    anywhere = pl.BlockSpec(memory_space=pl.ANY)
    near = pl.BlockSpec(memory_space=pltpu.VMEM)
    once = pl.Buffered(1)
    weights = sum(shape[0] * shape[1] for shape in shapes)
    return pl.pallas_call(
        functools.partial(middle_kernel, shapes, heads),
        grid=(rest + 5 * tiles,),
        in_specs=[head_block] * 5
        + [fixed] * 3
        + [tall_block] * 2
        + [whole_block(a) for a in (gain_float, query_w, key_w, value_w)]
        + [left_block(0, 3), left_block(3), left_block(4)]
        + [whole_block(d_branch)]
        + [anywhere] * len(sums),
        out_specs=[
            pl.BlockSpec((length, width), lambda i: (0, 0), pipeline_mode=once),
            pl.BlockSpec((8, width), lambda i: (0, 0), pipeline_mode=once),
            pl.BlockSpec((TILE, width), lambda i: (jnp.clip(i - rest, 0, 5 * tiles - 1), 0)),
        ]
        + [near] * len(sums),
        out_shape=[
            jax.ShapeDtypeStruct((length, width), jnp.bfloat16),
            jax.ShapeDtypeStruct((8, width), jnp.float32),
            jax.ShapeDtypeStruct((5 * width, width), jnp.bfloat16),
        ]
        + [jax.ShapeDtypeStruct(shape, jnp.float32) for shape in shapes],
        scratch_shapes=[pltpu.VMEM((length, width), jnp.bfloat16)] * 3
        + [pltpu.VMEM((length, HEAD_DIM), jnp.float32)] * 2
        + scatter_scratch(shapes),
        compiler_params=pltpu.CompilerParams(
            collective_id=collective_id, has_side_effects=True, vmem_limit_bytes=62 * 2**20
        ),
        cost_estimate=cost(24 * length * width * width, 64 * length * width + 64 * weights),
        name="middle_all",
    )(
        queries,
        keys_in,
        values_in,
        mixed,
        d_mixed,
        log_total,
        cos_full,
        sin_full,
        resid,
        d_middle,
        gain_float,
        query_w,
        key_w,
        value_w,
        normed,
        mixed,
        first_out,
        d_branch,
        *(part.reshape(sizes + part.shape[1:]) for part in sums),
    )


def rope_full(positions):
    cosine, sine = rope_table(positions)
    return jnp.concatenate([cosine, cosine], 1), jnp.concatenate([-sine, sine], 1)


def whole_block(array):
    return pl.BlockSpec(array.shape, lambda *_: (0,) * array.ndim, pipeline_mode=pl.Buffered(1))


def row_block(rows, width):
    return pl.BlockSpec((rows, width), lambda i: (i, 0))


def compute_params(megabytes=58):
    return pltpu.CompilerParams(vmem_limit_bytes=megabytes * 2**20)


def cost(flops, nbytes):
    return pl.CostEstimate(flops=int(flops), bytes_accessed=int(nbytes), transcendentals=0)


def unit_rows(values):
    scale_rows = rms_scale(values)
    return scale_rows, values * scale_rows


def pull_norm(values, upstream, gain_row):
    scale_rows, normal = unit_rows(values)
    gain_part = jnp.sum(upstream * normal, 0, keepdims=True)
    scaled = upstream * gain_row
    return scale_rows * (scaled - normal * jnp.mean(scaled * normal, -1, keepdims=True)), gain_part


def turned_heads(values, cos, sin):
    parts = []
    for head in range(values.shape[1] // HEAD_DIM):
        one = values[:, head * HEAD_DIM : (head + 1) * HEAD_DIM]
        parts.append(one * cos + pltpu.roll(one, HEAD_DIM // 2, 1) * sin)
    return jnp.concatenate(parts, 1)


def project_heads(resid, gain_ref, wq_ref, wk_ref, wv_ref, cos_ref, sin_ref, q_ref, k_ref, v_ref):
    normed = (unit_rows(resid)[1] * gain_ref[0:1, :]).astype(jnp.bfloat16)
    cos, sin = cos_ref[...], sin_ref[...]
    q_ref[...] = turned_heads(dot_n(normed, wq_ref[...]), cos, sin).astype(jnp.bfloat16)
    k_ref[...] = turned_heads(dot_n(normed, wk_ref[...]), cos, sin).astype(jnp.bfloat16)
    v_ref[...] = dot_n(normed, wv_ref[...]).astype(jnp.bfloat16)
    return normed


def first_heads_kernel(r_ref, gain_ref, wq_ref, wk_ref, wv_ref, cos_ref, sin_ref, q_ref, k_ref, v_ref):
    resid = r_ref[...].astype(jnp.float32)
    project_heads(resid, gain_ref, wq_ref, wk_ref, wv_ref, cos_ref, sin_ref, q_ref, k_ref, v_ref)


def first_heads(resid, gain_float, query_w, key_w, value_w, cos, sin):
    rows, width = resid.shape
    tile = min(TILE, rows)
    fixed = (gain_float, query_w, key_w, value_w)
    return pl.pallas_call(
        first_heads_kernel,
        grid=(rows // tile,),
        in_specs=[row_block(tile, width)] + [whole_block(a) for a in fixed] + [row_block(tile, HEAD_DIM)] * 2,
        out_specs=[row_block(tile, width)] * 3,
        out_shape=[jax.ShapeDtypeStruct((rows, width), jnp.bfloat16)] * 3,
        compiler_params=compute_params(),
        cost_estimate=cost(6 * rows * width * width, 8 * rows * width + 6 * width * width),
        name="first_heads",
    )(resid, *fixed, cos, sin)


def last_heads_kernel(
    start_ref, first_ref, wa_ref, gain_ref, wq_ref, wk_ref, wv_ref, cos_ref, sin_ref, r_ref, n_ref, q_ref, k_ref, v_ref
):
    resid = start_ref[...].astype(jnp.float32) + dot_n(first_ref[...], wa_ref[...])
    r_ref[...] = resid
    n_ref[...] = project_heads(resid, gain_ref, wq_ref, wk_ref, wv_ref, cos_ref, sin_ref, q_ref, k_ref, v_ref)


def last_heads(starting, first_out, adapt_w, gain_float, query_w, key_w, value_w, cos, sin):
    rows, width = starting.shape
    upper = pl.BlockSpec((width, width), lambda i: (0, 0), pipeline_mode=pl.Buffered(1))
    fixed = (gain_float, query_w, key_w, value_w)
    like = jax.ShapeDtypeStruct((rows, width), jnp.bfloat16)
    return pl.pallas_call(
        last_heads_kernel,
        grid=(rows // TILE,),
        in_specs=[row_block(TILE, width)] * 2
        + [upper]
        + [whole_block(a) for a in fixed]
        + [row_block(TILE, HEAD_DIM)] * 2,
        out_specs=[row_block(TILE, width)] * 5,
        out_shape=[jax.ShapeDtypeStruct((rows, width), jnp.float32)] + [like] * 4,
        compiler_params=compute_params(),
        cost_estimate=cost(8 * rows * width * width, 16 * rows * width + 8 * width * width),
        name="last_heads",
    )(starting, first_out, adapt_w, *fixed, cos, sin)


def column_chunks(total, chunk=768):
    return [(at, min(chunk, total - at)) for at in range(0, total, chunk)]


def forward_rows(resid, mixed, gain_ref, wo_ref, wg_ref, wu_ref, wd_ref, keep):
    branch = dot_n(mixed, wo_ref[...])
    middle = resid + unit_rows(branch)[1] * gain_ref[1:2, :]
    mlp_in = (unit_rows(middle)[1] * gain_ref[2:3, :]).astype(jnp.bfloat16)
    down_out = None
    for at, size in column_chunks(wg_ref.shape[1]):
        columns = slice(at, at + size)
        gate_pre = dot_n(mlp_in, wg_ref[:, columns])
        up_pre = dot_n(mlp_in, wu_ref[:, columns])
        sigma = 1.0 / (1.0 + jnp.exp(-gate_pre))
        hidden = (gate_pre * sigma * up_pre).astype(jnp.bfloat16)
        keep(columns, gate_pre, up_pre, hidden)
        part = dot_n(hidden, wd_ref[columns, :])
        down_out = part if down_out is None else down_out + part
    return branch, middle, mlp_in, down_out


def first_rows_kernel(r_ref, mixed_ref, gain_ref, wo_ref, wg_ref, wu_ref, wd_ref, out_ref):
    resid = r_ref[...].astype(jnp.float32)
    _, middle, _, down_out = forward_rows(
        resid, mixed_ref[...], gain_ref, wo_ref, wg_ref, wu_ref, wd_ref, lambda *_: None
    )
    out_ref[...] = (middle + unit_rows(down_out)[1] * gain_ref[3:4, :]).astype(jnp.bfloat16)


def first_rows(resid, mixed, gain_float, output_w, gate_w, up_w, down_w):
    rows, width = resid.shape
    tile = min(TILE, rows)
    fixed = (gain_float, output_w, gate_w, up_w, down_w)
    weights = output_w.size + gate_w.size + up_w.size + down_w.size
    return pl.pallas_call(
        first_rows_kernel,
        grid=(rows // tile,),
        in_specs=[row_block(tile, width)] * 2 + [whole_block(a) for a in fixed],
        out_specs=row_block(tile, width),
        out_shape=jax.ShapeDtypeStruct((rows, width), jnp.bfloat16),
        compiler_params=compute_params(),
        cost_estimate=cost(2 * rows * weights, 6 * rows * width + 2 * weights),
        name="first_rows",
    )(resid, mixed, *fixed)


def last_rows_kernel(
    r_ref,
    mixed_ref,
    up_ref,
    gain_ref,
    wo_ref,
    wg_ref,
    wu_ref,
    wd_ref,
    out_ref,
    hidden_ref,
    dd_ref,
    mlp_ref,
    dg_ref,
    du_ref,
    dmid_ref,
    db_ref,
    dmix_ref,
    gains_ref,
    gate_sc,
    up_sc,
):
    def keep(columns, gate_pre, up_pre, hidden):
        gate_sc[:, columns] = gate_pre
        up_sc[:, columns] = up_pre
        hidden_ref[:, columns] = hidden

    branch, middle, mlp_in, down_out = forward_rows(
        r_ref[...], mixed_ref[...], gain_ref, wo_ref, wg_ref, wu_ref, wd_ref, keep
    )
    mlp_ref[...] = mlp_in
    out_ref[...] = (middle + unit_rows(down_out)[1] * gain_ref[3:4, :]).astype(jnp.bfloat16)
    d_result = up_ref[...].astype(jnp.float32)
    d_down, gain_four = pull_norm(down_out, d_result, gain_ref[3:4, :])
    d_down = d_down.astype(jnp.bfloat16)
    dd_ref[...] = d_down
    d_mlp = None
    for at, size in column_chunks(wg_ref.shape[1]):
        columns = slice(at, at + size)
        d_hidden = dot_t(d_down, wd_ref[columns, :])
        gate_pre, up_pre = gate_sc[:, columns], up_sc[:, columns]
        sigma = 1.0 / (1.0 + jnp.exp(-gate_pre))
        d_gate = (d_hidden * up_pre * sigma * (1.0 + gate_pre * (1.0 - sigma))).astype(jnp.bfloat16)
        d_up = (d_hidden * gate_pre * sigma).astype(jnp.bfloat16)
        dg_ref[:, columns] = d_gate
        du_ref[:, columns] = d_up
        part = dot_t(d_gate, wg_ref[:, columns]) + dot_t(d_up, wu_ref[:, columns])
        d_mlp = part if d_mlp is None else d_mlp + part
    d_middle, gain_three = pull_norm(middle, d_mlp, gain_ref[2:3, :])
    d_middle = d_middle + d_result
    dmid_ref[...] = d_middle
    d_branch, gain_two = pull_norm(branch, d_middle, gain_ref[1:2, :])
    d_branch = d_branch.astype(jnp.bfloat16)
    db_ref[...] = d_branch
    dmix_ref[...] = dot_t(d_branch, wo_ref[...]).astype(jnp.bfloat16)

    @pl.when(pl.program_id(0) == 0)
    def _():
        gains_ref[...] = jnp.zeros_like(gains_ref)

    gains_ref[0:1, :] += gain_two
    gains_ref[1:2, :] += gain_three
    gains_ref[2:3, :] += gain_four


def last_rows(resid, mixed, upstream, gain_float, output_w, gate_w, up_w, down_w):
    rows, width = resid.shape
    inner = gate_w.shape[1]
    fixed = (gain_float, output_w, gate_w, up_w, down_w)
    weights = output_w.size + gate_w.size + up_w.size + down_w.size
    narrow, wide = (jax.ShapeDtypeStruct((rows, w), jnp.bfloat16) for w in (width, inner))
    tall = jax.ShapeDtypeStruct((rows, width), jnp.float32)
    outs = [narrow, wide, narrow, narrow, wide, wide, tall, narrow, narrow]
    return pl.pallas_call(
        last_rows_kernel,
        grid=(rows // TILE,),
        in_specs=[row_block(TILE, width)] * 3 + [whole_block(a) for a in fixed],
        out_specs=[row_block(TILE, one.shape[1]) for one in outs]
        + [pl.BlockSpec((8, width), lambda i: (0, 0))],
        out_shape=outs + [jax.ShapeDtypeStruct((8, width), jnp.float32)],
        scratch_shapes=[pltpu.VMEM((TILE, inner), jnp.float32)] * 2,
        compiler_params=compute_params(),
        cost_estimate=cost(4 * rows * weights, 30 * rows * width + 2 * weights),
        name="last_rows",
    )(resid, mixed, upstream, *fixed)


def weight_grad_kernel(left_ref, right_ref, out_ref):
    out_ref[...] = dot_w(left_ref[...], right_ref[...]).astype(out_ref.dtype)


def weight_grad(left, right, tile=256):
    rows, height = left.shape
    width = right.shape[1]
    return pl.pallas_call(
        weight_grad_kernel,
        grid=(height // tile,),
        in_specs=[pl.BlockSpec((rows, tile), lambda i: (0, i)), whole_block(right)],
        out_specs=row_block(tile, width),
        out_shape=jax.ShapeDtypeStruct((height, width), jnp.bfloat16),
        compiler_params=compute_params(),
        cost_estimate=cost(2 * rows * height * width, 2 * (rows * (height + width) + height * width)),
        name="weight_grad",
    )(left, right)


def close_kernel(target_ref, final_ref, w_ref, s_ref, e_ref, dr_ref, grad_ref, gain_ref, *refs):
    _, _, x_size, k_size = grid_sizes()
    ctx = x_size * k_size
    parts_count = lax.axis_size("grp") * ctx
    me = lax.axis_index("grp") * ctx + lax.axis_index("ctx")
    final_out, ds_ref, de_ref = refs[:3]
    outs, refs = refs[3:9], refs[9:]
    home, first, total, adapt_part = refs[:4]
    buffers, refs = refs[4:34], refs[34:]
    sems, (send_sem, recv_sem, own_sem) = refs[:7], refs[7:]
    parts = [grad_ref.at[at] for at in range(4)] + [adapt_part, gain_ref]
    scatter = Scatter(row_views([out.shape for out in outs]), parts, outs, buffers, sems)
    early, late = (0, 1, 2, 3, 5), (4,)
    count, width = ds_ref.shape
    tiles = count // TILE

    barrier = pltpu.get_barrier_semaphore()

    def greet(at, carry):
        @pl.when(at != me)
        def _():
            pl.semaphore_signal(barrier, inc=1, device_id=flat_device(at, ctx), device_id_type=MESH)

        return carry

    lax.fori_loop(0, parts_count, greet, 0)
    pl.semaphore_wait(barrier, parts_count - 1)

    def leave(at, carry):
        @pl.when(at != me)
        def _():
            remote(dr_ref.at[at], home.at[me], send_sem.at[at], recv_sem.at[me], flat_device(at, ctx)).start()

        return carry

    lax.fori_loop(0, parts_count, leave, 0)
    own = pltpu.make_async_copy(dr_ref.at[me], home.at[me], own_sem.at[0])
    own_first = pltpu.make_async_copy(grad_ref.at[4], first, own_sem.at[1])
    own.start()
    own_first.start()
    scatter.begin(early)

    def order_rows(tile):
        rows = pl.ds(pl.multiple_of(tile * TILE, TILE), TILE)
        at_column = lax.broadcasted_iota(jnp.int32, (TILE, count), 1)
        return rows, (at_column == target_ref[rows, :]).astype(jnp.bfloat16)

    def at_home(tile):
        rows, order = order_rows(tile)
        d_home = dot_n(order, home[...].reshape(count, width)).astype(jnp.bfloat16)
        ds_ref[rows, :] = dot_t(d_home, w_ref[:width, :]).astype(jnp.bfloat16)
        de_ref[rows, :] = dot_t(d_home, w_ref[width:, :]).astype(jnp.bfloat16)
        upper, lower = dot_w(s_ref[rows, :], d_home), dot_w(e_ref[rows, :], d_home)
        if tile == 0:
            total[:width, :] = upper + first[...].reshape(width, width).astype(jnp.float32)
            total[width:, :] = lower
        else:
            total[:width, :] += upper
            total[width:, :] += lower

    for number in range(4):
        scatter.stage(early, number)
        if number < tiles:
            rows, order = order_rows(number)
            final_out[rows, :] = dot_n(order, final_ref[...]).astype(jnp.bfloat16)

    def arrive(at, carry):
        @pl.when(at != me)
        def _():
            remote(dr_ref.at[at], home.at[at], send_sem.at[at], recv_sem.at[at], flat_device(at, ctx)).wait()

        return carry

    lax.fori_loop(0, parts_count, arrive, 0)
    own.wait()
    own_first.wait()
    for tile in range(tiles):
        at_home(tile)
        if tile < scatter.stages() - 4:
            scatter.stage(early, 4 + tile)
    adapt_part[...] = total[...].reshape(adapt_part.shape).astype(adapt_part.dtype)
    scatter.begin(late)
    for number in range(scatter.stages()):
        scatter.stage(late, number)
    scatter.settle(early)
    scatter.settle(late)


def close_all(
    target, final_slots, adapt_w, once, embeds, d_resid, weight_parts, gain_part, block_len, collective_id
):
    sizes = grid_sizes()
    parts = lax.axis_size("grp") * lax.axis_size("ctx")
    width = weight_parts.shape[1]
    count = target.shape[0]
    side = width // parts
    square = weight_parts.reshape((5,) + sizes + (side, width))
    gain = gain_part.reshape(sizes + gain_part.shape[1:])
    shapes = [(side, width)] * 4 + [(2 * side, width), gain_part.shape[1:]]
    anywhere = pl.BlockSpec(memory_space=pl.ANY)
    near = pl.BlockSpec(memory_space=pltpu.VMEM)
    dma = pltpu.SemaphoreType.DMA
    like = jax.ShapeDtypeStruct((count, width), jnp.bfloat16)
    return pl.pallas_call(
        close_kernel,
        in_specs=[near] * 5 + [anywhere] * 3,
        out_specs=[near] * (3 + len(shapes)),
        out_shape=[like] * 3 + [jax.ShapeDtypeStruct(shape, jnp.float32) for shape in shapes],
        scratch_shapes=[
            pltpu.VMEM((parts, block_len, width), jnp.bfloat16),
            pltpu.VMEM(sizes + (side, width), jnp.bfloat16),
            pltpu.VMEM((2 * width, width), jnp.float32),
            pltpu.VMEM(sizes + (2 * side, width), jnp.bfloat16),
        ]
        + scatter_scratch(shapes)
        + [dma((parts,)), dma((parts,)), dma((2,))],
        compiler_params=pltpu.CompilerParams(
            collective_id=collective_id, has_side_effects=True, vmem_limit_bytes=62 * 2**20
        ),
        name="close_all",
    )(target, final_slots, adapt_w, once, embeds, d_resid, square, gain)


def paired_on_device(
    latents, embeds, cotangent, counts, w_adapt, w_query, w_key, w_value, w_out, w_gate, w_up, w_down, gains
):
    block_len, seqs, width = latents.shape
    parts = lax.axis_size("grp") * lax.axis_size("ctx")
    length = block_len * parts
    core = grid_place()[3]
    owner = core == 0

    twice = counts == 2
    slot = jnp.where(
        twice,
        2 * (jnp.cumsum(twice.astype(jnp.int32)) - 1),
        2 * (jnp.cumsum((~twice).astype(jnp.int32)) - 1) + 1,
    )
    row_count = block_len * seqs
    target = (slot[None, :] * block_len + jnp.arange(block_len, dtype=jnp.int32)[:, None]).reshape(row_count)
    latent_rows, embed_rows, slope_rows = (a.reshape(row_count, width) for a in (latents, embeds, cotangent))

    def exchange(values):
        return lax.all_to_all(values, BOTH, split_axis=0, concat_axis=0, tiled=True)

    half = block_len // 2
    gain_rows = jnp.pad(gains.reshape(1, -1), ((0, 15), (0, 0)))
    *matrices, gain_float, shared, starting, upstream = open_all(
        target.reshape(1, row_count),
        latent_rows,
        embed_rows,
        slope_rows,
        [w_adapt, w_query, w_key, w_value, w_out, w_gate, w_up, w_down, gain_rows],
        block_len,
        0,
    )
    adapt_w, query_w, key_w, value_w, output_w, gate_w, up_w, down_w = (
        matrix.reshape(-1, matrix.shape[-1]) for matrix in matrices
    )
    gain_float = gain_float.reshape((parts,) + gain_rows.shape)[:, 0].reshape((parts,) + gains.shape)
    gain_float = gain_float.transpose(1, 0, 2).reshape(gains.shape[0], width).astype(jnp.float32)
    shared = shared.reshape(length // 2, width)
    starting = exchange(starting).reshape(length, width)

    resid = shared
    local = jnp.arange(length // 2, dtype=jnp.int32)
    cos_half, sin_half = rope_full((local // half * 2 + core) * half + local % half)
    queries, keys_in, values_in = first_heads(resid, gain_float, query_w, key_w, value_w, cos_half, sin_half)
    far_keys, far_values = send(keys_in, 3), send(values_in, 3)
    mixed = attend_shared(core, half, queries, keys_in, values_in, far_keys, far_values)
    first_out = first_rows(resid, mixed, gain_float, output_w, gate_w, up_w, down_w)
    first_out, upstream = lax.optimization_barrier((first_out, upstream))
    upstream = exchange(upstream.reshape(parts, block_len, width)).reshape(length, width)
    far_out = send(first_out, 3, -1)
    first_out = jnp.stack(
        [first_out.reshape(-1, half, width), far_out.reshape(-1, half, width)], 1
    ).reshape(length, width)
    first_out = jnp.where(owner, first_out, jnp.zeros_like(first_out))

    cos_full, sin_full = rope_full(jnp.arange(length, dtype=jnp.int32))
    resid, normed, queries, keys_in, values_in = last_heads(
        starting, first_out, adapt_w, gain_float, query_w, key_w, value_w, cos_full, sin_full
    )
    mixed, log_total = attend_whole(queries, keys_in, values_in)
    result, hidden, d_down, mlp_in, d_gate, d_up, d_middle, d_branch, d_mixed, gain_rest = last_rows(
        resid, mixed, upstream, gain_float, output_w, gate_w, up_w, down_w
    )
    final_back = exchange(result.reshape(parts, block_len, width))
    down_part = weight_grad(hidden, d_down)
    gate_part = weight_grad(mlp_in, d_gate)
    up_part = weight_grad(mlp_in, d_up)

    def blocks(part):
        return part.reshape(parts, -1, part.shape[-1])

    d_resid, gain_one, weight_parts, gate_grad, up_grad, down_grad = middle_all(
        queries,
        keys_in,
        values_in,
        mixed,
        d_mixed,
        log_total,
        cos_full,
        sin_full,
        resid,
        d_middle,
        gain_float,
        query_w,
        key_w,
        value_w,
        normed,
        first_out,
        d_branch,
        [blocks(part) for part in (gate_part, up_part, down_part)],
        1,
    )
    gain_part = jnp.concatenate([gain_one[:1], gain_rest[:3]], 0)
    gain_part = gain_part.reshape(gains.shape[0], parts, gains.shape[1]).transpose(1, 0, 2)
    gain_part = jnp.pad(
        gain_part.reshape(parts, 1, gains.size).astype(jnp.bfloat16), ((0, 0), (0, 15), (0, 0))
    )
    final_back, latent_back, embed_back, query_grad, key_grad, value_grad, out_grad, adapt_grad, gain_grad = close_all(
        target.reshape(row_count, 1),
        final_back.reshape(row_count, width),
        adapt_w,
        jnp.where(twice[None, :, None], jnp.zeros_like(latents), latents).reshape(row_count, width),
        embed_rows,
        blocks(d_resid),
        weight_parts,
        gain_part,
        block_len,
        2,
    )
    gain_grad = gain_grad[0].reshape(gains.shape)
    return (
        final_back.reshape(latents.shape),
        latent_back.reshape(latents.shape),
        embed_back.reshape(latents.shape),
        adapt_grad,
        query_grad,
        key_grad,
        value_grad,
        out_grad,
        gate_grad,
        up_grad,
        down_grad,
        gain_grad,
    )


def on_device(latents, *others):
    ctx = lax.axis_size("ctx")
    parts = lax.axis_size("grp") * ctx
    if latents.shape[1] == parts and ctx == 4 and latents.shape[0] % 16 == 0:
        return paired_on_device(latents, *others)
    return spread_on_device(latents, *others)


def solution(mesh):
    placed = (
        P(("grp", "ctx"), None, None),
        P(("grp", "ctx"), None, None),
        P(("grp", "ctx"), None, None),
        P(),
        P(("grp", "ctx"), None),
        P(("grp", "ctx"), None),
        P(("grp", "ctx"), None),
        P(("grp", "ctx"), None),
        P(("grp", "ctx"), None),
        P(("grp", "ctx"), None),
        P(("grp", "ctx"), None),
        P(("grp", "ctx"), None),
        P(None, ("grp", "ctx")),
    )
    return jax.shard_map(
        on_device,
        mesh=mesh,
        in_specs=placed,
        out_specs=(
            P(("grp", "ctx"), None, None),
            P(("grp", "ctx"), None, None),
            P(("grp", "ctx"), None, None),
            P(("grp", "ctx"), None),
            P(("grp", "ctx"), None),
            P(("grp", "ctx"), None),
            P(("grp", "ctx"), None),
            P(("grp", "ctx"), None),
            P(("grp", "ctx"), None),
            P(("grp", "ctx"), None),
            P(("grp", "ctx"), None),
            P(None, ("grp", "ctx")),
        ),
        check_vma=False,
    )
```

```python
import functools

import jax
import jax.numpy as jnp
import numpy as np
from jax import lax
from jax.experimental import pallas as pl
from jax.experimental.pallas import tpu as pltpu
from jax.sharding import PartitionSpec as P

HEADS = 8
HEAD_DIM = 128


def rms_scale(values):
    return lax.rsqrt(jnp.mean(values * values, -1, keepdims=True) + 1e-06)


def norm_back(values, upstream, gain_vec):
    scale_rows = rms_scale(values)
    normal = values * scale_rows
    gain_part = jnp.sum(upstream * normal, 0)
    scaled = upstream * gain_vec
    return (
        scale_rows * (scaled - normal * jnp.mean(scaled * normal, -1, keepdims=True)),
        gain_part,
    )


def rope_table(positions):
    freq = 10000.0 ** (-2.0 * jnp.arange(HEAD_DIM // 2, dtype=jnp.float32) / HEAD_DIM)
    angle = positions.astype(jnp.float32)[:, None] * freq
    return (jnp.cos(angle), jnp.sin(angle))


def rotate(values, cosine, sine):
    half_dim = HEAD_DIM // 2
    first_half = values[..., :half_dim]
    second_half = values[..., half_dim:]
    cos_b = cosine[:, None, None, :]
    sin_b = sine[:, None, None, :]
    return jnp.concatenate(
        [first_half * cos_b - second_half * sin_b, second_half * cos_b + first_half * sin_b], -1
    )


def unrotate(grads, cosine, sine):
    half_dim = HEAD_DIM // 2
    first_half = grads[..., :half_dim]
    second_half = grads[..., half_dim:]
    cos_b = cosine[:, None, None, :]
    sin_b = sine[:, None, None, :]
    return jnp.concatenate(
        [first_half * cos_b + second_half * sin_b, second_half * cos_b - first_half * sin_b], -1
    )


def score_block(queries, keys_in, query_pos, key_pos_in):
    raw = jnp.einsum(
        "qshd,kshd->qshk", queries, keys_in, preferred_element_type=jnp.float32
    ) * HEAD_DIM ** (-0.5)
    causal = key_pos_in[None, :] <= query_pos[:, None]
    return jnp.where(causal[:, None, None, :], raw, -1e30)


def back_block(queries, keys_in, values_in, d_mixed, log_total, delta, query_pos, key_pos_in):
    scores = score_block(queries, keys_in, query_pos, key_pos_in)
    probs = jnp.exp(scores - log_total[..., None])
    d_probs = jnp.einsum("qshd,kshd->qshk", d_mixed, values_in, preferred_element_type=jnp.float32)
    slopes = (probs * (d_probs - delta[..., None])).astype(jnp.bfloat16)
    return (probs.astype(jnp.bfloat16), slopes)


def spread_on_device(
    latents,
    embeds,
    cotangent,
    counts,
    w_adapt,
    w_query,
    w_key,
    w_value,
    w_out,
    w_gate,
    w_up,
    w_down,
    gains,
):
    groups = lax.axis_size("grp")
    ctx_count = lax.axis_size("ctx")
    seq_total = latents.shape[1]
    seq_group = seq_total // groups
    block_len = latents.shape[0]
    model_width = latents.shape[2]
    group_len = groups * block_len
    adapt_w, query_w, key_w, value_w, output_w, gate_w, up_w, down_w, gain_rows = (
        lax.all_gather(w_adapt, ("grp", "ctx"), axis=0, tiled=True),
        lax.all_gather(w_query, ("grp", "ctx"), axis=0, tiled=True),
        lax.all_gather(w_key, ("grp", "ctx"), axis=0, tiled=True),
        lax.all_gather(w_value, ("grp", "ctx"), axis=0, tiled=True),
        lax.all_gather(w_out, ("grp", "ctx"), axis=0, tiled=True),
        lax.all_gather(w_gate, ("grp", "ctx"), axis=0, tiled=True),
        lax.all_gather(w_up, ("grp", "ctx"), axis=0, tiled=True),
        lax.all_gather(w_down, ("grp", "ctx"), axis=0, tiled=True),
        lax.all_gather(gains, ("grp", "ctx"), axis=1, tiled=True),
    )
    gain_float = gain_rows.astype(jnp.float32)
    seq_order = jnp.arange(seq_total, dtype=jnp.int32)
    latent_in, embed_in, slope_in = (
        lax.all_to_all(
            jnp.take(latents, seq_order, axis=1), "grp", split_axis=1, concat_axis=0, tiled=True
        ),
        lax.all_to_all(
            jnp.take(embeds, seq_order, axis=1), "grp", split_axis=1, concat_axis=0, tiled=True
        ),
        lax.all_to_all(
            jnp.take(cotangent, seq_order, axis=1), "grp", split_axis=1, concat_axis=0, tiled=True
        ),
    )
    ctx_index = lax.axis_index("ctx")

    def key_position(flat_index):
        source = flat_index // group_len
        within = flat_index % group_len
        return (within // block_len * ctx_count + source) * block_len + within % block_len

    query_pos = key_position(ctx_index * group_len + jnp.arange(group_len, dtype=jnp.int32))
    cos_query, sin_query = rope_table(query_pos)

    def attend_forward(queries, keys_in, values_in):
        piece = lax.all_gather(keys_in, "ctx", axis=0, tiled=True)
        scores = score_block(
            queries, piece, query_pos, key_position(jnp.arange(piece.shape[0], dtype=jnp.int32))
        )
        log_total = jax.nn.logsumexp(scores, -1)
        probs = jnp.exp(scores - log_total[..., None]).astype(jnp.bfloat16)
        mixed_raw = jnp.einsum(
            "qshk,kshd->qshd",
            probs,
            lax.all_gather(values_in, "ctx", axis=0, tiled=True),
            preferred_element_type=jnp.float32,
        )
        return (mixed_raw.astype(jnp.bfloat16), (queries, keys_in, values_in, log_total, mixed_raw))

    def core_block(latent, embedding):
        seq_batch = latent.shape[1]
        row_count = group_len * seq_batch
        joined = jnp.concatenate([latent.astype(jnp.bfloat16), embedding], -1).reshape(
            row_count, 2 * model_width
        )
        resid = jnp.dot(joined, adapt_w, preferred_element_type=jnp.float32)
        normed = (resid * rms_scale(resid) * gain_float[0]).astype(jnp.bfloat16)

        def heads_of(matrix):
            return jnp.dot(normed, matrix, preferred_element_type=jnp.float32).reshape(
                group_len, seq_batch, HEADS, HEAD_DIM
            )

        queries = rotate(heads_of(query_w), cos_query, sin_query).astype(jnp.bfloat16)
        keys_in = rotate(heads_of(key_w), cos_query, sin_query).astype(jnp.bfloat16)
        values_in = heads_of(value_w).astype(jnp.bfloat16)
        mixed, kept = attend_forward(queries, keys_in, values_in)
        mixed_flat = mixed.reshape(row_count, model_width)
        branch = jnp.dot(mixed_flat, output_w, preferred_element_type=jnp.float32)
        middle = resid + branch * rms_scale(branch) * gain_float[1]
        mlp_in = (middle * rms_scale(middle) * gain_float[2]).astype(jnp.bfloat16)
        gate_pre = jnp.dot(mlp_in, gate_w, preferred_element_type=jnp.float32)
        up_pre = jnp.dot(mlp_in, up_w, preferred_element_type=jnp.float32)
        hidden = (jax.nn.silu(gate_pre) * up_pre).astype(jnp.bfloat16)
        down_out = jnp.dot(hidden, down_w, preferred_element_type=jnp.float32)
        result = middle + down_out * rms_scale(down_out) * gain_float[3]
        flat_saved = tuple(
            (
                stored.reshape(group_len, seq_batch, stored.shape[-1])
                for stored in (
                    joined,
                    resid,
                    normed,
                    mixed_flat,
                    branch,
                    middle,
                    mlp_in,
                    gate_pre,
                    up_pre,
                    hidden,
                    down_out,
                )
            )
        )
        return (result.reshape(group_len, seq_batch, model_width), (flat_saved, kept))

    group_counts = lax.dynamic_slice_in_dim(
        jnp.take(counts, seq_order), lax.axis_index("grp") * seq_group, seq_group
    )
    first_out, first_saved = core_block(latent_in, embed_in)
    last_in = jnp.where(group_counts[None, :, None] == 2, first_out, latent_in.astype(jnp.float32))
    final_out, saved = core_block(last_in, embed_in)
    upstream = slope_in.astype(jnp.float32)
    flat_saved, kept = saved
    (
        joined,
        resid,
        normed,
        mixed_flat,
        branch,
        middle,
        mlp_in,
        gate_pre,
        up_pre,
        hidden,
        down_out,
    ) = tuple((stored.reshape(-1, stored.shape[-1]) for stored in flat_saved))
    seq_batch = upstream.shape[1]
    d_result = upstream.reshape(-1, model_width)
    d_down, gain_four = norm_back(down_out, d_result, gain_float[3])
    d_down = d_down.astype(jnp.bfloat16)
    down_part = jnp.einsum("rf,rd->fd", hidden, d_down, preferred_element_type=jnp.float32)
    d_hidden = jnp.einsum("rd,fd->rf", d_down, down_w, preferred_element_type=jnp.float32)
    sigma = jax.nn.sigmoid(gate_pre)
    d_gate = (d_hidden * up_pre * sigma * (1.0 + gate_pre * (1.0 - sigma))).astype(jnp.bfloat16)
    d_up = (d_hidden * gate_pre * sigma).astype(jnp.bfloat16)
    gate_part = jnp.einsum("rd,rf->df", mlp_in, d_gate, preferred_element_type=jnp.float32)
    up_part = jnp.einsum("rd,rf->df", mlp_in, d_up, preferred_element_type=jnp.float32)
    d_mlp = jnp.einsum(
        "rf,df->rd", d_gate, gate_w, preferred_element_type=jnp.float32
    ) + jnp.einsum("rf,df->rd", d_up, up_w, preferred_element_type=jnp.float32)
    d_middle, gain_three = norm_back(middle, d_mlp, gain_float[2])
    d_middle = d_middle + d_result
    d_branch, gain_two = norm_back(branch, d_middle, gain_float[1])
    d_branch = d_branch.astype(jnp.bfloat16)
    out_part = jnp.einsum("re,rd->ed", mixed_flat, d_branch, preferred_element_type=jnp.float32)
    d_mixed = jnp.einsum(
        "rd,ed->re", d_branch, output_w, preferred_element_type=jnp.float32
    ).astype(jnp.bfloat16)
    attend_d_mixed = d_mixed.reshape(group_len, seq_batch, HEADS, HEAD_DIM)
    queries, keys_in, values_in, log_total, mixed_raw = kept
    delta = jnp.sum(attend_d_mixed.astype(jnp.float32) * mixed_raw, -1)
    key_part = lax.all_gather(keys_in, "ctx", axis=0, tiled=True)
    value_part = lax.all_gather(values_in, "ctx", axis=0, tiled=True)
    key_pos_in = key_position(jnp.arange(key_part.shape[0], dtype=jnp.int32))
    probs_low, slopes = back_block(
        queries, key_part, value_part, attend_d_mixed, log_total, delta, query_pos, key_pos_in
    )
    d_query = HEAD_DIM ** (-0.5) * jnp.einsum(
        "qshk,kshd->qshd", slopes, key_part, preferred_element_type=jnp.float32
    )
    pull_stacked = jnp.stack([probs_low, slopes])
    d_query, stacked = (d_query, pull_stacked)
    d_key = HEAD_DIM ** (-0.5) * jnp.einsum(
        "qshk,qshd->kshd", stacked[1], queries, preferred_element_type=jnp.float32
    )
    d_value = jnp.einsum(
        "qshk,qshd->kshd", stacked[0], attend_d_mixed, preferred_element_type=jnp.float32
    )
    paired = lax.psum_scatter(
        jnp.concatenate([d_key, d_value], -1).astype(jnp.bfloat16),
        "ctx",
        scatter_dimension=0,
        tiled=True,
    ).astype(jnp.float32)
    d_query, d_key, d_value = (
        unrotate(d_query, cos_query, sin_query).astype(jnp.bfloat16),
        unrotate(paired[..., :HEAD_DIM], cos_query, sin_query).astype(jnp.bfloat16),
        paired[..., HEAD_DIM:].astype(jnp.bfloat16),
    )
    d_query = d_query.reshape(-1, model_width)
    d_key = d_key.reshape(-1, model_width)
    d_value = d_value.reshape(-1, model_width)
    query_part = jnp.einsum("rd,re->de", normed, d_query, preferred_element_type=jnp.float32)
    key_part = jnp.einsum("rd,re->de", normed, d_key, preferred_element_type=jnp.float32)
    value_part = jnp.einsum("rd,re->de", normed, d_value, preferred_element_type=jnp.float32)
    d_normed = (
        jnp.einsum("re,de->rd", d_query, query_w, preferred_element_type=jnp.float32)
        + jnp.einsum("re,de->rd", d_key, key_w, preferred_element_type=jnp.float32)
        + jnp.einsum("re,de->rd", d_value, value_w, preferred_element_type=jnp.float32)
    )
    d_resid, gain_one = norm_back(resid, d_normed, gain_float[0])
    d_resid = (d_resid + d_middle).astype(jnp.bfloat16)
    adapt_part = jnp.einsum("rk,rd->kd", joined, d_resid, preferred_element_type=jnp.float32)
    d_joined = jnp.einsum("rd,kd->rk", d_resid, adapt_w, preferred_element_type=jnp.float32)
    gain_part = jnp.stack([gain_one, gain_two, gain_three, gain_four])
    d_joined, grads = (
        d_joined.reshape(group_len, seq_batch, 2 * model_width),
        (
            adapt_part,
            query_part,
            key_part,
            value_part,
            out_part,
            gate_part,
            up_part,
            down_part,
            gain_part,
        ),
    )
    final_back, latent_back, embed_back = (
        lax.all_to_all(
            final_out.astype(jnp.bfloat16), "grp", split_axis=0, concat_axis=1, tiled=True
        ),
        lax.all_to_all(
            d_joined[..., :model_width].astype(jnp.bfloat16),
            "grp",
            split_axis=0,
            concat_axis=1,
            tiled=True,
        ),
        lax.all_to_all(
            d_joined[..., model_width:].astype(jnp.bfloat16),
            "grp",
            split_axis=0,
            concat_axis=1,
            tiled=True,
        ),
    )
    seq_index = jnp.arange(seq_total, dtype=jnp.int32)
    inverse = jnp.sum(jnp.where(seq_order[:, None] == seq_index[None, :], seq_index[:, None], 0), 0)
    (
        adapt_part,
        query_part,
        key_part,
        value_part,
        out_part,
        gate_part,
        up_part,
        down_part,
        gain_part,
    ) = grads
    summed = (
        lax.psum_scatter(adapt_part, ("grp", "ctx"), scatter_dimension=0, tiled=True),
        lax.psum_scatter(query_part, ("grp", "ctx"), scatter_dimension=0, tiled=True),
        lax.psum_scatter(key_part, ("grp", "ctx"), scatter_dimension=0, tiled=True),
        lax.psum_scatter(value_part, ("grp", "ctx"), scatter_dimension=0, tiled=True),
        lax.psum_scatter(out_part, ("grp", "ctx"), scatter_dimension=0, tiled=True),
        lax.psum_scatter(gate_part, ("grp", "ctx"), scatter_dimension=0, tiled=True),
        lax.psum_scatter(up_part, ("grp", "ctx"), scatter_dimension=0, tiled=True),
        lax.psum_scatter(down_part, ("grp", "ctx"), scatter_dimension=0, tiled=True),
        lax.psum_scatter(gain_part, ("grp", "ctx"), scatter_dimension=1, tiled=True),
    )
    return (
        jnp.take(final_back, inverse, axis=1),
        jnp.take(latent_back, inverse, axis=1),
        jnp.take(embed_back, inverse, axis=1),
        summed[0],
        summed[1],
        summed[2],
        summed[3],
        summed[4],
        summed[5],
        summed[6],
        summed[7],
        summed[8],
    )


BOTH = ("grp", "ctx")
LOG2E = 1.4426950408889634
SCALE = HEAD_DIM ** (-0.5)
TILE = 256
NEG = -1e30


def grid_sizes():
    ctx = lax.axis_size("ctx")
    x_size = ctx // 2
    return lax.axis_size("grp") // x_size, x_size, x_size, 2


def grid_place():
    z_size, y_size, x_size, k_size = grid_sizes()
    g, c = lax.axis_index("grp"), lax.axis_index("ctx")
    return g // y_size, g % y_size, c // k_size, c % k_size


def send(values, axis, shift=None, keep=None):
    sizes = grid_sizes()
    pairs = []
    for flat in range(sizes[0] * sizes[1] * sizes[2] * sizes[3]):
        rest, spot = flat, [0, 0, 0, 0]
        for at in (3, 2, 1, 0):
            spot[at] = rest % sizes[at]
            rest //= sizes[at]
        own = spot[axis]
        other = 1 - own if shift is None else own + shift
        if 0 <= other < sizes[axis] and (keep is None or keep(own)):
            spot[axis] = other
            target = ((spot[0] * sizes[1] + spot[1]) * sizes[2] + spot[2]) * sizes[3] + spot[3]
            pairs.append((flat, target))
    return lax.ppermute(values, BOTH, pairs)


MESH = pl.DeviceIdType.MESH


def device_at(z, y, x, k):
    _, y_size, _, k_size = grid_sizes()
    return (z * y_size + y, x * k_size + k)


def order_of(y, x, turn):
    first = (y + turn * (1 - 2 * y), x + (1 - turn) * (1 - 2 * x))
    second = (y + (1 - turn) * (1 - 2 * y), x + turn * (1 - 2 * x))
    return first, second


def greet_line(z, y, x, k, z_size):
    barrier = pltpu.get_barrier_semaphore()
    for device in (device_at(z, 1 - y, x, k), device_at(z, y, 1 - x, k), device_at(z, y, x, 1 - k)):
        pl.semaphore_signal(barrier, inc=1, device_id=device, device_id_type=MESH)

    @pl.when(z > 0)
    def _():
        pl.semaphore_signal(barrier, inc=1, device_id=device_at(z - 1, y, x, k), device_id_type=MESH)

    @pl.when(z < z_size - 1)
    def _():
        pl.semaphore_signal(barrier, inc=1, device_id=device_at(z + 1, y, x, k), device_id_type=MESH)

    pl.semaphore_wait(barrier, 3 + jnp.minimum(z, 1) + jnp.minimum(z_size - 1 - z, 1))


def remote(source, target, send_sem, recv_sem, device):
    return pltpu.make_async_remote_copy(
        src_ref=source,
        dst_ref=target,
        send_sem=send_sem,
        recv_sem=recv_sem,
        device_id=device,
        device_id_type=MESH,
    )


def row_views(shapes):
    views = []
    for at, (rows, width) in enumerate(shapes):
        if rows % 32 == 0 and rows * width >= 2**16:
            views += [(at, 0, rows // 2, 0), (at, rows // 2, rows // 2, 1)]
        else:
            views.append((at, 0, rows, at % 2))
    return views


def at_offsets(z, z_size, step, body):
    if step == 0:
        body(z, True, True)
        return

    @pl.when(z >= step)
    def _():
        body(z - step, True, False)

    @pl.when(z + step < z_size)
    def _():
        body(z + step, False, True)


def greet_all(parts, me, ctx):
    barrier = pltpu.get_barrier_semaphore()

    def greet(at, carry):
        @pl.when(at != me)
        def _():
            pl.semaphore_signal(barrier, inc=1, device_id=flat_device(at, ctx), device_id_type=MESH)

        return carry

    lax.fori_loop(0, parts, greet, 0)
    pl.semaphore_wait(barrier, parts - 1)


def each_other(first, last, me, act):
    def body(at, carry):
        @pl.when(at != me)
        def _():
            act(at)

        return carry

    lax.fori_loop(first, last, body, 0)


def flat_device(at, ctx):
    return (at // ctx, at % ctx)


class Gather:
    def __init__(self, views, count, shards, outs, sems):
        self.z_size = grid_sizes()[0]
        self.place = grid_place()
        self.views, self.count, self.shards, self.outs = views, count, shards, outs
        self.local_sem, self.z_send, self.z_recv, self.p_send, self.p_recv, self.k_send, self.k_recv = sems

    def at(self, step, body):
        at_offsets(self.place[0], self.z_size, step, body)

    def spot(self, g, slot_z, at_y, at_x):
        at, first_row, rows, _ = self.views[g]
        return self.outs[at].at[slot_z, at_y, at_x, self.place[3], pl.ds(first_row, rows)]

    def source(self, g, block, own):
        at, first_row, rows, _ = self.views[g]
        return self.shards[at].at[pl.ds(first_row, rows)] if own else block

    def z_copy(self, g, slot_z, way, own=False):
        z, y, x, k = self.place
        block = self.spot(g, slot_z, y, x)
        device = device_at(z + 1 - 2 * way, y, x, k)
        return remote(self.source(g, block, own), block, self.z_send.at[g, slot_z, way], self.z_recv.at[g, slot_z], device)

    def plane_copy(self, g, slot_z, kind, own=False):
        z, y, x, k = self.place
        first, second = order_of(y, x, (self.views[g][3] + slot_z) % 2)
        from_at = first if kind == 2 else (y, x)
        to_at = first if kind == 0 else second
        block = self.spot(g, slot_z, from_at[0], from_at[1])
        device = device_at(z, to_at[0], to_at[1], k)
        source = self.source(g, block, own)
        return remote(source, block, self.p_send.at[g, slot_z, kind], self.p_recv.at[g, slot_z, kind], device)

    def core_copy(self, at, slot_z):
        z, y, x, k = self.place
        block = self.outs[at].at[slot_z, :, :, k]
        return remote(block, block, self.k_send.at[at, slot_z], self.k_recv.at[at, slot_z], device_at(z, y, x, 1 - k))

    def own_copy(self, at):
        z, y, x, k = self.place
        return pltpu.make_async_copy(self.shards[at], self.outs[at].at[z, y, x, k], self.local_sem.at[at])

    def each_way(self, g, slot_z, up, down, act):
        z, own = self.place[0], up and down
        if up:

            @pl.when(z < self.z_size - 1)
            def _():
                act(self.z_copy(g, slot_z, 0, own))

        if down:

            @pl.when(z > 0)
            def _():
                act(self.z_copy(g, slot_z, 1, own))

    def series(self, arrays):
        return [g for g, view in enumerate(self.views) if view[0] in arrays]

    def arrive(self, arrays, step):
        def body(slot_z, up, down):
            for g in self.series(arrays):
                if step > 0:
                    self.z_copy(g, slot_z, 1 if up else 0).wait_recv()
                self.each_way(g, slot_z, up, down, lambda copy: copy.start())

        self.at(step, body)

    def spread(self, arrays, step):
        def body(slot_z, up, down):
            for g in self.series(arrays):
                self.plane_copy(g, slot_z, 0, step == 0).start()
                self.plane_copy(g, slot_z, 1, step == 0).start()

        self.at(step, body)

    def pass_on(self, arrays, step):
        def body(slot_z, up, down):
            for g in self.series(arrays):
                self.plane_copy(g, slot_z, 0).wait_recv()
                self.plane_copy(g, slot_z, 2).start()

        self.at(step, body)

    def cross(self, arrays, step):
        def body(slot_z, up, down):
            for g in self.series(arrays):
                self.plane_copy(g, slot_z, 1).wait_recv()
                self.plane_copy(g, slot_z, 2).wait_recv()
            for at in arrays:
                if step == 0:
                    self.own_copy(at).wait()
                self.core_copy(at, slot_z).start()

        self.at(step, body)

    def complete(self, arrays):
        for slot_z in range(self.z_size):
            for at in arrays:
                self.core_copy(at, slot_z).wait_recv()

    def settle(self, arrays):
        def body(slot_z, up, down):
            for g in self.series(arrays):
                self.each_way(g, slot_z, up, down, lambda copy: copy.wait_send())
                for kind in range(3):
                    self.plane_copy(g, slot_z, kind).wait_send()

        for step in range(self.z_size):
            self.at(step, body)
        for slot_z in range(self.z_size):
            for at in arrays:
                self.core_copy(at, slot_z).wait_send()


def open_kernel(views, count, block_len, *refs):
    z_size, _, x_size, k_size = grid_sizes()
    z, y, x, k = grid_place()
    ctx = x_size * k_size
    parts = lax.axis_size("grp") * ctx
    me = lax.axis_index("grp") * ctx + lax.axis_index("ctx")
    target_ref, s_ref, e_ref, c_ref = refs[:4]
    shards, refs = refs[4 : 4 + count], refs[4 + count :]
    outs, refs = refs[:count], refs[count:]
    shared_out, start_ref, up_ref, joined, shared_held = refs[:5]
    gather = Gather(views, count, shards, outs, refs[5:12])
    send_sem, recv_sem, own_sem = refs[12:]
    width = s_ref.shape[1]
    count_rows = s_ref.shape[0]
    half = block_len // 2
    tiles = count_rows // TILE
    slots = TILE // block_len
    adapt, early, late = (0,), (1, 2, 3, 4, 8), (5, 6, 7)

    greet_all(parts, me, ctx)

    def half_copy(at):
        device = flat_device(at, ctx)
        return remote(shared_held.at[at], shared_out.at[me], send_sem.at[at], recv_sem.at[me], device)

    own_half = pltpu.make_async_copy(shared_held.at[me], shared_out.at[me], own_sem)

    def reorder(tile):
        rows = pl.ds(pl.multiple_of(tile * TILE, TILE), TILE)
        at_row = lax.broadcasted_iota(jnp.int32, (TILE, count_rows), 0) + tile * TILE
        order = (at_row == target_ref[...]).astype(jnp.bfloat16)
        joined[rows, :width] = dot_n(order, s_ref[...]).astype(jnp.bfloat16)
        joined[rows, width:] = dot_n(order, e_ref[...]).astype(jnp.bfloat16)
        up_ref[rows, :] = dot_n(order, c_ref[...]).astype(jnp.bfloat16)

    def apply(tile):
        rows = pl.ds(pl.multiple_of(tile * TILE, TILE), TILE)
        weight = outs[0][...].reshape(2 * width, width)
        embed_part = dot_n(joined[rows, width:], weight[width:]).astype(jnp.bfloat16)
        adapted = dot_n(joined[rows, :], weight).astype(jnp.bfloat16)
        for pair in range(slots // 2):
            at = tile * slots + 2 * pair
            even = slice(2 * pair * block_len, (2 * pair + 1) * block_len)
            odd = slice((2 * pair + 1) * block_len, (2 * pair + 2) * block_len)
            start_ref[at] = embed_part[even]
            start_ref[at + 1] = adapted[odd]
            shared_held[at] = adapted[even][:half]
            shared_held[at + 1] = adapted[even][half:]

        each_other(tile * slots, (tile + 1) * slots, me, lambda at: half_copy(at).start())

    for step in range(z_size):
        gather.arrive(adapt, step)
        gather.spread(adapt, step)
        if step == 0:
            for at in range(count):
                gather.own_copy(at).start()
        gather.arrive(early, step)
        if step < tiles:
            reorder(step)
        gather.spread(early, step)
        gather.pass_on(adapt, step)
        if step > 0:
            gather.cross(adapt, step - 1)
            gather.pass_on(early, step - 1)
        if step == z_size - 2:
            gather.arrive(late, 0)
    gather.spread(late, 0)
    gather.cross(adapt, z_size - 1)
    for tile in range(z_size, tiles):
        reorder(tile)
    gather.arrive(late, 1)
    gather.pass_on(early, z_size - 1)
    gather.spread(late, 1)
    gather.complete(adapt)
    for tile in range(tiles):
        apply(tile)
        if tile == 0:
            gather.pass_on(late, 0)
        if tile == 1:
            gather.arrive(late, 2)
            gather.spread(late, 2)
        if tile == 2:
            gather.pass_on(late, 1)
    own_half.start()
    gather.arrive(late, 3)
    gather.spread(late, 3)
    for step in range(z_size):
        gather.cross(early, step)
    gather.cross(late, 0)
    gather.pass_on(late, 2)
    gather.cross(late, 1)
    gather.pass_on(late, 3)
    gather.cross(late, 2)
    gather.cross(late, 3)
    gather.complete(early + late)
    gather.settle(adapt + early + late)

    def settle_half(at):
        device = flat_device(at, ctx)
        remote(shared_held.at[at], shared_out.at[at], send_sem.at[at], recv_sem.at[at], device).wait()

    each_other(0, parts, me, settle_half)
    own_half.wait()


def open_all(target, latents, embeds, cotangent, shards, block_len, collective_id):
    sizes = grid_sizes()
    parts = lax.axis_size("grp") * lax.axis_size("ctx")
    count, z_size = len(shards), sizes[0]
    rows, width = latents.shape
    views = row_views([shard.shape for shard in shards])
    series = len(views)
    anywhere = pl.BlockSpec(memory_space=pl.ANY)
    near = pl.BlockSpec(memory_space=pltpu.VMEM)
    dma = pltpu.SemaphoreType.DMA
    half = block_len // 2
    return pl.pallas_call(
        functools.partial(open_kernel, views, count, block_len),
        in_specs=[near] * 4 + [anywhere] * count,
        out_specs=[near] + [anywhere] * count + [near] * 2,
        out_shape=[jax.ShapeDtypeStruct(sizes + shard.shape, shard.dtype) for shard in shards]
        + [
            jax.ShapeDtypeStruct((parts, half, width), jnp.bfloat16),
            jax.ShapeDtypeStruct((parts, block_len, width), jnp.bfloat16),
            jax.ShapeDtypeStruct((rows, width), jnp.bfloat16),
        ],
        scratch_shapes=[
            pltpu.VMEM((rows, 2 * width), jnp.bfloat16),
            pltpu.VMEM((parts, half, width), jnp.bfloat16),
            dma((count,)),
            dma((series, z_size, 2)),
            dma((series, z_size)),
            dma((series, z_size, 3)),
            dma((series, z_size, 3)),
            dma((count, z_size)),
            dma((count, z_size)),
            dma((parts,)),
            dma((parts,)),
            dma,
        ],
        compiler_params=pltpu.CompilerParams(
            collective_id=collective_id, has_side_effects=True, vmem_limit_bytes=56 * 2**20
        ),
        name="open_all",
    )(target, latents, embeds, cotangent, *shards)


class Scatter:
    def __init__(self, views, parts, outs, buffers, sems):
        self.z_size = grid_sizes()[0]
        self.place = grid_place()
        self.views, self.parts, self.outs = views, parts, outs
        count = len(parts)
        self.held, self.mine, self.from_second, self.from_first, self.from_z = (
            buffers[at * count : (at + 1) * count] for at in range(5)
        )
        self.local_sem, self.k_send, self.k_recv, self.p_send, self.p_recv, self.z_send, self.z_recv = sems

    def at(self, step, body):
        if 0 <= step < self.z_size:
            at_offsets(self.place[0], self.z_size, step, body)

    def series(self, arrays):
        return [g for g, view in enumerate(self.views) if view[0] in arrays]

    def rows_of(self, g):
        return pl.ds(self.views[g][1], self.views[g][2])

    def turns(self, g, slot_z):
        return order_of(self.place[1], self.place[2], (self.views[g][3] + slot_z) % 2)

    def core_copy(self, at, slot_z):
        z, y, x, k = self.place
        return remote(
            self.parts[at].at[slot_z, :, :, 1 - k],
            self.held[at].at[slot_z],
            self.k_send.at[at, slot_z],
            self.k_recv.at[at, slot_z],
            device_at(z, y, x, 1 - k),
        )

    def own_copy(self, at, slot_z, side):
        return pltpu.make_async_copy(
            self.parts[at].at[slot_z, :, :, self.place[3]], self.mine[at].at[side], self.local_sem.at[at, side]
        )

    def second_copy(self, g, slot_z, kind):
        z, y, x, k = self.place
        at, (_, second) = self.views[g][0], self.turns(g, slot_z)
        block = second if kind == 0 else (1 - y, 1 - x)
        return remote(
            self.held[at].at[slot_z, block[0], block[1], self.rows_of(g)],
            self.from_second[at].at[slot_z, kind, self.rows_of(g)],
            self.p_send.at[g, slot_z, kind],
            self.p_recv.at[g, slot_z, kind],
            device_at(z, second[0], second[1], k),
        )

    def first_copy(self, g, slot_z):
        z, y, x, k = self.place
        at, (first, _) = self.views[g][0], self.turns(g, slot_z)
        return remote(
            self.held[at].at[slot_z, first[0], first[1], self.rows_of(g)],
            self.from_first[at].at[slot_z, self.rows_of(g)],
            self.p_send.at[g, slot_z, 2],
            self.p_recv.at[g, slot_z, 2],
            device_at(z, first[0], first[1], k),
        )

    def z_copy(self, at, slot_z, way, lands_home, here=None):
        z, y, x, k = self.place
        side = z + 1 - 2 * way if here is None else here
        buffer = self.z_size if way == 1 and lands_home else slot_z
        return remote(
            self.held[at].at[slot_z, y, x],
            self.from_z[at].at[buffer],
            self.z_send.at[at, slot_z, way],
            self.z_recv.at[at, slot_z, way],
            device_at(side, y, x, k),
        )

    def begin(self, arrays):
        def body(slot_z, below, above):
            for at in arrays:
                self.core_copy(at, slot_z).start()

        for step in range(self.z_size - 1, -1, -1):
            self.at(step, body)

    def fold_core(self, arrays, step):
        def fetch(slot_z, below, above):
            for at in arrays:
                self.own_copy(at, slot_z, 0 if below else 1).start()

        def body(slot_z, below, above):
            _, y, x, _ = self.place
            side = 0 if below else 1
            for at in arrays:
                self.own_copy(at, slot_z, side).wait()
                self.core_copy(at, slot_z).wait_recv()
            for g in self.series(arrays):
                at, rows = self.views[g][0], self.rows_of(g)
                held, mine = self.held[at], self.mine[at]
                first, second = self.turns(g, slot_z)
                for spot in (second, (1 - y, 1 - x)):
                    here = (slot_z, spot[0], spot[1], rows)
                    held[here] = held[here] + mine[(side,) + here[1:]]
                self.second_copy(g, slot_z, 0).start()
                self.second_copy(g, slot_z, 1).start()
                for spot in (first, (y, x)):
                    here = (slot_z, spot[0], spot[1], rows)
                    held[here] = held[here] + mine[(side,) + here[1:]]

        self.at(step, fetch)
        self.at(step, body)

    def fold_second(self, arrays, step):
        def body(slot_z, below, above):
            for g in self.series(arrays):
                at, rows = self.views[g][0], self.rows_of(g)
                held, come = self.held[at], self.from_second[at]
                first, _ = self.turns(g, slot_z)
                self.second_copy(g, slot_z, 1).wait_recv()
                here = (slot_z, first[0], first[1], rows)
                held[here] = held[here] + come[slot_z, 1, rows]
                self.first_copy(g, slot_z).start()

        self.at(step, body)

    def fold_first(self, arrays, step):
        z, y, x, _ = self.place
        home = step == 0

        def body(slot_z, below, above):
            for g in self.series(arrays):
                at, rows = self.views[g][0], self.rows_of(g)
                held = self.held[at]
                here = (slot_z, y, x, rows)
                self.second_copy(g, slot_z, 0).wait_recv()
                self.first_copy(g, slot_z).wait_recv()
                held[here] = held[here] + self.from_second[at][slot_z, 0, rows] + self.from_first[at][slot_z, rows]
            if home:
                for at in arrays:
                    self.outs[at][...] = self.held[at][slot_z, y, x].astype(jnp.float32)
            for way, use in ((0, above), (1, below)):
                if not use:
                    continue
                came, source = (z > 0, z - 1) if way == 0 else (z < self.z_size - 1, z + 1)

                @pl.when(came)
                def _(way=way, source=source):
                    for at in arrays:
                        self.z_copy(at, slot_z, way, home, source).wait_recv()
                        come = self.from_z[at][self.z_size if way == 1 and home else slot_z]
                        if home:
                            self.outs[at][...] += come.astype(jnp.float32)
                        else:
                            self.held[at][slot_z, y, x] = self.held[at][slot_z, y, x] + come

                if not home:
                    for at in arrays:
                        self.z_copy(at, slot_z, way, step == 1).start()

        self.at(step, body)

    def settle(self, arrays):
        for step in range(self.z_size):

            def body(slot_z, below, above, step=step):
                for at in arrays:
                    self.core_copy(at, slot_z).wait_send()
                    if step > 0:
                        self.z_copy(at, slot_z, 0 if above else 1, step == 1).wait_send()
                for g in self.series(arrays):
                    self.second_copy(g, slot_z, 0).wait_send()
                    self.second_copy(g, slot_z, 1).wait_send()
                    self.first_copy(g, slot_z).wait_send()

            self.at(step, body)

    def stage(self, arrays, number):
        far = self.z_size - 1
        self.fold_core(arrays, far - number)
        self.fold_second(arrays, far - number + 1)
        self.fold_first(arrays, far - number + 2)

    def stages(self):
        return self.z_size + 2


def scatter_scratch(shapes):
    z_size, y_size, x_size, _ = grid_sizes()
    count, series = len(shapes), len(row_views(shapes))
    leads = ((z_size, y_size, x_size), (2, y_size, x_size), (z_size, 2), (z_size,), (z_size + 1,))
    dma = pltpu.SemaphoreType.DMA
    return [pltpu.VMEM(lead + shape, jnp.bfloat16) for lead in leads for shape in shapes] + [
        dma((count, 2)),
        dma((count, z_size)),
        dma((count, z_size)),
        dma((series, z_size, 3)),
        dma((series, z_size, 3)),
        dma((count, z_size, 2)),
        dma((count, z_size, 2)),
    ]


def dot_t(left, right):
    return lax.dot_general(left, right, (((1,), (1,)), ((), ())), preferred_element_type=jnp.float32)


def dot_n(left, right):
    return jnp.dot(left, right, preferred_element_type=jnp.float32)


def dot_w(left, right):
    return lax.dot_general(left, right, (((0,), (0,)), ((), ())), preferred_element_type=jnp.float32)


def below(rows, columns):
    at_row = lax.broadcasted_iota(jnp.int32, (rows, columns), 0)
    at_column = lax.broadcasted_iota(jnp.int32, (rows, columns), 1)
    return at_column <= at_row


def whole_attend(q_ref, k_ref, v_ref, o_ref, log_ref):
    head = pl.program_id(0)
    length = q_ref.shape[0]
    lane = lax.broadcasted_iota(jnp.int32, (TILE, 128), 1)
    for at in range(length // TILE):
        rows = pl.ds(at * TILE, TILE)
        seen = (at + 1) * TILE
        raw = dot_t(q_ref[rows, :], k_ref[:seen, :]) * (SCALE * LOG2E)
        last = jnp.where(below(TILE, TILE), raw[:, at * TILE :], NEG)
        raw = jnp.concatenate([raw[:, : at * TILE], last], 1) if at else last
        top = jnp.max(raw, 1, keepdims=True)
        weight = jnp.exp2(raw - top)
        total = jnp.sum(weight, 1, keepdims=True)
        mixed = dot_n(weight.astype(jnp.bfloat16), v_ref[:seen, :])
        o_ref[rows, :] = (mixed / total).astype(o_ref.dtype)
        log_total = top + jnp.log2(total)
        log_ref[rows, :] = jnp.where(lane == head, log_total, log_ref[rows, :])


def attend_whole(queries, keys_in, values_in):
    length, width = queries.shape
    head_block = pl.BlockSpec((length, HEAD_DIM), lambda h: (0, h))
    return pl.pallas_call(
        whole_attend,
        grid=(width // HEAD_DIM,),
        in_specs=[head_block] * 3,
        out_specs=[head_block, pl.BlockSpec((length, 128), lambda h: (0, 0))],
        out_shape=[
            jax.ShapeDtypeStruct((length, width), jnp.bfloat16),
            jax.ShapeDtypeStruct((length, 128), jnp.float32),
        ],
        compiler_params=pltpu.CompilerParams(vmem_limit_bytes=60 * 2**20),
        cost_estimate=pl.CostEstimate(
            flops=2 * length * length * width, bytes_accessed=8 * length * width, transcendentals=0
        ),
        name="attend_whole",
    )(queries, keys_in, values_in)


def shared_attend(block_len, core_ref, q_ref, k_ref, v_ref, ok_ref, ov_ref, o_ref):
    core = core_ref[0]
    length = q_ref.shape[0]
    for at in range(length // TILE):
        rows = pl.ds(at * TILE, TILE)
        seen = (at + 1) * TILE
        queries = q_ref[rows, :]
        raw = dot_t(queries, k_ref[:seen, :]) * (SCALE * LOG2E)
        far = dot_t(queries, ok_ref[:seen, :]) * (SCALE * LOG2E)
        at_row = lax.broadcasted_iota(jnp.int32, (TILE, TILE), 0)
        at_column = lax.broadcasted_iota(jnp.int32, (TILE, TILE), 1)
        near_last = jnp.where(at_column <= at_row, raw[:, at * TILE :], NEG)
        far_ok = at_column // block_len < at_row // block_len + core
        far_last = jnp.where(far_ok, far[:, at * TILE :], NEG)
        raw = jnp.concatenate([raw[:, : at * TILE], near_last], 1) if at else near_last
        far = jnp.concatenate([far[:, : at * TILE], far_last], 1) if at else far_last
        top = jnp.maximum(jnp.max(raw, 1, keepdims=True), jnp.max(far, 1, keepdims=True))
        weight = jnp.exp2(raw - top)
        far_weight = jnp.exp2(far - top)
        total = jnp.sum(weight, 1, keepdims=True) + jnp.sum(far_weight, 1, keepdims=True)
        mixed = dot_n(weight.astype(jnp.bfloat16), v_ref[:seen, :])
        mixed = mixed + dot_n(far_weight.astype(jnp.bfloat16), ov_ref[:seen, :])
        o_ref[rows, :] = (mixed / total).astype(o_ref.dtype)


def attend_shared(core, block_len, queries, keys_in, values_in, far_keys, far_values):
    length, width = queries.shape
    head_block = pl.BlockSpec((length, HEAD_DIM), lambda h: (0, h))
    return pl.pallas_call(
        functools.partial(shared_attend, block_len),
        grid=(width // HEAD_DIM,),
        in_specs=[pl.BlockSpec(memory_space=pltpu.SMEM)] + [head_block] * 5,
        out_specs=head_block,
        out_shape=jax.ShapeDtypeStruct((length, width), jnp.bfloat16),
        compiler_params=pltpu.CompilerParams(vmem_limit_bytes=60 * 2**20),
        cost_estimate=pl.CostEstimate(
            flops=4 * length * length * width, bytes_accessed=12 * length * width, transcendentals=0
        ),
        name="attend_shared",
    )(core.reshape(1), queries, keys_in, values_in, far_keys, far_values)


def middle_plan(z_size, total):
    last = total - 1
    places = {
        "fold_core": [1 + 2 * at for at in range(z_size)],
        "fold_second": ([6, 9, 12, 20] + [last] * z_size)[:z_size],
        "fold_first": ([12, 20] + [last] * z_size)[:z_size],
    }
    plan = {}
    for number in range(z_size + 2):
        for delay, act in enumerate(places):
            if 0 <= number - delay < z_size:
                at = min(places[act][number - delay], last)
                plan.setdefault(at, []).append((act, z_size - 1 - number + delay))
    return plan


def middle_kernel(
    shapes,
    heads,
    q_ref,
    k_ref,
    v_ref,
    o_ref,
    do_ref,
    log_ref,
    cos_ref,
    sin_ref,
    r_ref,
    dmid_ref,
    gain_ref,
    wq_ref,
    wk_ref,
    wv_ref,
    normed_ref,
    mixed_ref,
    first_ref,
    db_ref,
    *refs,
):
    count = len(shapes)
    parts, refs = refs[:count], refs[count:]
    home_out, gains_ref, grad_ref = refs[:3]
    outs, refs = refs[3 : 3 + count], refs[3 + count :]
    dq_all, dk_all, dv_all, dr_ref, dk_sum, dv_sum = refs[:6]
    sems, (send_sem, recv_sem, own_sem) = refs[6 + 5 * count : -3], refs[-3:]
    scatter = Scatter(row_views(shapes), parts, outs, refs[6 : 6 + 5 * count], sems)
    arrays = tuple(range(count))
    step = pl.program_id(0)
    ctx = lax.axis_size("ctx")
    devices = lax.axis_size("grp") * ctx
    me = lax.axis_index("grp") * ctx + lax.axis_index("ctx")
    block_len = dr_ref.shape[0] // devices
    near_home = TILE // block_len

    def home_copy(at):
        rows = pl.ds(pl.multiple_of(at * block_len, block_len), block_len)
        device = flat_device(at, ctx)
        return remote(dr_ref.at[rows], home_out.at[me], send_sem.at[at], recv_sem.at[me], device)

    def own_home():
        rows = pl.ds(pl.multiple_of(me * block_len, block_len), block_len)
        return pltpu.make_async_copy(dr_ref.at[rows], home_out.at[me], own_sem)

    def settle_home(at):
        rows = pl.ds(pl.multiple_of(at * block_len, block_len), block_len)
        device = flat_device(at, ctx)
        remote(dr_ref.at[rows], home_out.at[at], send_sem.at[at], recv_sem.at[at], device).wait()
    length = q_ref.shape[0]
    tiles = length // TILE
    rest = heads + tiles
    total = rest + 5 * tiles

    @pl.when(step == 0)
    def _():
        greet_all(devices, me, ctx)
        scatter.begin(arrays)
        gains_ref[...] = jnp.zeros_like(gains_ref)

    for at_step, acts in middle_plan(scatter.z_size, total).items():

        @pl.when(step == at_step)
        def _(acts=acts):
            for act, layer in acts:
                getattr(scatter, act)(arrays, layer)

    @pl.when(step < heads)
    def _():
        head = step
        columns = pl.ds(pl.multiple_of(head * HEAD_DIM, HEAD_DIM), HEAD_DIM)
        lane = lax.broadcasted_iota(jnp.int32, (TILE, 128), 1)

        def unrotated(grads, rows):
            turned = pltpu.roll(grads, HEAD_DIM // 2, 1)
            return grads * cos_ref[rows, :] - turned * sin_ref[rows, :]

        for at in range(tiles):
            rows = pl.ds(at * TILE, TILE)
            seen = (at + 1) * TILE
            queries, d_mixed = q_ref[rows, :], do_ref[rows, :]
            log_total = jnp.sum(jnp.where(lane == head, log_ref[rows, :], 0.0), 1, keepdims=True)
            delta = jnp.sum(d_mixed.astype(jnp.float32) * o_ref[rows, :].astype(jnp.float32), 1, keepdims=True)
            raw = dot_t(queries, k_ref[:seen, :]) * (SCALE * LOG2E)
            last = jnp.where(below(TILE, TILE), raw[:, at * TILE :], NEG)
            raw = jnp.concatenate([raw[:, : at * TILE], last], 1) if at else last
            probs = jnp.exp2(raw - log_total)
            d_probs = dot_t(d_mixed, v_ref[:seen, :])
            slopes = (probs * (d_probs - delta)).astype(jnp.bfloat16)
            d_query = dot_n(slopes, k_ref[:seen, :]) * SCALE
            dq_all[rows, columns] = unrotated(d_query, rows).astype(dq_all.dtype)
            d_value = dot_w(probs.astype(jnp.bfloat16), d_mixed)
            d_key = dot_w(slopes, queries)
            if at:
                before = pl.ds(0, at * TILE)
                dv_sum[before, :] += d_value[: at * TILE]
                dk_sum[before, :] += d_key[: at * TILE]
            dv_sum[rows, :] = d_value[at * TILE :]
            dk_sum[rows, :] = d_key[at * TILE :]
        dk_all[:, columns] = unrotated(dk_sum[...] * SCALE, pl.ds(0, length)).astype(dk_all.dtype)
        dv_all[:, columns] = dv_sum[...].astype(dv_all.dtype)

    @pl.when((step >= heads) & (step < rest))
    def _():
        rows = pl.ds(pl.multiple_of((step - heads) * TILE, TILE), TILE)
        d_normed = (
            dot_t(dq_all[rows, :], wq_ref[...])
            + dot_t(dk_all[rows, :], wk_ref[...])
            + dot_t(dv_all[rows, :], wv_ref[...])
        )
        d_resid, gain_one = pull_norm(r_ref[...], d_normed, gain_ref[0:1, :])
        dr_ref[rows, :] = (d_resid + dmid_ref[...]).astype(jnp.bfloat16)
        gains_ref[0:1, :] += gain_one
        first = (step - heads) * near_home
        each_other(first, first + near_home, me, lambda at: home_copy(at).start())

    pairs = (
        (normed_ref, dq_all),
        (normed_ref, dk_all),
        (normed_ref, dv_all),
        (mixed_ref, db_ref),
        (first_ref, dr_ref),
    )
    for at, (left, right) in enumerate(pairs):

        @pl.when((step >= rest + at * tiles) & (step < rest + (at + 1) * tiles))
        def _(left=left, right=right):
            grad_ref[...] = dot_w(left[...], right[...]).astype(grad_ref.dtype)

    @pl.when(step == rest)
    def _():
        own_home().start()

    @pl.when(step == total - 1)
    def _():
        scatter.settle(arrays)
        each_other(0, devices, me, settle_home)
        own_home().wait()


def middle_all(
    queries,
    keys_in,
    values_in,
    mixed,
    d_mixed,
    log_total,
    cos_full,
    sin_full,
    resid,
    d_middle,
    gain_float,
    query_w,
    key_w,
    value_w,
    normed,
    first_out,
    d_branch,
    sums,
    collective_id,
):
    sizes = grid_sizes()
    length, width = queries.shape
    heads, tiles = width // HEAD_DIM, length // TILE
    rest = heads + tiles
    shapes = [part.shape[1:] for part in sums]
    head_block = pl.BlockSpec((length, HEAD_DIM), lambda i: (0, jnp.minimum(i, heads - 1)))
    tall_block = pl.BlockSpec((TILE, width), lambda i: (jnp.clip(i - heads, 0, tiles - 1), 0))

    def left_block(first, repeats=1):
        def place(i):
            inside = jnp.clip(i - rest - first * tiles, 0, repeats * tiles - 1)
            return (0, inside % tiles)

        return pl.BlockSpec((length, TILE), place)

    fixed = pl.BlockSpec((length, 128), lambda i: (0, 0), pipeline_mode=pl.Buffered(1))
    anywhere = pl.BlockSpec(memory_space=pl.ANY)
    near = pl.BlockSpec(memory_space=pltpu.VMEM)
    once = pl.Buffered(1)
    weights = sum(shape[0] * shape[1] for shape in shapes)
    devices = lax.axis_size("grp") * lax.axis_size("ctx")
    dma = pltpu.SemaphoreType.DMA
    return pl.pallas_call(
        functools.partial(middle_kernel, shapes, heads),
        grid=(rest + 5 * tiles,),
        in_specs=[head_block] * 5
        + [fixed] * 3
        + [tall_block] * 2
        + [whole_block(a) for a in (gain_float, query_w, key_w, value_w)]
        + [left_block(0, 3), left_block(3), left_block(4)]
        + [whole_block(d_branch)]
        + [anywhere] * len(sums),
        out_specs=[
            anywhere,
            pl.BlockSpec((8, width), lambda i: (0, 0), pipeline_mode=once),
            pl.BlockSpec((TILE, width), lambda i: (jnp.clip(i - rest, 0, 5 * tiles - 1), 0)),
        ]
        + [near] * len(sums),
        out_shape=[
            jax.ShapeDtypeStruct((devices, length // devices, width), jnp.bfloat16),
            jax.ShapeDtypeStruct((8, width), jnp.float32),
            jax.ShapeDtypeStruct((5 * width, width), jnp.bfloat16),
        ]
        + [jax.ShapeDtypeStruct(shape, jnp.float32) for shape in shapes],
        scratch_shapes=[pltpu.VMEM((length, width), jnp.bfloat16)] * 4
        + [pltpu.VMEM((length, HEAD_DIM), jnp.float32)] * 2
        + scatter_scratch(shapes)
        + [dma((devices,)), dma((devices,)), dma],
        compiler_params=pltpu.CompilerParams(
            collective_id=collective_id, has_side_effects=True, vmem_limit_bytes=62 * 2**20
        ),
        cost_estimate=cost(24 * length * width * width, 64 * length * width + 64 * weights),
        name="middle_all",
    )(
        queries,
        keys_in,
        values_in,
        mixed,
        d_mixed,
        log_total,
        cos_full,
        sin_full,
        resid,
        d_middle,
        gain_float,
        query_w,
        key_w,
        value_w,
        normed,
        mixed,
        first_out,
        d_branch,
        *(part.reshape(sizes + part.shape[1:]) for part in sums),
    )


def rope_full(length):
    freq = np.float32(10000.0) ** (np.float32(-2.0 / HEAD_DIM) * np.arange(HEAD_DIM // 2, dtype=np.float32))
    angle = np.arange(length, dtype=np.float32)[:, None] * freq
    cosine, sine = np.cos(angle).astype(np.float32), np.sin(angle).astype(np.float32)
    return jnp.asarray(np.concatenate([cosine, cosine], 1)), jnp.asarray(np.concatenate([-sine, sine], 1))


def whole_block(array):
    return pl.BlockSpec(array.shape, lambda *_: (0,) * array.ndim, pipeline_mode=pl.Buffered(1))


def row_block(rows, width):
    return pl.BlockSpec((rows, width), lambda i: (i, 0))


def compute_params(megabytes=58):
    return pltpu.CompilerParams(vmem_limit_bytes=megabytes * 2**20)


def cost(flops, nbytes):
    return pl.CostEstimate(flops=int(flops), bytes_accessed=int(nbytes), transcendentals=0)


def unit_rows(values):
    scale_rows = rms_scale(values)
    return scale_rows, values * scale_rows


def pull_norm(values, upstream, gain_row):
    scale_rows, normal = unit_rows(values)
    gain_part = jnp.sum(upstream * normal, 0, keepdims=True)
    scaled = upstream * gain_row
    return scale_rows * (scaled - normal * jnp.mean(scaled * normal, -1, keepdims=True)), gain_part


def turned_heads(values, cos, sin):
    parts = []
    for head in range(values.shape[1] // HEAD_DIM):
        one = values[:, head * HEAD_DIM : (head + 1) * HEAD_DIM]
        parts.append(one * cos + pltpu.roll(one, HEAD_DIM // 2, 1) * sin)
    return jnp.concatenate(parts, 1)


COLUMNS = 256


def column_block(rows, column=COLUMNS):
    return pl.BlockSpec((rows, column), lambda i: (0, i))


def write_heads(step_normed, wq_ref, wk_ref, wv_ref, cos, sin, q_ref, k_ref, v_ref):
    normed = step_normed[...]
    q_ref[...] = turned_heads(dot_n(normed, wq_ref[...]), cos, sin).astype(jnp.bfloat16)
    k_ref[...] = turned_heads(dot_n(normed, wk_ref[...]), cos, sin).astype(jnp.bfloat16)
    v_ref[...] = dot_n(normed, wv_ref[...]).astype(jnp.bfloat16)


def first_heads_kernel(
    r_ref, gain_ref, cos_ref, sin_ref, wq_ref, wk_ref, wv_ref, q_ref, k_ref, v_ref, normed_sc
):
    @pl.when(pl.program_id(0) == 0)
    def _():
        resid = r_ref[...].astype(jnp.float32)
        normed_sc[...] = (unit_rows(resid)[1] * gain_ref[0:1, :]).astype(jnp.bfloat16)

    core = lax.axis_index("ctx") % cos_ref.shape[1]
    cos, sin = (table[:, core].reshape(-1, HEAD_DIM) for table in (cos_ref, sin_ref))
    write_heads(normed_sc, wq_ref, wk_ref, wv_ref, cos, sin, q_ref, k_ref, v_ref)


def first_heads(resid, gain_float, query_w, key_w, value_w, cos, sin):
    rows, width = resid.shape
    return pl.pallas_call(
        first_heads_kernel,
        grid=(width // COLUMNS,),
        in_specs=[whole_block(a) for a in (resid, gain_float, cos, sin)] + [column_block(width)] * 3,
        out_specs=[column_block(rows)] * 3,
        out_shape=[jax.ShapeDtypeStruct((rows, width), jnp.bfloat16)] * 3,
        scratch_shapes=[pltpu.VMEM((rows, width), jnp.bfloat16)],
        compiler_params=compute_params(),
        cost_estimate=cost(6 * rows * width * width, 8 * rows * width + 6 * width * width),
        name="first_heads",
    )(resid, gain_float, cos, sin, query_w, key_w, value_w)


def last_heads_kernel(
    start_ref,
    near_ref,
    far_ref,
    wa_ref,
    gain_ref,
    cos_ref,
    sin_ref,
    wq_ref,
    wk_ref,
    wv_ref,
    r_ref,
    n_ref,
    first_ref,
    q_ref,
    k_ref,
    v_ref,
):
    @pl.when(pl.program_id(0) == 0)
    def _():
        owner = lax.axis_index("ctx") % 2 == 0
        blocks, half, width = near_ref.shape
        both = jnp.concatenate([near_ref[...], far_ref[...]], 1).reshape(2 * blocks * half, width)
        first_ref[...] = jnp.where(owner, both, jnp.zeros_like(both))
        resid = start_ref[...].astype(jnp.float32) + dot_n(first_ref[...], wa_ref[...])
        r_ref[...] = resid
        n_ref[...] = (unit_rows(resid)[1] * gain_ref[0:1, :]).astype(jnp.bfloat16)

    write_heads(n_ref, wq_ref, wk_ref, wv_ref, cos_ref[...], sin_ref[...], q_ref, k_ref, v_ref)


def last_heads(starting, near_out, far_out, adapt_w, gain_float, query_w, key_w, value_w, cos, sin):
    rows, width = starting.shape
    upper = pl.BlockSpec((width, width), lambda i: (0, 0), pipeline_mode=pl.Buffered(1))
    like = jax.ShapeDtypeStruct((rows, width), jnp.bfloat16)
    tall = jax.ShapeDtypeStruct((rows, width), jnp.float32)
    return pl.pallas_call(
        last_heads_kernel,
        grid=(width // COLUMNS,),
        in_specs=[whole_block(a) for a in (starting, near_out, far_out)]
        + [upper]
        + [whole_block(a) for a in (gain_float, cos, sin)]
        + [column_block(width)] * 3,
        out_specs=[whole_block(tall)] + [whole_block(like)] * 2 + [column_block(rows)] * 3,
        out_shape=[tall] + [like] * 5,
        compiler_params=compute_params(),
        cost_estimate=cost(8 * rows * width * width, 16 * rows * width + 8 * width * width),
        name="last_heads",
    )(starting, near_out, far_out, adapt_w, gain_float, cos, sin, query_w, key_w, value_w)


def first_rows_kernel(
    r_ref, mixed_ref, gain_ref, wo_ref, wg_ref, wu_ref, wd_ref, out_ref, middle_sc, mlp_sc, total_sc
):
    step = pl.program_id(0)

    @pl.when(step == 0)
    def _():
        branch = dot_n(mixed_ref[...], wo_ref[...])
        middle = r_ref[...].astype(jnp.float32) + unit_rows(branch)[1] * gain_ref[1:2, :]
        middle_sc[...] = middle
        mlp_sc[...] = (unit_rows(middle)[1] * gain_ref[2:3, :]).astype(jnp.bfloat16)
        total_sc[...] = jnp.zeros_like(total_sc)

    mlp_in = mlp_sc[...]
    gate_pre = dot_n(mlp_in, wg_ref[...])
    up_pre = dot_n(mlp_in, wu_ref[...])
    hidden = (gate_pre / (1.0 + jnp.exp(-gate_pre)) * up_pre).astype(jnp.bfloat16)
    total_sc[...] += dot_n(hidden, wd_ref[...])

    @pl.when(step == pl.num_programs(0) - 1)
    def _():
        out_ref[...] = (middle_sc[...] + unit_rows(total_sc[...])[1] * gain_ref[3:4, :]).astype(jnp.bfloat16)


def first_rows(resid, mixed, gain_float, output_w, gate_w, up_w, down_w):
    rows, width = resid.shape
    inner = gate_w.shape[1]
    like = jax.ShapeDtypeStruct((rows, width), jnp.bfloat16)
    weights = output_w.size + 3 * gate_w.size
    return pl.pallas_call(
        first_rows_kernel,
        grid=(inner // COLUMNS,),
        in_specs=[whole_block(a) for a in (resid, mixed, gain_float, output_w)]
        + [column_block(width)] * 2
        + [row_block(COLUMNS, width)],
        out_specs=whole_block(like),
        out_shape=like,
        scratch_shapes=[
            pltpu.VMEM((rows, width), jnp.float32),
            pltpu.VMEM((rows, width), jnp.bfloat16),
            pltpu.VMEM((rows, width), jnp.float32),
        ],
        compiler_params=compute_params(),
        cost_estimate=cost(2 * rows * weights, 6 * rows * width + 2 * weights),
        name="first_rows",
    )(resid, mixed, gain_float, output_w, gate_w, up_w, down_w)


def last_rows_kernel(
    r_ref,
    mixed_ref,
    gain_ref,
    wo_ref,
    wg_ref,
    wu_ref,
    wd_ref,
    out_ref,
    branch_ref,
    middle_ref,
    mlp_ref,
    down_ref,
    gate_ref,
    up_ref,
    hidden_ref,
):
    step = pl.program_id(0)

    @pl.when(step == 0)
    def _():
        branch = dot_n(mixed_ref[...], wo_ref[...])
        branch_ref[...] = branch
        middle = r_ref[...] + unit_rows(branch)[1] * gain_ref[1:2, :]
        middle_ref[...] = middle
        mlp_ref[...] = (unit_rows(middle)[1] * gain_ref[2:3, :]).astype(jnp.bfloat16)
        down_ref[...] = jnp.zeros_like(down_ref)

    mlp_in = mlp_ref[...]
    gate_pre = dot_n(mlp_in, wg_ref[...])
    up_pre = dot_n(mlp_in, wu_ref[...])
    hidden = (gate_pre / (1.0 + jnp.exp(-gate_pre)) * up_pre).astype(jnp.bfloat16)
    gate_ref[...] = gate_pre.astype(jnp.bfloat16)
    up_ref[...] = up_pre.astype(jnp.bfloat16)
    hidden_ref[...] = hidden
    down_ref[...] += dot_n(hidden, wd_ref[...])

    @pl.when(step == pl.num_programs(0) - 1)
    def _():
        out_ref[...] = (middle_ref[...] + unit_rows(down_ref[...])[1] * gain_ref[3:4, :]).astype(jnp.bfloat16)


def last_rows(resid, mixed, gain_float, output_w, gate_w, up_w, down_w):
    rows, width = resid.shape
    inner = gate_w.shape[1]
    narrow, wide = (jax.ShapeDtypeStruct((rows, w), jnp.bfloat16) for w in (width, inner))
    tall = jax.ShapeDtypeStruct((rows, width), jnp.float32)
    weights = output_w.size + 3 * gate_w.size
    whole = [narrow, tall, tall, narrow, tall]
    return pl.pallas_call(
        last_rows_kernel,
        grid=(inner // COLUMNS,),
        in_specs=[whole_block(a) for a in (resid, mixed, gain_float, output_w)]
        + [column_block(width)] * 2
        + [row_block(COLUMNS, width)],
        out_specs=[whole_block(one) for one in whole] + [column_block(rows)] * 3,
        out_shape=whole + [wide] * 3,
        compiler_params=compute_params(),
        cost_estimate=cost(2 * rows * weights, 22 * rows * width + 6 * rows * inner + 2 * weights),
        name="last_rows",
    )(resid, mixed, gain_float, output_w, gate_w, up_w, down_w)


def back_rows_kernel(
    down_ref,
    slope_ref,
    middle_ref,
    branch_ref,
    mlp_ref,
    gain_ref,
    wo_ref,
    wg_ref,
    wu_ref,
    wd_ref,
    gate_ref,
    up_ref,
    hidden_ref,
    dmid_ref,
    db_ref,
    dmix_ref,
    gains_ref,
    dwg_ref,
    dwu_ref,
    dwd_ref,
    dd_sc,
    total_sc,
):
    step = pl.program_id(0)

    @pl.when(step == 0)
    def _():
        gains_ref[...] = jnp.zeros_like(gains_ref)
        d_down, gain_four = pull_norm(down_ref[...], slope_ref[...].astype(jnp.float32), gain_ref[3:4, :])
        gains_ref[2:3, :] = gain_four
        dd_sc[...] = d_down.astype(jnp.bfloat16)
        total_sc[...] = jnp.zeros_like(total_sc)

    d_down, mlp_in = dd_sc[...], mlp_ref[...]
    d_hidden = dot_t(d_down, wd_ref[...])
    gate_pre, up_pre = gate_ref[...].astype(jnp.float32), up_ref[...].astype(jnp.float32)
    sigma = 1.0 / (1.0 + jnp.exp(-gate_pre))
    d_gate = (d_hidden * up_pre * sigma * (1.0 + gate_pre * (1.0 - sigma))).astype(jnp.bfloat16)
    d_up = (d_hidden * gate_pre * sigma).astype(jnp.bfloat16)
    dwd_ref[...] = dot_w(hidden_ref[...], d_down).astype(jnp.bfloat16)
    dwg_ref[...] = dot_w(mlp_in, d_gate).astype(jnp.bfloat16)
    dwu_ref[...] = dot_w(mlp_in, d_up).astype(jnp.bfloat16)
    total_sc[...] += dot_t(jnp.concatenate([d_gate, d_up], 1), jnp.concatenate([wg_ref[...], wu_ref[...]], 1))

    @pl.when(step == pl.num_programs(0) - 1)
    def _():
        d_middle, gain_three = pull_norm(middle_ref[...], total_sc[...], gain_ref[2:3, :])
        gains_ref[1:2, :] = gain_three
        d_middle = d_middle + slope_ref[...].astype(jnp.float32)
        dmid_ref[...] = d_middle
        d_branch, gain_two = pull_norm(branch_ref[...], d_middle, gain_ref[1:2, :])
        gains_ref[0:1, :] = gain_two
        d_branch = d_branch.astype(jnp.bfloat16)
        db_ref[...] = d_branch
        dmix_ref[...] = dot_t(d_branch, wo_ref[...]).astype(jnp.bfloat16)


def back_rows(down_out, upstream, middle, branch, mlp_in, gain_float, output_w, gate_w, up_w, down_w, gate_pre, up_pre, hidden):
    rows, width = middle.shape
    inner = gate_w.shape[1]
    narrow = jax.ShapeDtypeStruct((rows, width), jnp.bfloat16)
    tall = jax.ShapeDtypeStruct((rows, width), jnp.float32)
    gains = jax.ShapeDtypeStruct((8, width), jnp.float32)
    wide = jax.ShapeDtypeStruct(gate_w.shape, jnp.bfloat16)
    whole = [tall, narrow, narrow, gains]
    fixed = (down_out, upstream, middle, branch, mlp_in, gain_float, output_w)
    return pl.pallas_call(
        back_rows_kernel,
        grid=(inner // COLUMNS,),
        in_specs=[whole_block(a) for a in fixed]
        + [column_block(width)] * 2
        + [row_block(COLUMNS, width)]
        + [column_block(rows)] * 3,
        out_specs=[whole_block(one) for one in whole] + [column_block(width)] * 2 + [row_block(COLUMNS, width)],
        out_shape=whole + [wide, wide, jax.ShapeDtypeStruct(down_w.shape, jnp.bfloat16)],
        scratch_shapes=[pltpu.VMEM((rows, width), jnp.bfloat16), pltpu.VMEM((rows, width), jnp.float32)],
        compiler_params=compute_params(),
        cost_estimate=cost(12 * rows * gate_w.size, 24 * rows * width + 6 * rows * inner + 12 * gate_w.size),
        name="back_rows",
    )(*fixed, gate_w, up_w, down_w, gate_pre, up_pre, hidden)


def close_kernel(target_ref, final_ref, w_ref, s_ref, e_ref, home, grad_ref, gain_ref, *refs):
    final_out, ds_ref, de_ref = refs[:3]
    outs, refs = refs[3:9], refs[9:]
    first, total, adapt_part, *refs = refs
    buffers, sems, own_sem = refs[:30], refs[30:37], refs[37]
    parts = [grad_ref.at[at] for at in range(4)] + [adapt_part, gain_ref]
    scatter = Scatter(row_views([out.shape for out in outs]), parts, outs, buffers, sems)
    early, late = (0, 1, 2, 3, 5), (4,)
    count, width = ds_ref.shape
    tiles = count // TILE

    greet_line(*scatter.place, scatter.z_size)
    scatter.begin(early)
    own_first = pltpu.make_async_copy(grad_ref.at[4], first, own_sem)
    own_first.start()

    def order_rows(tile):
        rows = pl.ds(tile * TILE, TILE)
        at_row = lax.broadcasted_iota(jnp.int32, (count, TILE), 0)
        return rows, (at_row == target_ref[:, rows]).astype(jnp.bfloat16)

    def at_home(tile):
        rows, order = order_rows(tile)
        d_home = dot_w(order, home[...].reshape(count, width)).astype(jnp.bfloat16)
        ds_ref[rows, :] = dot_t(d_home, w_ref[:width, :]).astype(jnp.bfloat16)
        de_ref[rows, :] = dot_t(d_home, w_ref[width:, :]).astype(jnp.bfloat16)
        upper, lower = dot_w(s_ref[rows, :], d_home), dot_w(e_ref[rows, :], d_home)
        if tile == 0:
            own_first.wait()
            total[:width, :] = upper + first[...].reshape(width, width).astype(jnp.float32)
            total[width:, :] = lower
        else:
            total[:width, :] += upper
            total[width:, :] += lower

    for tile in range(tiles):
        at_home(tile)
        if tile < scatter.z_size:
            scatter.stage(early, tile)
    adapt_part[...] = total[...].reshape(adapt_part.shape).astype(adapt_part.dtype)
    scatter.begin(late)
    for number in range(scatter.stages()):
        if number >= tiles:
            scatter.stage(early, number)
        scatter.stage(late, number)
        if number < tiles:
            rows, order = order_rows(number)
            final_out[rows, :] = dot_w(order, final_ref[...]).astype(jnp.bfloat16)
    scatter.settle(early)
    scatter.settle(late)


def close_all(
    target, final_slots, adapt_w, once, embeds, d_home, weight_parts, gain_part, collective_id
):
    sizes = grid_sizes()
    parts = lax.axis_size("grp") * lax.axis_size("ctx")
    count, width = embeds.shape
    side = width // parts
    square = weight_parts.reshape((5,) + sizes + (side, width))
    gain = gain_part.reshape(sizes + gain_part.shape[1:])
    shapes = [(side, width)] * 4 + [(2 * side, width), gain_part.shape[1:]]
    anywhere = pl.BlockSpec(memory_space=pl.ANY)
    near = pl.BlockSpec(memory_space=pltpu.VMEM)
    dma = pltpu.SemaphoreType.DMA
    like = jax.ShapeDtypeStruct((count, width), jnp.bfloat16)
    return pl.pallas_call(
        close_kernel,
        in_specs=[near] * 6 + [anywhere] * 2,
        out_specs=[near] * (3 + len(shapes)),
        out_shape=[like] * 3 + [jax.ShapeDtypeStruct(shape, jnp.float32) for shape in shapes],
        scratch_shapes=[
            pltpu.VMEM(sizes + (side, width), jnp.bfloat16),
            pltpu.VMEM((2 * width, width), jnp.float32),
            pltpu.VMEM(sizes + (2 * side, width), jnp.bfloat16),
        ]
        + scatter_scratch(shapes)
        + [dma],
        compiler_params=pltpu.CompilerParams(
            collective_id=collective_id, has_side_effects=True, vmem_limit_bytes=62 * 2**20
        ),
        name="close_all",
    )(target, final_slots, adapt_w, once, embeds, d_home, square, gain)


def paired_on_device(
    latents, embeds, cotangent, counts, w_adapt, w_query, w_key, w_value, w_out, w_gate, w_up, w_down, gains
):
    block_len, seqs, width = latents.shape
    parts = lax.axis_size("grp") * lax.axis_size("ctx")
    length = block_len * parts
    core = grid_place()[3]

    twice = counts == 2
    slot = jnp.where(
        twice,
        2 * (jnp.cumsum(twice.astype(jnp.int32)) - 1),
        2 * (jnp.cumsum((~twice).astype(jnp.int32)) - 1) + 1,
    )
    row_count = block_len * seqs
    target = (slot[None, :] * block_len + jnp.arange(block_len, dtype=jnp.int32)[:, None]).reshape(row_count)
    latent_rows, embed_rows, slope_rows = (a.reshape(row_count, width) for a in (latents, embeds, cotangent))

    def exchange(values):
        return lax.all_to_all(values, BOTH, split_axis=0, concat_axis=0, tiled=True)

    half = block_len // 2
    gain_rows = jnp.pad(gains.reshape(1, -1), ((0, 15), (0, 0)))
    *matrices, gain_float, shared, starting, upstream = open_all(
        target.reshape(1, row_count),
        latent_rows,
        embed_rows,
        slope_rows,
        [w_adapt, w_query, w_key, w_value, w_out, w_gate, w_up, w_down, gain_rows],
        block_len,
        0,
    )
    adapt_w, query_w, key_w, value_w, output_w, gate_w, up_w, down_w = (
        matrix.reshape(-1, matrix.shape[-1]) for matrix in matrices
    )
    gain_float = gain_float.reshape((parts,) + gain_rows.shape)[:, 0].reshape((parts,) + gains.shape)
    gain_float = gain_float.transpose(1, 0, 2).reshape(gains.shape[0], width).astype(jnp.float32)
    shared = shared.reshape(length // 2, width)
    starting = exchange(starting).reshape(length, width)

    cos_full, sin_full = rope_full(length)
    cos_half, sin_half = (table.reshape(parts, 2, half, HEAD_DIM) for table in (cos_full, sin_full))
    queries, keys_in, values_in = first_heads(shared, gain_float, query_w, key_w, value_w, cos_half, sin_half)
    far_keys, far_values = send(keys_in, 3), send(values_in, 3)
    mixed = attend_shared(core, half, queries, keys_in, values_in, far_keys, far_values)
    near_out = first_rows(shared, mixed, gain_float, output_w, gate_w, up_w, down_w)
    near_out, upstream = lax.optimization_barrier((near_out, upstream))
    upstream = exchange(upstream.reshape(parts, block_len, width)).reshape(length, width)
    far_out = send(near_out, 3, -1)

    resid, normed, first_out, queries, keys_in, values_in = last_heads(
        starting,
        near_out.reshape(parts, half, width),
        far_out.reshape(parts, half, width),
        adapt_w,
        gain_float,
        query_w,
        key_w,
        value_w,
        cos_full,
        sin_full,
    )
    mixed, log_total = attend_whole(queries, keys_in, values_in)
    result, branch, middle, mlp_in, down_out, gate_pre, up_pre, hidden = last_rows(
        resid, mixed, gain_float, output_w, gate_w, up_w, down_w
    )
    d_middle, d_branch, d_mixed, gain_rest, gate_part, up_part, down_part = back_rows(
        down_out,
        upstream,
        middle,
        branch,
        mlp_in,
        gain_float,
        output_w,
        gate_w,
        up_w,
        down_w,
        gate_pre,
        up_pre,
        hidden,
    )
    result, upstream = lax.optimization_barrier((result, upstream))
    final_back = exchange(result.reshape(parts, block_len, width))

    def blocks(part):
        return part.reshape(parts, -1, part.shape[-1])

    d_home, gain_one, weight_parts, gate_grad, up_grad, down_grad = middle_all(
        queries,
        keys_in,
        values_in,
        mixed,
        d_mixed,
        log_total,
        cos_full,
        sin_full,
        resid,
        d_middle,
        gain_float,
        query_w,
        key_w,
        value_w,
        normed,
        first_out,
        d_branch,
        [blocks(part) for part in (gate_part, up_part, down_part)],
        1,
    )
    gain_part = jnp.concatenate([gain_one[:1], gain_rest[:3]], 0)
    gain_part = gain_part.reshape(gains.shape[0], parts, gains.shape[1]).transpose(1, 0, 2)
    gain_part = jnp.pad(
        gain_part.reshape(parts, 1, gains.size).astype(jnp.bfloat16), ((0, 0), (0, 15), (0, 0))
    )
    final_back, latent_back, embed_back, query_grad, key_grad, value_grad, out_grad, adapt_grad, gain_grad = close_all(
        target.reshape(1, row_count),
        final_back.reshape(row_count, width),
        adapt_w,
        jnp.where(twice[None, :, None], jnp.zeros_like(latents), latents).reshape(row_count, width),
        embed_rows,
        d_home,
        weight_parts,
        gain_part,
        2,
    )
    gain_grad = gain_grad[0].reshape(gains.shape)
    return (
        final_back.reshape(latents.shape),
        latent_back.reshape(latents.shape),
        embed_back.reshape(latents.shape),
        adapt_grad,
        query_grad,
        key_grad,
        value_grad,
        out_grad,
        gate_grad,
        up_grad,
        down_grad,
        gain_grad,
    )


def on_device(latents, *others):
    ctx = lax.axis_size("ctx")
    parts = lax.axis_size("grp") * ctx
    if latents.shape[1] == parts and ctx == 4 and latents.shape[0] % 16 == 0:
        return paired_on_device(latents, *others)
    return spread_on_device(latents, *others)


def solution(mesh):
    placed = (
        P(("grp", "ctx"), None, None),
        P(("grp", "ctx"), None, None),
        P(("grp", "ctx"), None, None),
        P(),
        P(("grp", "ctx"), None),
        P(("grp", "ctx"), None),
        P(("grp", "ctx"), None),
        P(("grp", "ctx"), None),
        P(("grp", "ctx"), None),
        P(("grp", "ctx"), None),
        P(("grp", "ctx"), None),
        P(("grp", "ctx"), None),
        P(None, ("grp", "ctx")),
    )
    return jax.shard_map(
        on_device,
        mesh=mesh,
        in_specs=placed,
        out_specs=(
            P(("grp", "ctx"), None, None),
            P(("grp", "ctx"), None, None),
            P(("grp", "ctx"), None, None),
            P(("grp", "ctx"), None),
            P(("grp", "ctx"), None),
            P(("grp", "ctx"), None),
            P(("grp", "ctx"), None),
            P(("grp", "ctx"), None),
            P(("grp", "ctx"), None),
            P(("grp", "ctx"), None),
            P(("grp", "ctx"), None),
            P(None, ("grp", "ctx")),
        ),
        check_vma=False,
    )
```

```python
import functools

import jax
import jax.numpy as jnp
import numpy as np
from jax import lax
from jax.experimental import pallas as pl
from jax.experimental.pallas import tpu as pltpu
from jax.sharding import PartitionSpec as P

HEADS = 8
HEAD_DIM = 128


def rms_scale(values):
    return lax.rsqrt(jnp.mean(values * values, -1, keepdims=True) + 1e-06)


def norm_back(values, upstream, gain_vec):
    scale_rows = rms_scale(values)
    normal = values * scale_rows
    gain_part = jnp.sum(upstream * normal, 0)
    scaled = upstream * gain_vec
    return (
        scale_rows * (scaled - normal * jnp.mean(scaled * normal, -1, keepdims=True)),
        gain_part,
    )


def rope_table(positions):
    freq = 10000.0 ** (-2.0 * jnp.arange(HEAD_DIM // 2, dtype=jnp.float32) / HEAD_DIM)
    angle = positions.astype(jnp.float32)[:, None] * freq
    return (jnp.cos(angle), jnp.sin(angle))


def rotate(values, cosine, sine):
    half_dim = HEAD_DIM // 2
    first_half = values[..., :half_dim]
    second_half = values[..., half_dim:]
    cos_b = cosine[:, None, None, :]
    sin_b = sine[:, None, None, :]
    return jnp.concatenate(
        [first_half * cos_b - second_half * sin_b, second_half * cos_b + first_half * sin_b], -1
    )


def unrotate(grads, cosine, sine):
    half_dim = HEAD_DIM // 2
    first_half = grads[..., :half_dim]
    second_half = grads[..., half_dim:]
    cos_b = cosine[:, None, None, :]
    sin_b = sine[:, None, None, :]
    return jnp.concatenate(
        [first_half * cos_b + second_half * sin_b, second_half * cos_b - first_half * sin_b], -1
    )


def score_block(queries, keys_in, query_pos, key_pos_in):
    raw = jnp.einsum(
        "qshd,kshd->qshk", queries, keys_in, preferred_element_type=jnp.float32
    ) * HEAD_DIM ** (-0.5)
    causal = key_pos_in[None, :] <= query_pos[:, None]
    return jnp.where(causal[:, None, None, :], raw, -1e30)


def back_block(queries, keys_in, values_in, d_mixed, log_total, delta, query_pos, key_pos_in):
    scores = score_block(queries, keys_in, query_pos, key_pos_in)
    probs = jnp.exp(scores - log_total[..., None])
    d_probs = jnp.einsum("qshd,kshd->qshk", d_mixed, values_in, preferred_element_type=jnp.float32)
    slopes = (probs * (d_probs - delta[..., None])).astype(jnp.bfloat16)
    return (probs.astype(jnp.bfloat16), slopes)


def spread_on_device(
    latents,
    embeds,
    cotangent,
    counts,
    w_adapt,
    w_query,
    w_key,
    w_value,
    w_out,
    w_gate,
    w_up,
    w_down,
    gains,
):
    groups = lax.axis_size("grp")
    ctx_count = lax.axis_size("ctx")
    seq_total = latents.shape[1]
    seq_group = seq_total // groups
    block_len = latents.shape[0]
    model_width = latents.shape[2]
    group_len = groups * block_len
    adapt_w, query_w, key_w, value_w, output_w, gate_w, up_w, down_w, gain_rows = (
        lax.all_gather(w_adapt, ("grp", "ctx"), axis=0, tiled=True),
        lax.all_gather(w_query, ("grp", "ctx"), axis=0, tiled=True),
        lax.all_gather(w_key, ("grp", "ctx"), axis=0, tiled=True),
        lax.all_gather(w_value, ("grp", "ctx"), axis=0, tiled=True),
        lax.all_gather(w_out, ("grp", "ctx"), axis=0, tiled=True),
        lax.all_gather(w_gate, ("grp", "ctx"), axis=0, tiled=True),
        lax.all_gather(w_up, ("grp", "ctx"), axis=0, tiled=True),
        lax.all_gather(w_down, ("grp", "ctx"), axis=0, tiled=True),
        lax.all_gather(gains, ("grp", "ctx"), axis=1, tiled=True),
    )
    gain_float = gain_rows.astype(jnp.float32)
    seq_order = jnp.arange(seq_total, dtype=jnp.int32)
    latent_in, embed_in, slope_in = (
        lax.all_to_all(
            jnp.take(latents, seq_order, axis=1), "grp", split_axis=1, concat_axis=0, tiled=True
        ),
        lax.all_to_all(
            jnp.take(embeds, seq_order, axis=1), "grp", split_axis=1, concat_axis=0, tiled=True
        ),
        lax.all_to_all(
            jnp.take(cotangent, seq_order, axis=1), "grp", split_axis=1, concat_axis=0, tiled=True
        ),
    )
    ctx_index = lax.axis_index("ctx")

    def key_position(flat_index):
        source = flat_index // group_len
        within = flat_index % group_len
        return (within // block_len * ctx_count + source) * block_len + within % block_len

    query_pos = key_position(ctx_index * group_len + jnp.arange(group_len, dtype=jnp.int32))
    cos_query, sin_query = rope_table(query_pos)

    def attend_forward(queries, keys_in, values_in):
        piece = lax.all_gather(keys_in, "ctx", axis=0, tiled=True)
        scores = score_block(
            queries, piece, query_pos, key_position(jnp.arange(piece.shape[0], dtype=jnp.int32))
        )
        log_total = jax.nn.logsumexp(scores, -1)
        probs = jnp.exp(scores - log_total[..., None]).astype(jnp.bfloat16)
        mixed_raw = jnp.einsum(
            "qshk,kshd->qshd",
            probs,
            lax.all_gather(values_in, "ctx", axis=0, tiled=True),
            preferred_element_type=jnp.float32,
        )
        return (mixed_raw.astype(jnp.bfloat16), (queries, keys_in, values_in, log_total, mixed_raw))

    def core_block(latent, embedding):
        seq_batch = latent.shape[1]
        row_count = group_len * seq_batch
        joined = jnp.concatenate([latent.astype(jnp.bfloat16), embedding], -1).reshape(
            row_count, 2 * model_width
        )
        resid = jnp.dot(joined, adapt_w, preferred_element_type=jnp.float32)
        normed = (resid * rms_scale(resid) * gain_float[0]).astype(jnp.bfloat16)

        def heads_of(matrix):
            return jnp.dot(normed, matrix, preferred_element_type=jnp.float32).reshape(
                group_len, seq_batch, HEADS, HEAD_DIM
            )

        queries = rotate(heads_of(query_w), cos_query, sin_query).astype(jnp.bfloat16)
        keys_in = rotate(heads_of(key_w), cos_query, sin_query).astype(jnp.bfloat16)
        values_in = heads_of(value_w).astype(jnp.bfloat16)
        mixed, kept = attend_forward(queries, keys_in, values_in)
        mixed_flat = mixed.reshape(row_count, model_width)
        branch = jnp.dot(mixed_flat, output_w, preferred_element_type=jnp.float32)
        middle = resid + branch * rms_scale(branch) * gain_float[1]
        mlp_in = (middle * rms_scale(middle) * gain_float[2]).astype(jnp.bfloat16)
        gate_pre = jnp.dot(mlp_in, gate_w, preferred_element_type=jnp.float32)
        up_pre = jnp.dot(mlp_in, up_w, preferred_element_type=jnp.float32)
        hidden = (jax.nn.silu(gate_pre) * up_pre).astype(jnp.bfloat16)
        down_out = jnp.dot(hidden, down_w, preferred_element_type=jnp.float32)
        result = middle + down_out * rms_scale(down_out) * gain_float[3]
        flat_saved = tuple(
            (
                stored.reshape(group_len, seq_batch, stored.shape[-1])
                for stored in (
                    joined,
                    resid,
                    normed,
                    mixed_flat,
                    branch,
                    middle,
                    mlp_in,
                    gate_pre,
                    up_pre,
                    hidden,
                    down_out,
                )
            )
        )
        return (result.reshape(group_len, seq_batch, model_width), (flat_saved, kept))

    group_counts = lax.dynamic_slice_in_dim(
        jnp.take(counts, seq_order), lax.axis_index("grp") * seq_group, seq_group
    )
    first_out, first_saved = core_block(latent_in, embed_in)
    last_in = jnp.where(group_counts[None, :, None] == 2, first_out, latent_in.astype(jnp.float32))
    final_out, saved = core_block(last_in, embed_in)
    upstream = slope_in.astype(jnp.float32)
    flat_saved, kept = saved
    (
        joined,
        resid,
        normed,
        mixed_flat,
        branch,
        middle,
        mlp_in,
        gate_pre,
        up_pre,
        hidden,
        down_out,
    ) = tuple((stored.reshape(-1, stored.shape[-1]) for stored in flat_saved))
    seq_batch = upstream.shape[1]
    d_result = upstream.reshape(-1, model_width)
    d_down, gain_four = norm_back(down_out, d_result, gain_float[3])
    d_down = d_down.astype(jnp.bfloat16)
    down_part = jnp.einsum("rf,rd->fd", hidden, d_down, preferred_element_type=jnp.float32)
    d_hidden = jnp.einsum("rd,fd->rf", d_down, down_w, preferred_element_type=jnp.float32)
    sigma = jax.nn.sigmoid(gate_pre)
    d_gate = (d_hidden * up_pre * sigma * (1.0 + gate_pre * (1.0 - sigma))).astype(jnp.bfloat16)
    d_up = (d_hidden * gate_pre * sigma).astype(jnp.bfloat16)
    gate_part = jnp.einsum("rd,rf->df", mlp_in, d_gate, preferred_element_type=jnp.float32)
    up_part = jnp.einsum("rd,rf->df", mlp_in, d_up, preferred_element_type=jnp.float32)
    d_mlp = jnp.einsum(
        "rf,df->rd", d_gate, gate_w, preferred_element_type=jnp.float32
    ) + jnp.einsum("rf,df->rd", d_up, up_w, preferred_element_type=jnp.float32)
    d_middle, gain_three = norm_back(middle, d_mlp, gain_float[2])
    d_middle = d_middle + d_result
    d_branch, gain_two = norm_back(branch, d_middle, gain_float[1])
    d_branch = d_branch.astype(jnp.bfloat16)
    out_part = jnp.einsum("re,rd->ed", mixed_flat, d_branch, preferred_element_type=jnp.float32)
    d_mixed = jnp.einsum(
        "rd,ed->re", d_branch, output_w, preferred_element_type=jnp.float32
    ).astype(jnp.bfloat16)
    attend_d_mixed = d_mixed.reshape(group_len, seq_batch, HEADS, HEAD_DIM)
    queries, keys_in, values_in, log_total, mixed_raw = kept
    delta = jnp.sum(attend_d_mixed.astype(jnp.float32) * mixed_raw, -1)
    key_part = lax.all_gather(keys_in, "ctx", axis=0, tiled=True)
    value_part = lax.all_gather(values_in, "ctx", axis=0, tiled=True)
    key_pos_in = key_position(jnp.arange(key_part.shape[0], dtype=jnp.int32))
    probs_low, slopes = back_block(
        queries, key_part, value_part, attend_d_mixed, log_total, delta, query_pos, key_pos_in
    )
    d_query = HEAD_DIM ** (-0.5) * jnp.einsum(
        "qshk,kshd->qshd", slopes, key_part, preferred_element_type=jnp.float32
    )
    pull_stacked = jnp.stack([probs_low, slopes])
    d_query, stacked = (d_query, pull_stacked)
    d_key = HEAD_DIM ** (-0.5) * jnp.einsum(
        "qshk,qshd->kshd", stacked[1], queries, preferred_element_type=jnp.float32
    )
    d_value = jnp.einsum(
        "qshk,qshd->kshd", stacked[0], attend_d_mixed, preferred_element_type=jnp.float32
    )
    paired = lax.psum_scatter(
        jnp.concatenate([d_key, d_value], -1).astype(jnp.bfloat16),
        "ctx",
        scatter_dimension=0,
        tiled=True,
    ).astype(jnp.float32)
    d_query, d_key, d_value = (
        unrotate(d_query, cos_query, sin_query).astype(jnp.bfloat16),
        unrotate(paired[..., :HEAD_DIM], cos_query, sin_query).astype(jnp.bfloat16),
        paired[..., HEAD_DIM:].astype(jnp.bfloat16),
    )
    d_query = d_query.reshape(-1, model_width)
    d_key = d_key.reshape(-1, model_width)
    d_value = d_value.reshape(-1, model_width)
    query_part = jnp.einsum("rd,re->de", normed, d_query, preferred_element_type=jnp.float32)
    key_part = jnp.einsum("rd,re->de", normed, d_key, preferred_element_type=jnp.float32)
    value_part = jnp.einsum("rd,re->de", normed, d_value, preferred_element_type=jnp.float32)
    d_normed = (
        jnp.einsum("re,de->rd", d_query, query_w, preferred_element_type=jnp.float32)
        + jnp.einsum("re,de->rd", d_key, key_w, preferred_element_type=jnp.float32)
        + jnp.einsum("re,de->rd", d_value, value_w, preferred_element_type=jnp.float32)
    )
    d_resid, gain_one = norm_back(resid, d_normed, gain_float[0])
    d_resid = (d_resid + d_middle).astype(jnp.bfloat16)
    adapt_part = jnp.einsum("rk,rd->kd", joined, d_resid, preferred_element_type=jnp.float32)
    d_joined = jnp.einsum("rd,kd->rk", d_resid, adapt_w, preferred_element_type=jnp.float32)
    gain_part = jnp.stack([gain_one, gain_two, gain_three, gain_four])
    d_joined, grads = (
        d_joined.reshape(group_len, seq_batch, 2 * model_width),
        (
            adapt_part,
            query_part,
            key_part,
            value_part,
            out_part,
            gate_part,
            up_part,
            down_part,
            gain_part,
        ),
    )
    final_back, latent_back, embed_back = (
        lax.all_to_all(
            final_out.astype(jnp.bfloat16), "grp", split_axis=0, concat_axis=1, tiled=True
        ),
        lax.all_to_all(
            d_joined[..., :model_width].astype(jnp.bfloat16),
            "grp",
            split_axis=0,
            concat_axis=1,
            tiled=True,
        ),
        lax.all_to_all(
            d_joined[..., model_width:].astype(jnp.bfloat16),
            "grp",
            split_axis=0,
            concat_axis=1,
            tiled=True,
        ),
    )
    seq_index = jnp.arange(seq_total, dtype=jnp.int32)
    inverse = jnp.sum(jnp.where(seq_order[:, None] == seq_index[None, :], seq_index[:, None], 0), 0)
    (
        adapt_part,
        query_part,
        key_part,
        value_part,
        out_part,
        gate_part,
        up_part,
        down_part,
        gain_part,
    ) = grads
    summed = (
        lax.psum_scatter(adapt_part, ("grp", "ctx"), scatter_dimension=0, tiled=True),
        lax.psum_scatter(query_part, ("grp", "ctx"), scatter_dimension=0, tiled=True),
        lax.psum_scatter(key_part, ("grp", "ctx"), scatter_dimension=0, tiled=True),
        lax.psum_scatter(value_part, ("grp", "ctx"), scatter_dimension=0, tiled=True),
        lax.psum_scatter(out_part, ("grp", "ctx"), scatter_dimension=0, tiled=True),
        lax.psum_scatter(gate_part, ("grp", "ctx"), scatter_dimension=0, tiled=True),
        lax.psum_scatter(up_part, ("grp", "ctx"), scatter_dimension=0, tiled=True),
        lax.psum_scatter(down_part, ("grp", "ctx"), scatter_dimension=0, tiled=True),
        lax.psum_scatter(gain_part, ("grp", "ctx"), scatter_dimension=1, tiled=True),
    )
    return (
        jnp.take(final_back, inverse, axis=1),
        jnp.take(latent_back, inverse, axis=1),
        jnp.take(embed_back, inverse, axis=1),
        summed[0],
        summed[1],
        summed[2],
        summed[3],
        summed[4],
        summed[5],
        summed[6],
        summed[7],
        summed[8],
    )


BOTH = ("grp", "ctx")
LOG2E = 1.4426950408889634
SCALE = HEAD_DIM ** (-0.5)
TILE = 256
NEG = -1e30


def grid_sizes():
    ctx = lax.axis_size("ctx")
    x_size = ctx // 2
    return lax.axis_size("grp") // x_size, x_size, x_size, 2


def grid_place():
    z_size, y_size, x_size, k_size = grid_sizes()
    g, c = lax.axis_index("grp"), lax.axis_index("ctx")
    return g // y_size, g % y_size, c // k_size, c % k_size


def send(values, axis, shift=None, keep=None):
    sizes = grid_sizes()
    pairs = []
    for flat in range(sizes[0] * sizes[1] * sizes[2] * sizes[3]):
        rest, spot = flat, [0, 0, 0, 0]
        for at in (3, 2, 1, 0):
            spot[at] = rest % sizes[at]
            rest //= sizes[at]
        own = spot[axis]
        other = 1 - own if shift is None else own + shift
        if 0 <= other < sizes[axis] and (keep is None or keep(own)):
            spot[axis] = other
            target = ((spot[0] * sizes[1] + spot[1]) * sizes[2] + spot[2]) * sizes[3] + spot[3]
            pairs.append((flat, target))
    return lax.ppermute(values, BOTH, pairs)


MESH = pl.DeviceIdType.MESH


def device_at(z, y, x, k):
    _, y_size, _, k_size = grid_sizes()
    return (z * y_size + y, x * k_size + k)


def order_of(y, x, turn):
    first = (y + turn * (1 - 2 * y), x + (1 - turn) * (1 - 2 * x))
    second = (y + (1 - turn) * (1 - 2 * y), x + turn * (1 - 2 * x))
    return first, second


def greet_line(z, y, x, k, z_size):
    barrier = pltpu.get_barrier_semaphore()
    for device in (device_at(z, 1 - y, x, k), device_at(z, y, 1 - x, k), device_at(z, y, x, 1 - k)):
        pl.semaphore_signal(barrier, inc=1, device_id=device, device_id_type=MESH)

    @pl.when(z > 0)
    def _():
        pl.semaphore_signal(barrier, inc=1, device_id=device_at(z - 1, y, x, k), device_id_type=MESH)

    @pl.when(z < z_size - 1)
    def _():
        pl.semaphore_signal(barrier, inc=1, device_id=device_at(z + 1, y, x, k), device_id_type=MESH)

    pl.semaphore_wait(barrier, 3 + jnp.minimum(z, 1) + jnp.minimum(z_size - 1 - z, 1))


def remote(source, target, send_sem, recv_sem, device):
    return pltpu.make_async_remote_copy(
        src_ref=source,
        dst_ref=target,
        send_sem=send_sem,
        recv_sem=recv_sem,
        device_id=device,
        device_id_type=MESH,
    )


def row_views(shapes):
    views = []
    for at, (rows, width) in enumerate(shapes):
        if rows % 32 == 0 and rows * width >= 2**16:
            views += [(at, 0, rows // 2, 0), (at, rows // 2, rows // 2, 1)]
        else:
            views.append((at, 0, rows, at % 2))
    return views


def at_offsets(z, z_size, step, body):
    if step == 0:
        body(z, True, True)
        return

    @pl.when(z >= step)
    def _():
        body(z - step, True, False)

    @pl.when(z + step < z_size)
    def _():
        body(z + step, False, True)


def greet_all(parts, me, ctx):
    barrier = pltpu.get_barrier_semaphore()

    def greet(at, carry):
        @pl.when(at != me)
        def _():
            pl.semaphore_signal(barrier, inc=1, device_id=flat_device(at, ctx), device_id_type=MESH)

        return carry

    lax.fori_loop(0, parts, greet, 0)
    pl.semaphore_wait(barrier, parts - 1)


def each_other(first, last, me, act):
    def body(at, carry):
        @pl.when(at != me)
        def _():
            act(at)

        return carry

    lax.fori_loop(first, last, body, 0)


def flat_device(at, ctx):
    return (at // ctx, at % ctx)


class Gather:
    def __init__(self, views, count, shards, outs, sems):
        self.z_size = grid_sizes()[0]
        self.place = grid_place()
        self.views, self.count, self.shards, self.outs = views, count, shards, outs
        self.local_sem, self.z_send, self.z_recv, self.p_send, self.p_recv, self.k_send, self.k_recv = sems

    def at(self, step, body):
        at_offsets(self.place[0], self.z_size, step, body)

    def spot(self, g, slot_z, at_y, at_x):
        at, first_row, rows, _ = self.views[g]
        return self.outs[at].at[slot_z, at_y, at_x, self.place[3], pl.ds(first_row, rows)]

    def source(self, g, block, own):
        at, first_row, rows, _ = self.views[g]
        return self.shards[at].at[pl.ds(first_row, rows)] if own else block

    def z_copy(self, g, slot_z, way, own=False):
        z, y, x, k = self.place
        block = self.spot(g, slot_z, y, x)
        device = device_at(z + 1 - 2 * way, y, x, k)
        return remote(self.source(g, block, own), block, self.z_send.at[g, slot_z, way], self.z_recv.at[g, slot_z], device)

    def plane_copy(self, g, slot_z, kind, own=False):
        z, y, x, k = self.place
        first, second = order_of(y, x, (self.views[g][3] + slot_z) % 2)
        from_at = first if kind == 2 else (y, x)
        to_at = first if kind == 0 else second
        block = self.spot(g, slot_z, from_at[0], from_at[1])
        device = device_at(z, to_at[0], to_at[1], k)
        source = self.source(g, block, own)
        return remote(source, block, self.p_send.at[g, slot_z, kind], self.p_recv.at[g, slot_z, kind], device)

    def core_copy(self, at, slot_z):
        z, y, x, k = self.place
        block = self.outs[at].at[slot_z, :, :, k]
        return remote(block, block, self.k_send.at[at, slot_z], self.k_recv.at[at, slot_z], device_at(z, y, x, 1 - k))

    def own_copy(self, at):
        z, y, x, k = self.place
        return pltpu.make_async_copy(self.shards[at], self.outs[at].at[z, y, x, k], self.local_sem.at[at])

    def each_way(self, g, slot_z, up, down, act):
        z, own = self.place[0], up and down
        if up:

            @pl.when(z < self.z_size - 1)
            def _():
                act(self.z_copy(g, slot_z, 0, own))

        if down:

            @pl.when(z > 0)
            def _():
                act(self.z_copy(g, slot_z, 1, own))

    def series(self, arrays):
        return [g for g, view in enumerate(self.views) if view[0] in arrays]

    def arrive(self, arrays, step):
        def body(slot_z, up, down):
            for g in self.series(arrays):
                if step > 0:
                    self.z_copy(g, slot_z, 1 if up else 0).wait_recv()
                self.each_way(g, slot_z, up, down, lambda copy: copy.start())

        self.at(step, body)

    def spread(self, arrays, step):
        def body(slot_z, up, down):
            for g in self.series(arrays):
                self.plane_copy(g, slot_z, 0, step == 0).start()
                self.plane_copy(g, slot_z, 1, step == 0).start()

        self.at(step, body)

    def pass_on(self, arrays, step):
        def body(slot_z, up, down):
            for g in self.series(arrays):
                self.plane_copy(g, slot_z, 0).wait_recv()
                self.plane_copy(g, slot_z, 2).start()

        self.at(step, body)

    def cross(self, arrays, step):
        def body(slot_z, up, down):
            for g in self.series(arrays):
                self.plane_copy(g, slot_z, 1).wait_recv()
                self.plane_copy(g, slot_z, 2).wait_recv()
            for at in arrays:
                if step == 0:
                    self.own_copy(at).wait()
                self.core_copy(at, slot_z).start()

        self.at(step, body)

    def complete(self, arrays):
        for slot_z in range(self.z_size):
            for at in arrays:
                self.core_copy(at, slot_z).wait_recv()

    def settle(self, arrays):
        def body(slot_z, up, down):
            for g in self.series(arrays):
                self.each_way(g, slot_z, up, down, lambda copy: copy.wait_send())
                for kind in range(3):
                    self.plane_copy(g, slot_z, kind).wait_send()

        for step in range(self.z_size):
            self.at(step, body)
        for slot_z in range(self.z_size):
            for at in arrays:
                self.core_copy(at, slot_z).wait_send()


def open_kernel(views, count, block_len, *refs):
    z_size, _, x_size, k_size = grid_sizes()
    z, y, x, k = grid_place()
    ctx = x_size * k_size
    parts = lax.axis_size("grp") * ctx
    me = lax.axis_index("grp") * ctx + lax.axis_index("ctx")
    target_ref, s_ref, e_ref, c_ref = refs[:4]
    shards, refs = refs[4 : 4 + count], refs[4 + count :]
    outs, refs = refs[:count], refs[count:]
    shared_out, start_ref, up_ref, joined, shared_held = refs[:5]
    gather = Gather(views, count, shards, outs, refs[5:12])
    send_sem, recv_sem, own_sem = refs[12:]
    width = s_ref.shape[1]
    count_rows = s_ref.shape[0]
    half = block_len // 2
    tiles = count_rows // TILE
    slots = TILE // block_len
    adapt, early, late = (0,), (1, 2, 3, 4, 8), (5, 6, 7)

    greet_all(parts, me, ctx)

    def half_copy(at):
        device = flat_device(at, ctx)
        return remote(shared_held.at[at], shared_out.at[me], send_sem.at[at], recv_sem.at[me], device)

    own_half = pltpu.make_async_copy(shared_held.at[me], shared_out.at[me], own_sem)

    def reorder(tile):
        rows = pl.ds(pl.multiple_of(tile * TILE, TILE), TILE)
        at_row = lax.broadcasted_iota(jnp.int32, (TILE, count_rows), 0) + tile * TILE
        order = (at_row == target_ref[...]).astype(jnp.bfloat16)
        joined[rows, :width] = dot_n(order, s_ref[...]).astype(jnp.bfloat16)
        joined[rows, width:] = dot_n(order, e_ref[...]).astype(jnp.bfloat16)
        up_ref[rows, :] = dot_n(order, c_ref[...]).astype(jnp.bfloat16)

    def apply(tile):
        rows = pl.ds(pl.multiple_of(tile * TILE, TILE), TILE)
        weight = outs[0][...].reshape(2 * width, width)
        embed_part = dot_n(joined[rows, width:], weight[width:]).astype(jnp.bfloat16)
        adapted = dot_n(joined[rows, :], weight).astype(jnp.bfloat16)
        for pair in range(slots // 2):
            at = tile * slots + 2 * pair
            even = slice(2 * pair * block_len, (2 * pair + 1) * block_len)
            odd = slice((2 * pair + 1) * block_len, (2 * pair + 2) * block_len)
            start_ref[at] = embed_part[even]
            start_ref[at + 1] = adapted[odd]
            shared_held[at] = adapted[even][:half]
            shared_held[at + 1] = adapted[even][half:]

        each_other(tile * slots, (tile + 1) * slots, me, lambda at: half_copy(at).start())

    for step in range(z_size):
        gather.arrive(adapt, step)
        gather.spread(adapt, step)
        if step == 0:
            for at in range(count):
                gather.own_copy(at).start()
        gather.arrive(early, step)
        if step < tiles:
            reorder(step)
        gather.spread(early, step)
        gather.pass_on(adapt, step)
        if step > 0:
            gather.cross(adapt, step - 1)
            gather.pass_on(early, step - 1)
        if step == z_size - 2:
            gather.arrive(late, 0)
    gather.spread(late, 0)
    gather.cross(adapt, z_size - 1)
    for tile in range(z_size, tiles):
        reorder(tile)
    gather.arrive(late, 1)
    gather.pass_on(early, z_size - 1)
    gather.spread(late, 1)
    gather.complete(adapt)
    for tile in range(tiles):
        apply(tile)
        if tile == 0:
            gather.pass_on(late, 0)
        if tile == 1:
            gather.arrive(late, 2)
            gather.spread(late, 2)
        if tile == 2:
            gather.pass_on(late, 1)
    own_half.start()
    gather.arrive(late, 3)
    gather.spread(late, 3)
    for step in range(z_size):
        gather.cross(early, step)
    gather.cross(late, 0)
    gather.pass_on(late, 2)
    gather.cross(late, 1)
    gather.pass_on(late, 3)
    gather.cross(late, 2)
    gather.cross(late, 3)
    gather.complete(early + late)
    gather.settle(adapt + early + late)

    def settle_half(at):
        device = flat_device(at, ctx)
        remote(shared_held.at[at], shared_out.at[at], send_sem.at[at], recv_sem.at[at], device).wait()

    each_other(0, parts, me, settle_half)
    own_half.wait()


def open_all(target, latents, embeds, cotangent, shards, block_len, collective_id):
    sizes = grid_sizes()
    parts = lax.axis_size("grp") * lax.axis_size("ctx")
    count, z_size = len(shards), sizes[0]
    rows, width = latents.shape
    views = row_views([shard.shape for shard in shards])
    series = len(views)
    anywhere = pl.BlockSpec(memory_space=pl.ANY)
    near = pl.BlockSpec(memory_space=pltpu.VMEM)
    dma = pltpu.SemaphoreType.DMA
    half = block_len // 2
    return pl.pallas_call(
        functools.partial(open_kernel, views, count, block_len),
        in_specs=[near] * 4 + [anywhere] * count,
        out_specs=[near] + [anywhere] * count + [near] * 2,
        out_shape=[jax.ShapeDtypeStruct(sizes + shard.shape, shard.dtype) for shard in shards]
        + [
            jax.ShapeDtypeStruct((parts, half, width), jnp.bfloat16),
            jax.ShapeDtypeStruct((parts, block_len, width), jnp.bfloat16),
            jax.ShapeDtypeStruct((rows, width), jnp.bfloat16),
        ],
        scratch_shapes=[
            pltpu.VMEM((rows, 2 * width), jnp.bfloat16),
            pltpu.VMEM((parts, half, width), jnp.bfloat16),
            dma((count,)),
            dma((series, z_size, 2)),
            dma((series, z_size)),
            dma((series, z_size, 3)),
            dma((series, z_size, 3)),
            dma((count, z_size)),
            dma((count, z_size)),
            dma((parts,)),
            dma((parts,)),
            dma,
        ],
        compiler_params=pltpu.CompilerParams(
            collective_id=collective_id, has_side_effects=True, vmem_limit_bytes=56 * 2**20
        ),
        name="open_all",
    )(target, latents, embeds, cotangent, *shards)


class Scatter:
    def __init__(self, views, parts, outs, buffers, sems):
        self.z_size = grid_sizes()[0]
        self.place = grid_place()
        self.views, self.parts, self.outs = views, parts, outs
        count = len(parts)
        self.held, self.mine, self.from_second, self.from_first, self.from_z = (
            buffers[at * count : (at + 1) * count] for at in range(5)
        )
        self.local_sem, self.k_send, self.k_recv, self.p_send, self.p_recv, self.z_send, self.z_recv = sems

    def at(self, step, body):
        if 0 <= step < self.z_size:
            at_offsets(self.place[0], self.z_size, step, body)

    def series(self, arrays):
        return [g for g, view in enumerate(self.views) if view[0] in arrays]

    def rows_of(self, g):
        return pl.ds(self.views[g][1], self.views[g][2])

    def turns(self, g, slot_z):
        return order_of(self.place[1], self.place[2], (self.views[g][3] + slot_z) % 2)

    def core_copy(self, at, slot_z):
        z, y, x, k = self.place
        return remote(
            self.parts[at].at[slot_z, :, :, 1 - k],
            self.held[at].at[slot_z],
            self.k_send.at[at, slot_z],
            self.k_recv.at[at, slot_z],
            device_at(z, y, x, 1 - k),
        )

    def own_copy(self, at, slot_z, side):
        return pltpu.make_async_copy(
            self.parts[at].at[slot_z, :, :, self.place[3]], self.mine[at].at[side], self.local_sem.at[at, side]
        )

    def second_copy(self, g, slot_z, kind):
        z, y, x, k = self.place
        at, (_, second) = self.views[g][0], self.turns(g, slot_z)
        block = second if kind == 0 else (1 - y, 1 - x)
        return remote(
            self.held[at].at[slot_z, block[0], block[1], self.rows_of(g)],
            self.from_second[at].at[slot_z, kind, self.rows_of(g)],
            self.p_send.at[g, slot_z, kind],
            self.p_recv.at[g, slot_z, kind],
            device_at(z, second[0], second[1], k),
        )

    def first_copy(self, g, slot_z):
        z, y, x, k = self.place
        at, (first, _) = self.views[g][0], self.turns(g, slot_z)
        return remote(
            self.held[at].at[slot_z, first[0], first[1], self.rows_of(g)],
            self.from_first[at].at[slot_z, self.rows_of(g)],
            self.p_send.at[g, slot_z, 2],
            self.p_recv.at[g, slot_z, 2],
            device_at(z, first[0], first[1], k),
        )

    def z_copy(self, at, slot_z, way, lands_home, here=None):
        z, y, x, k = self.place
        side = z + 1 - 2 * way if here is None else here
        buffer = self.z_size if way == 1 and lands_home else slot_z
        return remote(
            self.held[at].at[slot_z, y, x],
            self.from_z[at].at[buffer],
            self.z_send.at[at, slot_z, way],
            self.z_recv.at[at, slot_z, way],
            device_at(side, y, x, k),
        )

    def begin(self, arrays):
        def body(slot_z, below, above):
            for at in arrays:
                self.core_copy(at, slot_z).start()

        for step in range(self.z_size - 1, -1, -1):
            self.at(step, body)

    def fold_core(self, arrays, step):
        def fetch(slot_z, below, above):
            for at in arrays:
                self.own_copy(at, slot_z, 0 if below else 1).start()

        def body(slot_z, below, above):
            _, y, x, _ = self.place
            side = 0 if below else 1
            for at in arrays:
                self.own_copy(at, slot_z, side).wait()
                self.core_copy(at, slot_z).wait_recv()
            for g in self.series(arrays):
                at, rows = self.views[g][0], self.rows_of(g)
                held, mine = self.held[at], self.mine[at]
                first, second = self.turns(g, slot_z)
                for spot in (second, (1 - y, 1 - x)):
                    here = (slot_z, spot[0], spot[1], rows)
                    held[here] = held[here] + mine[(side,) + here[1:]]
                self.second_copy(g, slot_z, 0).start()
                self.second_copy(g, slot_z, 1).start()
                for spot in (first, (y, x)):
                    here = (slot_z, spot[0], spot[1], rows)
                    held[here] = held[here] + mine[(side,) + here[1:]]

        self.at(step, fetch)
        self.at(step, body)

    def fold_second(self, arrays, step):
        def body(slot_z, below, above):
            for g in self.series(arrays):
                at, rows = self.views[g][0], self.rows_of(g)
                held, come = self.held[at], self.from_second[at]
                first, _ = self.turns(g, slot_z)
                self.second_copy(g, slot_z, 1).wait_recv()
                here = (slot_z, first[0], first[1], rows)
                held[here] = held[here] + come[slot_z, 1, rows]
                self.first_copy(g, slot_z).start()

        self.at(step, body)

    def fold_first(self, arrays, step):
        z, y, x, _ = self.place
        home = step == 0

        def body(slot_z, below, above):
            for g in self.series(arrays):
                at, rows = self.views[g][0], self.rows_of(g)
                held = self.held[at]
                here = (slot_z, y, x, rows)
                self.second_copy(g, slot_z, 0).wait_recv()
                self.first_copy(g, slot_z).wait_recv()
                held[here] = held[here] + self.from_second[at][slot_z, 0, rows] + self.from_first[at][slot_z, rows]
            if home:
                for at in arrays:
                    self.outs[at][...] = self.held[at][slot_z, y, x].astype(jnp.float32)
            for way, use in ((0, above), (1, below)):
                if not use:
                    continue
                came, source = (z > 0, z - 1) if way == 0 else (z < self.z_size - 1, z + 1)

                @pl.when(came)
                def _(way=way, source=source):
                    for at in arrays:
                        self.z_copy(at, slot_z, way, home, source).wait_recv()
                        come = self.from_z[at][self.z_size if way == 1 and home else slot_z]
                        if home:
                            self.outs[at][...] += come.astype(jnp.float32)
                        else:
                            self.held[at][slot_z, y, x] = self.held[at][slot_z, y, x] + come

                if not home:
                    for at in arrays:
                        self.z_copy(at, slot_z, way, step == 1).start()

        self.at(step, body)

    def settle(self, arrays):
        for step in range(self.z_size):

            def body(slot_z, below, above, step=step):
                for at in arrays:
                    self.core_copy(at, slot_z).wait_send()
                    if step > 0:
                        self.z_copy(at, slot_z, 0 if above else 1, step == 1).wait_send()
                for g in self.series(arrays):
                    self.second_copy(g, slot_z, 0).wait_send()
                    self.second_copy(g, slot_z, 1).wait_send()
                    self.first_copy(g, slot_z).wait_send()

            self.at(step, body)

    def stage(self, arrays, number):
        far = self.z_size - 1
        self.fold_core(arrays, far - number)
        self.fold_second(arrays, far - number + 1)
        self.fold_first(arrays, far - number + 2)

    def stages(self):
        return self.z_size + 2


def scatter_scratch(shapes):
    z_size, y_size, x_size, _ = grid_sizes()
    count, series = len(shapes), len(row_views(shapes))
    leads = ((z_size, y_size, x_size), (2, y_size, x_size), (z_size, 2), (z_size,), (z_size + 1,))
    dma = pltpu.SemaphoreType.DMA
    return [pltpu.VMEM(lead + shape, jnp.bfloat16) for lead in leads for shape in shapes] + [
        dma((count, 2)),
        dma((count, z_size)),
        dma((count, z_size)),
        dma((series, z_size, 3)),
        dma((series, z_size, 3)),
        dma((count, z_size, 2)),
        dma((count, z_size, 2)),
    ]


def dot_t(left, right):
    return lax.dot_general(left, right, (((1,), (1,)), ((), ())), preferred_element_type=jnp.float32)


def dot_n(left, right):
    return jnp.dot(left, right, preferred_element_type=jnp.float32)


def dot_w(left, right):
    return lax.dot_general(left, right, (((0,), (0,)), ((), ())), preferred_element_type=jnp.float32)


def below(rows, columns):
    at_row = lax.broadcasted_iota(jnp.int32, (rows, columns), 0)
    at_column = lax.broadcasted_iota(jnp.int32, (rows, columns), 1)
    return at_column <= at_row


def whole_attend(q_ref, k_ref, v_ref, o_ref, log_ref):
    head = pl.program_id(0)
    length = q_ref.shape[0]
    lane = lax.broadcasted_iota(jnp.int32, (TILE, 128), 1)
    for at in range(length // TILE):
        rows = pl.ds(at * TILE, TILE)
        seen = (at + 1) * TILE
        raw = dot_t(q_ref[rows, :], k_ref[:seen, :]) * (SCALE * LOG2E)
        last = jnp.where(below(TILE, TILE), raw[:, at * TILE :], NEG)
        raw = jnp.concatenate([raw[:, : at * TILE], last], 1) if at else last
        top = jnp.max(raw, 1, keepdims=True)
        weight = jnp.exp2(raw - top)
        total = jnp.sum(weight, 1, keepdims=True)
        mixed = dot_n(weight.astype(jnp.bfloat16), v_ref[:seen, :])
        o_ref[rows, :] = (mixed / total).astype(o_ref.dtype)
        log_total = top + jnp.log2(total)
        log_ref[rows, :] = jnp.where(lane == head, log_total, log_ref[rows, :])


def attend_whole(queries, keys_in, values_in):
    length, width = queries.shape
    head_block = pl.BlockSpec((length, HEAD_DIM), lambda h: (0, h))
    return pl.pallas_call(
        whole_attend,
        grid=(width // HEAD_DIM,),
        in_specs=[head_block] * 3,
        out_specs=[head_block, pl.BlockSpec((length, 128), lambda h: (0, 0))],
        out_shape=[
            jax.ShapeDtypeStruct((length, width), jnp.bfloat16),
            jax.ShapeDtypeStruct((length, 128), jnp.float32),
        ],
        compiler_params=pltpu.CompilerParams(vmem_limit_bytes=60 * 2**20),
        cost_estimate=pl.CostEstimate(
            flops=2 * length * length * width, bytes_accessed=8 * length * width, transcendentals=0
        ),
        name="attend_whole",
    )(queries, keys_in, values_in)


def shared_attend(block_len, core_ref, q_ref, k_ref, v_ref, ok_ref, ov_ref, o_ref):
    core = core_ref[0]
    length = q_ref.shape[0]
    for at in range(length // TILE):
        rows = pl.ds(at * TILE, TILE)
        seen = (at + 1) * TILE
        queries = q_ref[rows, :]
        raw = dot_t(queries, k_ref[:seen, :]) * (SCALE * LOG2E)
        far = dot_t(queries, ok_ref[:seen, :]) * (SCALE * LOG2E)
        at_row = lax.broadcasted_iota(jnp.int32, (TILE, TILE), 0)
        at_column = lax.broadcasted_iota(jnp.int32, (TILE, TILE), 1)
        near_last = jnp.where(at_column <= at_row, raw[:, at * TILE :], NEG)
        far_ok = at_column // block_len < at_row // block_len + core
        far_last = jnp.where(far_ok, far[:, at * TILE :], NEG)
        raw = jnp.concatenate([raw[:, : at * TILE], near_last], 1) if at else near_last
        far = jnp.concatenate([far[:, : at * TILE], far_last], 1) if at else far_last
        top = jnp.maximum(jnp.max(raw, 1, keepdims=True), jnp.max(far, 1, keepdims=True))
        weight = jnp.exp2(raw - top)
        far_weight = jnp.exp2(far - top)
        total = jnp.sum(weight, 1, keepdims=True) + jnp.sum(far_weight, 1, keepdims=True)
        mixed = dot_n(weight.astype(jnp.bfloat16), v_ref[:seen, :])
        mixed = mixed + dot_n(far_weight.astype(jnp.bfloat16), ov_ref[:seen, :])
        o_ref[rows, :] = (mixed / total).astype(o_ref.dtype)


def attend_shared(core, block_len, queries, keys_in, values_in, far_keys, far_values):
    length, width = queries.shape
    head_block = pl.BlockSpec((length, HEAD_DIM), lambda h: (0, h))
    return pl.pallas_call(
        functools.partial(shared_attend, block_len),
        grid=(width // HEAD_DIM,),
        in_specs=[pl.BlockSpec(memory_space=pltpu.SMEM)] + [head_block] * 5,
        out_specs=head_block,
        out_shape=jax.ShapeDtypeStruct((length, width), jnp.bfloat16),
        compiler_params=pltpu.CompilerParams(vmem_limit_bytes=60 * 2**20),
        cost_estimate=pl.CostEstimate(
            flops=4 * length * length * width, bytes_accessed=12 * length * width, transcendentals=0
        ),
        name="attend_shared",
    )(core.reshape(1), queries, keys_in, values_in, far_keys, far_values)


def middle_plan(z_size, total):
    last = total - 1
    places = {
        "fold_core": [1 + 2 * at for at in range(z_size)],
        "fold_second": ([6, 9, 12, 20] + [last] * z_size)[:z_size],
        "fold_first": ([12, 20] + [last] * z_size)[:z_size],
    }
    plan = {}
    for number in range(z_size + 2):
        for delay, act in enumerate(places):
            if 0 <= number - delay < z_size:
                at = min(places[act][number - delay], last)
                plan.setdefault(at, []).append((act, z_size - 1 - number + delay))
    return plan


def middle_kernel(
    shapes,
    heads,
    q_ref,
    k_ref,
    v_ref,
    o_ref,
    do_ref,
    log_ref,
    cos_ref,
    sin_ref,
    r_ref,
    dmid_ref,
    gain_ref,
    wq_ref,
    wk_ref,
    wv_ref,
    normed_ref,
    mixed_ref,
    first_ref,
    db_ref,
    *refs,
):
    count = len(shapes)
    parts, refs = refs[:count], refs[count:]
    home_out, gains_ref, grad_ref = refs[:3]
    outs, refs = refs[3 : 3 + count], refs[3 + count :]
    dq_all, dk_all, dv_all, dr_ref, dk_sum, dv_sum = refs[:6]
    sems, (send_sem, recv_sem, own_sem) = refs[6 + 5 * count : -3], refs[-3:]
    scatter = Scatter(row_views(shapes), parts, outs, refs[6 : 6 + 5 * count], sems)
    arrays = tuple(range(count))
    step = pl.program_id(0)
    ctx = lax.axis_size("ctx")
    devices = lax.axis_size("grp") * ctx
    me = lax.axis_index("grp") * ctx + lax.axis_index("ctx")
    block_len = dr_ref.shape[0] // devices
    near_home = TILE // block_len

    def home_copy(at):
        rows = pl.ds(pl.multiple_of(at * block_len, block_len), block_len)
        device = flat_device(at, ctx)
        return remote(dr_ref.at[rows], home_out.at[me], send_sem.at[at], recv_sem.at[me], device)

    def own_home():
        rows = pl.ds(pl.multiple_of(me * block_len, block_len), block_len)
        return pltpu.make_async_copy(dr_ref.at[rows], home_out.at[me], own_sem)

    def settle_home(at):
        rows = pl.ds(pl.multiple_of(at * block_len, block_len), block_len)
        device = flat_device(at, ctx)
        remote(dr_ref.at[rows], home_out.at[at], send_sem.at[at], recv_sem.at[at], device).wait()
    length = q_ref.shape[0]
    tiles = length // TILE
    rest = heads + tiles
    total = rest + 5 * tiles

    @pl.when(step == 0)
    def _():
        greet_all(devices, me, ctx)
        scatter.begin(arrays)
        gains_ref[...] = jnp.zeros_like(gains_ref)

    for at_step, acts in middle_plan(scatter.z_size, total).items():

        @pl.when(step == at_step)
        def _(acts=acts):
            for act, layer in acts:
                getattr(scatter, act)(arrays, layer)

    @pl.when(step < heads)
    def _():
        head = step
        columns = pl.ds(pl.multiple_of(head * HEAD_DIM, HEAD_DIM), HEAD_DIM)
        lane = lax.broadcasted_iota(jnp.int32, (TILE, 128), 1)

        def unrotated(grads, rows):
            turned = pltpu.roll(grads, HEAD_DIM // 2, 1)
            return grads * cos_ref[rows, :] - turned * sin_ref[rows, :]

        for at in range(tiles):
            rows = pl.ds(at * TILE, TILE)
            seen = (at + 1) * TILE
            queries, d_mixed = q_ref[rows, :], do_ref[rows, :]
            log_total = jnp.sum(jnp.where(lane == head, log_ref[rows, :], 0.0), 1, keepdims=True)
            delta = jnp.sum(d_mixed.astype(jnp.float32) * o_ref[rows, :].astype(jnp.float32), 1, keepdims=True)
            raw = dot_t(queries, k_ref[:seen, :]) * (SCALE * LOG2E)
            last = jnp.where(below(TILE, TILE), raw[:, at * TILE :], NEG)
            raw = jnp.concatenate([raw[:, : at * TILE], last], 1) if at else last
            probs = jnp.exp2(raw - log_total)
            d_probs = dot_t(d_mixed, v_ref[:seen, :])
            slopes = (probs * (d_probs - delta)).astype(jnp.bfloat16)
            d_query = dot_n(slopes, k_ref[:seen, :]) * SCALE
            dq_all[rows, columns] = unrotated(d_query, rows).astype(dq_all.dtype)
            d_value = dot_w(probs.astype(jnp.bfloat16), d_mixed)
            d_key = dot_w(slopes, queries)
            if at:
                before = pl.ds(0, at * TILE)
                dv_sum[before, :] += d_value[: at * TILE]
                dk_sum[before, :] += d_key[: at * TILE]
            dv_sum[rows, :] = d_value[at * TILE :]
            dk_sum[rows, :] = d_key[at * TILE :]
        dk_all[:, columns] = unrotated(dk_sum[...] * SCALE, pl.ds(0, length)).astype(dk_all.dtype)
        dv_all[:, columns] = dv_sum[...].astype(dv_all.dtype)

    @pl.when((step >= heads) & (step < rest))
    def _():
        rows = pl.ds(pl.multiple_of((step - heads) * TILE, TILE), TILE)
        d_normed = (
            dot_t(dq_all[rows, :], wq_ref[...])
            + dot_t(dk_all[rows, :], wk_ref[...])
            + dot_t(dv_all[rows, :], wv_ref[...])
        )
        d_resid, gain_one = pull_norm(r_ref[...].astype(jnp.float32), d_normed, gain_ref[0:1, :])
        dr_ref[rows, :] = (d_resid + dmid_ref[...].astype(jnp.float32)).astype(jnp.bfloat16)
        gains_ref[0:1, :] += gain_one
        first = (step - heads) * near_home
        each_other(first, first + near_home, me, lambda at: home_copy(at).start())

    pairs = (
        (normed_ref, dq_all),
        (normed_ref, dk_all),
        (normed_ref, dv_all),
        (mixed_ref, db_ref),
        (first_ref, dr_ref),
    )
    for at, (left, right) in enumerate(pairs):

        @pl.when((step >= rest + at * tiles) & (step < rest + (at + 1) * tiles))
        def _(left=left, right=right):
            grad_ref[...] = dot_w(left[...], right[...]).astype(grad_ref.dtype)

    @pl.when(step == rest)
    def _():
        own_home().start()

    @pl.when(step == total - 1)
    def _():
        scatter.settle(arrays)
        each_other(0, devices, me, settle_home)
        own_home().wait()


def middle_all(
    queries,
    keys_in,
    values_in,
    mixed,
    d_mixed,
    log_total,
    cos_full,
    sin_full,
    resid,
    d_middle,
    gain_float,
    query_w,
    key_w,
    value_w,
    normed,
    first_out,
    d_branch,
    sums,
    collective_id,
):
    sizes = grid_sizes()
    length, width = queries.shape
    heads, tiles = width // HEAD_DIM, length // TILE
    rest = heads + tiles
    shapes = [part.shape[1:] for part in sums]
    head_block = pl.BlockSpec((length, HEAD_DIM), lambda i: (0, jnp.minimum(i, heads - 1)))
    tall_block = pl.BlockSpec((TILE, width), lambda i: (jnp.clip(i - heads, 0, tiles - 1), 0))

    def left_block(first, repeats=1):
        def place(i):
            inside = jnp.clip(i - rest - first * tiles, 0, repeats * tiles - 1)
            return (0, inside % tiles)

        return pl.BlockSpec((length, TILE), place)

    fixed = pl.BlockSpec((length, 128), lambda i: (0, 0), pipeline_mode=pl.Buffered(1))
    anywhere = pl.BlockSpec(memory_space=pl.ANY)
    near = pl.BlockSpec(memory_space=pltpu.VMEM)
    once = pl.Buffered(1)
    weights = sum(shape[0] * shape[1] for shape in shapes)
    devices = lax.axis_size("grp") * lax.axis_size("ctx")
    dma = pltpu.SemaphoreType.DMA
    return pl.pallas_call(
        functools.partial(middle_kernel, shapes, heads),
        grid=(rest + 5 * tiles,),
        in_specs=[head_block] * 5
        + [fixed] * 3
        + [tall_block] * 2
        + [whole_block(a) for a in (gain_float, query_w, key_w, value_w)]
        + [left_block(0, 3), left_block(3), left_block(4)]
        + [whole_block(d_branch)]
        + [anywhere] * len(sums),
        out_specs=[
            anywhere,
            pl.BlockSpec((8, width), lambda i: (0, 0), pipeline_mode=once),
            pl.BlockSpec((TILE, width), lambda i: (jnp.clip(i - rest, 0, 5 * tiles - 1), 0)),
        ]
        + [near] * len(sums),
        out_shape=[
            jax.ShapeDtypeStruct((devices, length // devices, width), jnp.bfloat16),
            jax.ShapeDtypeStruct((8, width), jnp.float32),
            jax.ShapeDtypeStruct((5 * width, width), jnp.bfloat16),
        ]
        + [jax.ShapeDtypeStruct(shape, jnp.float32) for shape in shapes],
        scratch_shapes=[pltpu.VMEM((length, width), jnp.bfloat16)] * 4
        + [pltpu.VMEM((length, HEAD_DIM), jnp.float32)] * 2
        + scatter_scratch(shapes)
        + [dma((devices,)), dma((devices,)), dma],
        compiler_params=pltpu.CompilerParams(
            collective_id=collective_id, has_side_effects=True, vmem_limit_bytes=62 * 2**20
        ),
        cost_estimate=cost(24 * length * width * width, 64 * length * width + 64 * weights),
        name="middle_all",
    )(
        queries,
        keys_in,
        values_in,
        mixed,
        d_mixed,
        log_total,
        cos_full,
        sin_full,
        resid,
        d_middle,
        gain_float,
        query_w,
        key_w,
        value_w,
        normed,
        mixed,
        first_out,
        d_branch,
        *(part.reshape(sizes + part.shape[1:]) for part in sums),
    )


def rope_full(length):
    freq = np.float32(10000.0) ** (np.float32(-2.0 / HEAD_DIM) * np.arange(HEAD_DIM // 2, dtype=np.float32))
    angle = np.arange(length, dtype=np.float32)[:, None] * freq
    cosine, sine = np.cos(angle).astype(np.float32), np.sin(angle).astype(np.float32)
    return jnp.asarray(np.concatenate([cosine, cosine], 1)), jnp.asarray(np.concatenate([-sine, sine], 1))


def whole_block(array):
    return pl.BlockSpec(array.shape, lambda *_: (0,) * array.ndim, pipeline_mode=pl.Buffered(1))


def row_block(rows, width):
    return pl.BlockSpec((rows, width), lambda i: (i, 0))


def compute_params(megabytes=58):
    return pltpu.CompilerParams(vmem_limit_bytes=megabytes * 2**20)


def cost(flops, nbytes):
    return pl.CostEstimate(flops=int(flops), bytes_accessed=int(nbytes), transcendentals=0)


def unit_rows(values):
    scale_rows = rms_scale(values)
    return scale_rows, values * scale_rows


def pull_norm(values, upstream, gain_row):
    scale_rows, normal = unit_rows(values)
    gain_part = jnp.sum(upstream * normal, 0, keepdims=True)
    scaled = upstream * gain_row
    return scale_rows * (scaled - normal * jnp.mean(scaled * normal, -1, keepdims=True)), gain_part


def turned_heads(values, cos, sin):
    parts = []
    for head in range(values.shape[1] // HEAD_DIM):
        one = values[:, head * HEAD_DIM : (head + 1) * HEAD_DIM]
        parts.append(one * cos + pltpu.roll(one, HEAD_DIM // 2, 1) * sin)
    return jnp.concatenate(parts, 1)


COLUMNS = 256


def column_block(rows, column=COLUMNS):
    return pl.BlockSpec((rows, column), lambda i: (0, i))


def write_heads(step_normed, wq_ref, wk_ref, wv_ref, cos, sin, q_ref, k_ref, v_ref):
    normed = step_normed[...]
    q_ref[...] = turned_heads(dot_n(normed, wq_ref[...]), cos, sin).astype(jnp.bfloat16)
    k_ref[...] = turned_heads(dot_n(normed, wk_ref[...]), cos, sin).astype(jnp.bfloat16)
    v_ref[...] = dot_n(normed, wv_ref[...]).astype(jnp.bfloat16)


def first_heads_kernel(
    r_ref, gain_ref, cos_ref, sin_ref, wq_ref, wk_ref, wv_ref, q_ref, k_ref, v_ref, normed_sc
):
    @pl.when(pl.program_id(0) == 0)
    def _():
        resid = r_ref[...].astype(jnp.float32)
        normed_sc[...] = (unit_rows(resid)[1] * gain_ref[0:1, :]).astype(jnp.bfloat16)

    core = lax.axis_index("ctx") % cos_ref.shape[1]
    cos, sin = (table[:, core].reshape(-1, HEAD_DIM) for table in (cos_ref, sin_ref))
    write_heads(normed_sc, wq_ref, wk_ref, wv_ref, cos, sin, q_ref, k_ref, v_ref)


def first_heads(resid, gain_float, query_w, key_w, value_w, cos, sin):
    rows, width = resid.shape
    return pl.pallas_call(
        first_heads_kernel,
        grid=(width // COLUMNS,),
        in_specs=[whole_block(a) for a in (resid, gain_float, cos, sin)] + [column_block(width)] * 3,
        out_specs=[column_block(rows)] * 3,
        out_shape=[jax.ShapeDtypeStruct((rows, width), jnp.bfloat16)] * 3,
        scratch_shapes=[pltpu.VMEM((rows, width), jnp.bfloat16)],
        compiler_params=compute_params(),
        cost_estimate=cost(6 * rows * width * width, 8 * rows * width + 6 * width * width),
        name="first_heads",
    )(resid, gain_float, cos, sin, query_w, key_w, value_w)


def last_heads_kernel(
    start_ref,
    near_ref,
    far_ref,
    wa_ref,
    gain_ref,
    cos_ref,
    sin_ref,
    wq_ref,
    wk_ref,
    wv_ref,
    r_ref,
    n_ref,
    first_ref,
    q_ref,
    k_ref,
    v_ref,
):
    @pl.when(pl.program_id(0) == 0)
    def _():
        owner = lax.axis_index("ctx") % 2 == 0
        blocks, half, width = near_ref.shape
        both = jnp.concatenate([near_ref[...], far_ref[...]], 1).reshape(2 * blocks * half, width)
        first_ref[...] = jnp.where(owner, both, jnp.zeros_like(both))
        resid = start_ref[...].astype(jnp.float32) + dot_n(first_ref[...], wa_ref[...])
        r_ref[...] = resid.astype(jnp.bfloat16)
        n_ref[...] = (unit_rows(resid)[1] * gain_ref[0:1, :]).astype(jnp.bfloat16)

    write_heads(n_ref, wq_ref, wk_ref, wv_ref, cos_ref[...], sin_ref[...], q_ref, k_ref, v_ref)


def last_heads(starting, near_out, far_out, adapt_w, gain_float, query_w, key_w, value_w, cos, sin):
    rows, width = starting.shape
    upper = pl.BlockSpec((width, width), lambda i: (0, 0), pipeline_mode=pl.Buffered(1))
    like = jax.ShapeDtypeStruct((rows, width), jnp.bfloat16)
    return pl.pallas_call(
        last_heads_kernel,
        grid=(width // COLUMNS,),
        in_specs=[whole_block(a) for a in (starting, near_out, far_out)]
        + [upper]
        + [whole_block(a) for a in (gain_float, cos, sin)]
        + [column_block(width)] * 3,
        out_specs=[whole_block(like)] * 3 + [column_block(rows)] * 3,
        out_shape=[like] * 6,
        compiler_params=compute_params(),
        cost_estimate=cost(8 * rows * width * width, 16 * rows * width + 8 * width * width),
        name="last_heads",
    )(starting, near_out, far_out, adapt_w, gain_float, cos, sin, query_w, key_w, value_w)


def first_rows_kernel(
    r_ref, mixed_ref, gain_ref, wo_ref, wg_ref, wu_ref, wd_ref, out_ref, middle_sc, mlp_sc, total_sc
):
    step = pl.program_id(0)

    @pl.when(step == 0)
    def _():
        branch = dot_n(mixed_ref[...], wo_ref[...])
        middle = r_ref[...].astype(jnp.float32) + unit_rows(branch)[1] * gain_ref[1:2, :]
        middle_sc[...] = middle
        mlp_sc[...] = (unit_rows(middle)[1] * gain_ref[2:3, :]).astype(jnp.bfloat16)
        total_sc[...] = jnp.zeros_like(total_sc)

    mlp_in = mlp_sc[...]
    gate_pre = dot_n(mlp_in, wg_ref[...])
    up_pre = dot_n(mlp_in, wu_ref[...])
    hidden = (gate_pre / (1.0 + jnp.exp(-gate_pre)) * up_pre).astype(jnp.bfloat16)
    total_sc[...] += dot_n(hidden, wd_ref[...])

    @pl.when(step == pl.num_programs(0) - 1)
    def _():
        out_ref[...] = (middle_sc[...] + unit_rows(total_sc[...])[1] * gain_ref[3:4, :]).astype(jnp.bfloat16)


def first_rows(resid, mixed, gain_float, output_w, gate_w, up_w, down_w):
    rows, width = resid.shape
    inner = gate_w.shape[1]
    like = jax.ShapeDtypeStruct((rows, width), jnp.bfloat16)
    weights = output_w.size + 3 * gate_w.size
    return pl.pallas_call(
        first_rows_kernel,
        grid=(inner // COLUMNS,),
        in_specs=[whole_block(a) for a in (resid, mixed, gain_float, output_w)]
        + [column_block(width)] * 2
        + [row_block(COLUMNS, width)],
        out_specs=whole_block(like),
        out_shape=like,
        scratch_shapes=[
            pltpu.VMEM((rows, width), jnp.float32),
            pltpu.VMEM((rows, width), jnp.bfloat16),
            pltpu.VMEM((rows, width), jnp.float32),
        ],
        compiler_params=compute_params(),
        cost_estimate=cost(2 * rows * weights, 6 * rows * width + 2 * weights),
        name="first_rows",
    )(resid, mixed, gain_float, output_w, gate_w, up_w, down_w)


def last_rows_kernel(
    r_ref,
    mixed_ref,
    gain_ref,
    wo_ref,
    wg_ref,
    wu_ref,
    wd_ref,
    out_ref,
    branch_out,
    middle_out,
    mlp_out,
    down_ref,
    gate_ref,
    up_ref,
    hidden_ref,
    branch_sc,
    middle_sc,
    middle_low,
    mlp_sc,
    total_sc,
    sems,
):
    step = pl.program_id(0)
    copies = [
        pltpu.make_async_copy(source, target, sems.at[at])
        for at, (source, target) in enumerate(
            ((branch_sc, branch_out), (middle_low, middle_out), (mlp_sc, mlp_out))
        )
    ]

    @pl.when(step == 0)
    def _():
        branch = dot_n(mixed_ref[...], wo_ref[...])
        branch_sc[...] = branch.astype(jnp.bfloat16)
        middle = r_ref[...].astype(jnp.float32) + unit_rows(branch)[1] * gain_ref[1:2, :]
        middle_sc[...] = middle
        middle_low[...] = middle.astype(jnp.bfloat16)
        mlp_sc[...] = (unit_rows(middle)[1] * gain_ref[2:3, :]).astype(jnp.bfloat16)
        total_sc[...] = jnp.zeros_like(total_sc)
        for copy in copies:
            copy.start()

    mlp_in = mlp_sc[...]
    gate_pre = dot_n(mlp_in, wg_ref[...])
    up_pre = dot_n(mlp_in, wu_ref[...])
    hidden = (gate_pre / (1.0 + jnp.exp(-gate_pre)) * up_pre).astype(jnp.bfloat16)
    gate_ref[...] = gate_pre.astype(jnp.bfloat16)
    up_ref[...] = up_pre.astype(jnp.bfloat16)
    hidden_ref[...] = hidden
    total_sc[...] += dot_n(hidden, wd_ref[...])

    @pl.when(step == pl.num_programs(0) - 1)
    def _():
        down_out = total_sc[...]
        down_ref[...] = down_out.astype(jnp.bfloat16)
        out_ref[...] = (middle_sc[...] + unit_rows(down_out)[1] * gain_ref[3:4, :]).astype(jnp.bfloat16)
        for copy in copies:
            copy.wait()


def last_rows(resid, mixed, gain_float, output_w, gate_w, up_w, down_w):
    rows, width = resid.shape
    inner = gate_w.shape[1]
    narrow, wide = (jax.ShapeDtypeStruct((rows, w), jnp.bfloat16) for w in (width, inner))
    weights = output_w.size + 3 * gate_w.size
    low, tall = pltpu.VMEM((rows, width), jnp.bfloat16), pltpu.VMEM((rows, width), jnp.float32)
    anywhere = pl.BlockSpec(memory_space=pl.ANY)
    return pl.pallas_call(
        last_rows_kernel,
        grid=(inner // COLUMNS,),
        in_specs=[whole_block(a) for a in (resid, mixed, gain_float, output_w)]
        + [column_block(width)] * 2
        + [row_block(COLUMNS, width)],
        out_specs=[whole_block(narrow)] + [anywhere] * 3 + [whole_block(narrow)] + [column_block(rows)] * 3,
        out_shape=[narrow] * 5 + [wide] * 3,
        scratch_shapes=[low, tall, low, low, tall, pltpu.SemaphoreType.DMA((3,))],
        compiler_params=compute_params(),
        cost_estimate=cost(2 * rows * weights, 14 * rows * width + 6 * rows * inner + 2 * weights),
        name="last_rows",
    )(resid, mixed, gain_float, output_w, gate_w, up_w, down_w)


def back_rows_kernel(
    down_ref,
    slope_ref,
    mlp_ref,
    gain_ref,
    middle_in,
    branch_in,
    wo_in,
    wg_ref,
    wu_ref,
    wd_ref,
    gate_ref,
    up_ref,
    hidden_ref,
    dmid_ref,
    db_ref,
    dmix_ref,
    gains_ref,
    dwg_ref,
    dwu_ref,
    dwd_ref,
    dd_sc,
    total_sc,
    middle_sc,
    branch_sc,
    wo_sc,
    sems,
):
    step = pl.program_id(0)
    copies = [
        pltpu.make_async_copy(source, target, sems.at[at])
        for at, (source, target) in enumerate(((middle_in, middle_sc), (branch_in, branch_sc), (wo_in, wo_sc)))
    ]

    @pl.when(step == 0)
    def _():
        for copy in copies:
            copy.start()
        gains_ref[...] = jnp.zeros_like(gains_ref)
        d_down, gain_four = pull_norm(
            down_ref[...].astype(jnp.float32), slope_ref[...].astype(jnp.float32), gain_ref[3:4, :]
        )
        gains_ref[2:3, :] = gain_four
        dd_sc[...] = d_down.astype(jnp.bfloat16)
        total_sc[...] = jnp.zeros_like(total_sc)

    d_down, mlp_in = dd_sc[...], mlp_ref[...]
    d_hidden = dot_t(d_down, wd_ref[...])
    gate_pre, up_pre = gate_ref[...].astype(jnp.float32), up_ref[...].astype(jnp.float32)
    sigma = 1.0 / (1.0 + jnp.exp(-gate_pre))
    d_gate = (d_hidden * up_pre * sigma * (1.0 + gate_pre * (1.0 - sigma))).astype(jnp.bfloat16)
    d_up = (d_hidden * gate_pre * sigma).astype(jnp.bfloat16)
    dwd_ref[...] = dot_w(hidden_ref[...], d_down).astype(jnp.bfloat16)
    dwg_ref[...] = dot_w(mlp_in, d_gate).astype(jnp.bfloat16)
    dwu_ref[...] = dot_w(mlp_in, d_up).astype(jnp.bfloat16)
    total_sc[...] += dot_t(jnp.concatenate([d_gate, d_up], 1), jnp.concatenate([wg_ref[...], wu_ref[...]], 1))

    @pl.when(step == pl.num_programs(0) - 1)
    def _():
        for copy in copies:
            copy.wait()
        d_middle, gain_three = pull_norm(middle_sc[...].astype(jnp.float32), total_sc[...], gain_ref[2:3, :])
        gains_ref[1:2, :] = gain_three
        d_middle = d_middle + slope_ref[...].astype(jnp.float32)
        dmid_ref[...] = d_middle.astype(jnp.bfloat16)
        d_branch, gain_two = pull_norm(branch_sc[...].astype(jnp.float32), d_middle, gain_ref[1:2, :])
        gains_ref[0:1, :] = gain_two
        d_branch = d_branch.astype(jnp.bfloat16)
        db_ref[...] = d_branch
        dmix_ref[...] = dot_t(d_branch, wo_sc[...]).astype(jnp.bfloat16)


def back_rows(
    down_out, upstream, middle, branch, mlp_in, gain_float, output_w, gate_w, up_w, down_w, gate_pre, up_pre, hidden
):
    rows, width = middle.shape
    inner = gate_w.shape[1]
    narrow = jax.ShapeDtypeStruct((rows, width), jnp.bfloat16)
    gains = jax.ShapeDtypeStruct((8, width), jnp.float32)
    wide = jax.ShapeDtypeStruct(gate_w.shape, jnp.bfloat16)
    whole = [narrow] * 3 + [gains]
    near = (down_out, upstream, mlp_in, gain_float)
    low = pltpu.VMEM((rows, width), jnp.bfloat16)
    return pl.pallas_call(
        back_rows_kernel,
        grid=(inner // COLUMNS,),
        in_specs=[whole_block(a) for a in near]
        + [pl.BlockSpec(memory_space=pl.ANY)] * 3
        + [column_block(width)] * 2
        + [row_block(COLUMNS, width)]
        + [column_block(rows)] * 3,
        out_specs=[whole_block(one) for one in whole] + [column_block(width)] * 2 + [row_block(COLUMNS, width)],
        out_shape=whole + [wide, wide, jax.ShapeDtypeStruct(down_w.shape, jnp.bfloat16)],
        scratch_shapes=[
            low,
            pltpu.VMEM((rows, width), jnp.float32),
            low,
            low,
            pltpu.VMEM(output_w.shape, jnp.bfloat16),
            pltpu.SemaphoreType.DMA((3,)),
        ],
        compiler_params=compute_params(),
        cost_estimate=cost(12 * rows * gate_w.size, 18 * rows * width + 6 * rows * inner + 12 * gate_w.size),
        name="back_rows",
    )(*near, middle, branch, output_w, gate_w, up_w, down_w, gate_pre, up_pre, hidden)


def close_kernel(target_ref, final_ref, w_ref, s_ref, e_ref, home, grad_ref, gain_ref, *refs):
    final_out, ds_ref, de_ref = refs[:3]
    outs, refs = refs[3:9], refs[9:]
    first, total, adapt_part, *refs = refs
    buffers, sems, own_sem = refs[:30], refs[30:37], refs[37]
    parts = [grad_ref.at[at] for at in range(4)] + [adapt_part, gain_ref]
    scatter = Scatter(row_views([out.shape for out in outs]), parts, outs, buffers, sems)
    early, late = (0, 1, 2, 3, 5), (4,)
    count, width = ds_ref.shape
    tiles = count // TILE
    block_len = home.shape[1]

    greet_line(*scatter.place, scatter.z_size)
    scatter.begin(early)
    own_first = pltpu.make_async_copy(grad_ref.at[4], first, own_sem)
    own_first.start()

    def order_rows(tile):
        rows = pl.ds(tile * TILE, TILE)
        at_row = lax.broadcasted_iota(jnp.int32, (count, TILE), 0)
        return rows, (at_row == target_ref[:, rows]).astype(jnp.bfloat16)

    def at_home(tile):
        rows, order = order_rows(tile)
        d_slots = home[...].reshape(count, width)
        d_home = dot_w(order, d_slots).astype(jnp.bfloat16)
        at_row = lax.broadcasted_iota(jnp.int32, (count, TILE), 0)
        once = jnp.where(at_row // block_len % 2 == 1, order, jnp.zeros_like(order))
        d_once = dot_w(once, d_slots).astype(jnp.bfloat16)
        ds_ref[rows, :] = dot_t(d_home, w_ref[:width, :]).astype(jnp.bfloat16)
        de_ref[rows, :] = dot_t(d_home, w_ref[width:, :]).astype(jnp.bfloat16)
        upper, lower = dot_w(s_ref[rows, :], d_once), dot_w(e_ref[rows, :], d_home)
        if tile == 0:
            own_first.wait()
            total[:width, :] = upper + first[...].reshape(width, width).astype(jnp.float32)
            total[width:, :] = lower
        else:
            total[:width, :] += upper
            total[width:, :] += lower

    for tile in range(tiles):
        at_home(tile)
        if tile < scatter.z_size:
            scatter.stage(early, tile)
    adapt_part[...] = total[...].reshape(adapt_part.shape).astype(adapt_part.dtype)
    scatter.begin(late)
    for number in range(scatter.stages()):
        if number >= tiles:
            scatter.stage(early, number)
        scatter.stage(late, number)
        if number < tiles:
            rows, order = order_rows(number)
            final_out[rows, :] = dot_w(order, final_ref[...]).astype(jnp.bfloat16)
    scatter.settle(early)
    scatter.settle(late)


def close_all(
    target, final_slots, adapt_w, once, embeds, d_home, weight_parts, gain_part, collective_id
):
    sizes = grid_sizes()
    parts = lax.axis_size("grp") * lax.axis_size("ctx")
    count, width = embeds.shape
    side = width // parts
    square = weight_parts.reshape((5,) + sizes + (side, width))
    gain = gain_part.reshape(sizes + gain_part.shape[1:])
    shapes = [(side, width)] * 4 + [(2 * side, width), gain_part.shape[1:]]
    anywhere = pl.BlockSpec(memory_space=pl.ANY)
    near = pl.BlockSpec(memory_space=pltpu.VMEM)
    dma = pltpu.SemaphoreType.DMA
    like = jax.ShapeDtypeStruct((count, width), jnp.bfloat16)
    return pl.pallas_call(
        close_kernel,
        in_specs=[near] * 6 + [anywhere] * 2,
        out_specs=[near] * (3 + len(shapes)),
        out_shape=[like] * 3 + [jax.ShapeDtypeStruct(shape, jnp.float32) for shape in shapes],
        scratch_shapes=[
            pltpu.VMEM(sizes + (side, width), jnp.bfloat16),
            pltpu.VMEM((2 * width, width), jnp.float32),
            pltpu.VMEM(sizes + (2 * side, width), jnp.bfloat16),
        ]
        + scatter_scratch(shapes)
        + [dma],
        compiler_params=pltpu.CompilerParams(
            collective_id=collective_id, has_side_effects=True, vmem_limit_bytes=62 * 2**20
        ),
        name="close_all",
    )(target, final_slots, adapt_w, once, embeds, d_home, square, gain)


def finish_kernel(count, *refs):
    for source, target in zip(refs[:count], refs[count:]):
        target[...] = source[...]


def finish_all(results):
    count = len(results)
    near = pl.BlockSpec(memory_space=pltpu.VMEM)
    return pl.pallas_call(
        functools.partial(finish_kernel, count),
        in_specs=[near] * count,
        out_specs=[near] * count,
        out_shape=[jax.ShapeDtypeStruct(one.shape, one.dtype) for one in results],
        compiler_params=compute_params(),
        name="finish_all",
    )(*results)


def paired_on_device(
    latents, embeds, cotangent, counts, w_adapt, w_query, w_key, w_value, w_out, w_gate, w_up, w_down, gains
):
    block_len, seqs, width = latents.shape
    parts = lax.axis_size("grp") * lax.axis_size("ctx")
    length = block_len * parts
    core = grid_place()[3]

    twice = counts == 2
    slot = jnp.where(
        twice,
        2 * (jnp.cumsum(twice.astype(jnp.int32)) - 1),
        2 * (jnp.cumsum((~twice).astype(jnp.int32)) - 1) + 1,
    )
    row_count = block_len * seqs
    target = (slot[None, :] * block_len + jnp.arange(block_len, dtype=jnp.int32)[:, None]).reshape(row_count)
    latent_rows, embed_rows, slope_rows = (a.reshape(row_count, width) for a in (latents, embeds, cotangent))

    def exchange(values):
        return lax.all_to_all(values, BOTH, split_axis=0, concat_axis=0, tiled=True)

    half = block_len // 2
    gain_rows = jnp.pad(gains.reshape(1, -1), ((0, 15), (0, 0)))
    *matrices, gain_float, shared, starting, upstream = open_all(
        target.reshape(1, row_count),
        latent_rows,
        embed_rows,
        slope_rows,
        [w_adapt, w_query, w_key, w_value, w_out, w_gate, w_up, w_down, gain_rows],
        block_len,
        0,
    )
    adapt_w, query_w, key_w, value_w, output_w, gate_w, up_w, down_w = (
        matrix.reshape(-1, matrix.shape[-1]) for matrix in matrices
    )
    gain_float = gain_float.reshape((parts,) + gain_rows.shape)[:, 0].reshape((parts,) + gains.shape)
    gain_float = gain_float.transpose(1, 0, 2).reshape(gains.shape[0], width).astype(jnp.float32)
    shared = shared.reshape(length // 2, width)
    starting = exchange(starting).reshape(length, width)

    cos_full, sin_full = rope_full(length)
    cos_half, sin_half = (table.reshape(parts, 2, half, HEAD_DIM) for table in (cos_full, sin_full))
    queries, keys_in, values_in = first_heads(shared, gain_float, query_w, key_w, value_w, cos_half, sin_half)
    far_keys, far_values = send(keys_in, 3), send(values_in, 3)
    mixed = attend_shared(core, half, queries, keys_in, values_in, far_keys, far_values)
    near_out = first_rows(shared, mixed, gain_float, output_w, gate_w, up_w, down_w)
    near_out, upstream = lax.optimization_barrier((near_out, upstream))
    upstream = exchange(upstream.reshape(parts, block_len, width)).reshape(length, width)
    far_out = send(near_out, 3, -1)

    resid, normed, first_out, queries, keys_in, values_in = last_heads(
        starting,
        near_out.reshape(parts, half, width),
        far_out.reshape(parts, half, width),
        adapt_w,
        gain_float,
        query_w,
        key_w,
        value_w,
        cos_full,
        sin_full,
    )
    mixed, log_total = attend_whole(queries, keys_in, values_in)
    result, branch, middle, mlp_in, down_out, gate_pre, up_pre, hidden = last_rows(
        resid, mixed, gain_float, output_w, gate_w, up_w, down_w
    )
    d_middle, d_branch, d_mixed, gain_rest, gate_part, up_part, down_part = back_rows(
        down_out,
        upstream,
        middle,
        branch,
        mlp_in,
        gain_float,
        output_w,
        gate_w,
        up_w,
        down_w,
        gate_pre,
        up_pre,
        hidden,
    )
    result, upstream = lax.optimization_barrier((result, upstream))
    final_back = exchange(result.reshape(parts, block_len, width))

    def blocks(part):
        return part.reshape(parts, -1, part.shape[-1])

    d_home, gain_one, weight_parts, gate_grad, up_grad, down_grad = middle_all(
        queries,
        keys_in,
        values_in,
        mixed,
        d_mixed,
        log_total,
        cos_full,
        sin_full,
        resid,
        d_middle,
        gain_float,
        query_w,
        key_w,
        value_w,
        normed,
        first_out,
        d_branch,
        [blocks(part) for part in (gate_part, up_part, down_part)],
        1,
    )
    gain_part = jnp.concatenate([gain_one[:1], gain_rest[:3]], 0)
    gain_part = gain_part.reshape(gains.shape[0], parts, gains.shape[1]).transpose(1, 0, 2)
    gain_part = jnp.pad(
        gain_part.reshape(parts, 1, gains.size).astype(jnp.bfloat16), ((0, 0), (0, 15), (0, 0))
    )
    final_back, latent_back, embed_back, query_grad, key_grad, value_grad, out_grad, adapt_grad, gain_grad = close_all(
        target.reshape(1, row_count),
        final_back.reshape(row_count, width),
        adapt_w,
        latent_rows,
        embed_rows,
        d_home,
        weight_parts,
        gain_part,
        2,
    )
    results = finish_all(
        [
            final_back,
            latent_back,
            embed_back,
            adapt_grad,
            query_grad,
            key_grad,
            value_grad,
            out_grad,
            gate_grad,
            up_grad,
            down_grad,
        ]
    )
    gain_grad = gain_grad[0].reshape(gains.shape)
    return tuple(one.reshape(latents.shape) for one in results[:3]) + tuple(results[3:]) + (gain_grad,)


def on_device(latents, *others):
    ctx = lax.axis_size("ctx")
    parts = lax.axis_size("grp") * ctx
    if latents.shape[1] == parts and ctx == 4 and latents.shape[0] % 16 == 0:
        return paired_on_device(latents, *others)
    return spread_on_device(latents, *others)


def solution(mesh):
    placed = (
        P(("grp", "ctx"), None, None),
        P(("grp", "ctx"), None, None),
        P(("grp", "ctx"), None, None),
        P(),
        P(("grp", "ctx"), None),
        P(("grp", "ctx"), None),
        P(("grp", "ctx"), None),
        P(("grp", "ctx"), None),
        P(("grp", "ctx"), None),
        P(("grp", "ctx"), None),
        P(("grp", "ctx"), None),
        P(("grp", "ctx"), None),
        P(None, ("grp", "ctx")),
    )
    return jax.shard_map(
        on_device,
        mesh=mesh,
        in_specs=placed,
        out_specs=(
            P(("grp", "ctx"), None, None),
            P(("grp", "ctx"), None, None),
            P(("grp", "ctx"), None, None),
            P(("grp", "ctx"), None),
            P(("grp", "ctx"), None),
            P(("grp", "ctx"), None),
            P(("grp", "ctx"), None),
            P(("grp", "ctx"), None),
            P(("grp", "ctx"), None),
            P(("grp", "ctx"), None),
            P(("grp", "ctx"), None),
            P(None, ("grp", "ctx")),
        ),
        check_vma=False,
    )
```
